128 devices in a mesh: grp: 4 (over x_hi, core), tile: 32 (over z, y, x_lo).
Axes of the slice: x: 4 (x_hi: 2, x_lo: 2; x = x_hi * 2 + x_lo), y: 4, z: 4, core: 2. Of those that a mesh axis runs over, the one named last changes fastest.
Arguments:
- object_tile: float32 [2048, 2, 512], P('tile'), may hold values from -5 to 5
- probe: float32 [8, 2, 256, 256], replicated, may hold values from -5 to 5
- offsets: int32 [256, 2], P(('grp', 'tile')), may hold values from 0 to 1792, as said below
- frame_ids: int32 [256], P(('grp', 'tile')), may hold values from 0 to 1, as said below
- frames: float32 [256, 256, 256], P(('grp', 'tile')), may hold values from 0.2 to 3
Outputs:
- updated: float32 [2048, 2, 512], P('tile')
The draws below stay inside these ranges and needn't reach their ends.
Inputs may be any that keep to these rules, and one draw needn't show every extreme that they name: Both offsets of a position are multiples of 32; the row offset is at most 1792 and the column offset at most 256, nodes of a regular grid of 57 x 9; the first position sits at the last node in both directions and the second at the anchor. `frame_ids`: in each aligned block of 2 positions the ids are a permutation of 0 to 1.
All inputs are finite; a program needn't handle non-finite values.
Results may differ from the reference program's by a relative error of at most 0.0014.
Values sent between devices are 32-bit elements; how exact they have to be, the bound alone decides.
A program may use at most 128 MiB of HBM per device.

```python
import math
import jax
import jax.numpy as jnp
from jax import lax

PATCH = 256
MODES = 8
STEP = 32
POS_DEV = 2
OBJ_W = 512
OBJ_H = 2048
POSITIONS = 256
GRID_ROWS = 57
GRID_COLS = 9


def draw_offsets(key, part):
    key = jax.random.fold_in(key, 11)
    row_key, col_key = jax.random.split(key)
    rows = jax.random.randint(row_key, (POSITIONS,), 0, GRID_ROWS) * STEP
    cols = jax.random.randint(col_key, (POSITIONS,), 0, GRID_COLS) * STEP
    rows = rows.at[0].set((GRID_ROWS - 1) * STEP).at[1].set(0)
    cols = cols.at[0].set((GRID_COLS - 1) * STEP).at[1].set(0)
    return jnp.stack([rows, cols], axis=1).astype(jnp.int32)


def draw_frame_ids(key, part):
    key = jax.random.fold_in(key, 23)
    keys = jax.random.split(key, POSITIONS // POS_DEV)
    blocks = jax.vmap(lambda single: jax.random.permutation(single, jnp.arange(POS_DEV, dtype=jnp.int32)))(keys)
    return blocks.reshape(-1).astype(jnp.int32)


def shard_levels(stream_key, dims, pieces, low, largest):
    loudness, own = 1.0, jax.random.fold_in(stream_key, 6)
    for dim, shards_of in pieces:
        draws = jnp.exp(jax.random.uniform(jax.random.fold_in(own, dim), (shards_of,), jnp.float32, low / len(pieces), largest / len(pieces)))
        loudness = loudness * jnp.repeat(draws, dims[dim] // shards_of).reshape([-1 if axis == dim else 1 for axis in range(len(dims))])
    return loudness


def bell_draw(key, dims, scale, reach, cuts=(), held_as=jnp.bfloat16):
    loudness = shard_levels(key, dims, cuts, -0.22, 0.18) if cuts else 1.0
    values = jax.random.normal(key, dims, jnp.float32) * scale * loudness
    return jnp.minimum(jnp.maximum(values, -reach), reach).astype(held_as)


def setup_inputs(seed: int = 0) -> dict:
    streams_of = jax.random.split(jax.random.key(seed), 6)
    object_tile = bell_draw(streams_of[0], (OBJ_H, 2, OBJ_W), 0.7, 5.0, ((0, 32),), jnp.float32)
    probe = bell_draw(streams_of[1], (MODES, 2, PATCH, PATCH), 0.35, 5.0, (), jnp.float32)
    offsets = draw_offsets(jax.random.fold_in(streams_of[5], 71), 0)
    frame_ids = draw_frame_ids(jax.random.fold_in(streams_of[5], 71), 0)
    frames = jnp.clip(0.2 + 2.8 * jax.random.uniform(streams_of[4], (POSITIONS, PATCH, PATCH), jnp.float32) ** shard_levels(streams_of[4], (POSITIONS, PATCH, PATCH), ((0, 128),), -0.2, 0.2), 0.2, 3.0)
    return dict(object_tile=object_tile, probe=probe, offsets=offsets, frame_ids=frame_ids, frames=frames)


def dft_tables(size):
    line = jnp.arange(size, dtype=jnp.int32)
    product = line[:, None] * line[None, :] % size
    angle = 2.0 * math.pi / size * product.astype(jnp.float32)
    scale = 1.0 / math.sqrt(size)
    real_part = jnp.cos(angle) * scale
    imag_part = -jnp.sin(angle) * scale
    left = jnp.concatenate([jnp.concatenate([real_part, -imag_part], axis=1), jnp.concatenate([imag_part, real_part], axis=1)], axis=0)
    right = jnp.concatenate([jnp.concatenate([real_part, imag_part], axis=1), jnp.concatenate([-imag_part, real_part], axis=1)], axis=0)
    return (left.astype(jnp.bfloat16), right.astype(jnp.bfloat16))

def transform(stacked, left, right, size):
    half = jnp.einsum('ab,mbc->mac', left.astype(jnp.float32), stacked.astype(jnp.float32)).astype(jnp.bfloat16)
    joined = jnp.concatenate([half[:, :size], half[:, size:]], axis=2)
    return jnp.einsum('mac,cd->mad', joined.astype(jnp.float32), right.astype(jnp.float32))

def position_term(patch, measured, probe, left, right, size):
    probe_re = probe[:, 0]
    probe_im = probe[:, 1]
    obj_re = patch[:, 0][None]
    obj_im = patch[:, 1][None]
    exit_re = probe_re * obj_re - probe_im * obj_im
    exit_im = probe_re * obj_im + probe_im * obj_re
    exit_wave = jnp.concatenate([exit_re, exit_im], axis=1).astype(jnp.bfloat16)
    far = transform(exit_wave, left, right, size)
    far_re = far[..., :size]
    far_im = far[..., size:]
    intensity = lax.optimization_barrier(jnp.sum(far_re * far_re + far_im * far_im, axis=0))
    ratio = jnp.sqrt(measured) / jnp.sqrt(jnp.maximum(intensity, 0.1))
    diff = jnp.concatenate([far_re * (ratio - 1.0), far_im * (ratio - 1.0)], axis=1).astype(jnp.bfloat16)
    chi = transform(diff, right, left, size)
    chi_re = chi[..., :size]
    chi_im = chi[..., size:]
    grad_re = lax.optimization_barrier(jnp.sum(probe_re * chi_re + probe_im * chi_im, axis=0))
    grad_im = lax.optimization_barrier(jnp.sum(probe_re * chi_im - probe_im * chi_re, axis=0))
    return (grad_re, grad_im)

def reference(object_tile, probe, offsets, frame_ids, frames):
    left, right = dft_tables(PATCH)
    lighting = lax.optimization_barrier(jnp.sum(probe[:, 0] * probe[:, 0] + probe[:, 1] * probe[:, 1], axis=0))
    height = object_tile.shape[0]
    width = object_tile.shape[2]
    zero = jnp.zeros((), jnp.int32)

    def visit(total, index):
        row = offsets[index, 0].astype(jnp.int32)
        col = offsets[index, 1].astype(jnp.int32)
        patch = lax.dynamic_slice(object_tile, (row, zero, col), (PATCH, 2, PATCH))
        which = (index // POS_DEV * POS_DEV + frame_ids[index]).astype(jnp.int32)
        measured = lax.dynamic_index_in_dim(frames, which, 0, keepdims=False)
        grad_re, grad_im = position_term(patch, measured, probe, left, right, PATCH)
        term = jnp.stack([grad_re, grad_im, lighting], axis=1)
        current = lax.dynamic_slice(total, (row, zero, col), (PATCH, 3, PATCH))
        total = lax.dynamic_update_slice(total, current + term, (row, zero, col))
        return (total, None)
    total = jnp.zeros((height, 3, width), jnp.float32)
    total, _ = lax.scan(visit, total, jnp.arange(offsets.shape[0], dtype=jnp.int32))
    return object_tile + total[:, :2] / (total[:, 2:3] + 0.1)
```

```python
import functools

import jax
import jax.numpy as jnp
import ml_dtypes
import numpy as np
from jax import lax
from jax.experimental import pallas as pl
from jax.experimental.pallas import tpu as pltpu
from jax.sharding import PartitionSpec as P

MESH = pl.DeviceIdType.MESH
BF16 = jnp.bfloat16
F32 = jnp.float32
VMEM_LIMIT = 48 << 20


def _weight(step):
    return sum(min(part, 4 - part) for part in step)


STEPS = sorted(
    [
        step
        for step in ((a, b, c) for a in range(4) for b in range(4) for c in range(4))
        if _weight(step) < 3
    ],
    key=_weight,
) + [
    (2, 1, 0),
    (2, 3, 0),
    (0, 2, 1),
    (0, 2, 3),
    (1, 0, 2),
    (3, 0, 2),
    (1, 1, 1),
    (1, 3, 3),
    (3, 1, 3),
    (3, 3, 1),
]
ALL_STEPS = [(a, b, c) for a in range(4) for b in range(4) for c in range(4)]


def here():
    grp = lax.axis_index("grp")
    tile = lax.axis_index("tile")
    x = (grp // 2) * 2 + tile % 2
    return x, (tile // 2) % 4, tile // 8, grp % 2


def moved(place, step, sign=1):
    return tuple((at + (sign * by) % 4) % 4 for at, by in zip(place, step))


def device(place, core):
    x, y, z = place
    return ((x // 2) * 2 + core, z * 8 + y * 2 + x % 2)


def class_of(place):
    x, y, z = place
    half = (x // 2) * 2
    return (x % 2) * 16 + ((y + half) % 4) * 4 + (z + half) % 4


def enter(place, core):
    barrier = pltpu.get_barrier_semaphore()
    for step in ALL_STEPS[1:]:
        pl.semaphore_signal(
            barrier, inc=1, device_id=device(moved(place, step), core), device_id_type=MESH
        )
    pl.semaphore_signal(barrier, inc=1, device_id=device(place, 1 - core), device_id_type=MESH)
    pl.semaphore_wait(barrier, 64)


def send(source, target, sems, to):
    copy = pltpu.make_async_remote_copy(
        src_ref=source,
        dst_ref=target,
        send_sem=sems.at[0],
        recv_sem=sems.at[1],
        device_id=to,
        device_id_type=MESH,
    )
    copy.start()


def arrived(ref, sems, which):
    pltpu.make_async_copy(ref, ref, sems.at[which]).wait()


def lanes_of(shape):
    return lax.broadcasted_iota(jnp.int32, shape, len(shape) - 1)


def gather_kernel(
    obj_ref, off_ref, patch_ref, offs_ref, mine, held, shifted, stage, places, off_sems, row_sems, patch_sems, sem
):
    x, y, z, core = here()
    place = (x, y, z)
    grp = lax.axis_index("grp")
    tile = lax.axis_index("tile")
    my_class = class_of(place)

    lane = lanes_of((1, 128))
    second = (lane // 8) % 2 == 1
    row = jnp.where(second, off_ref[1, 0], off_ref[0, 0]) // 32 + lane % 8
    col = jnp.where(second, off_ref[1, 1], off_ref[0, 1]) // 32
    mine[0] = col * 128 + row

    enter(place, core)
    for k in range(1, 32):
        send(mine.at[0], offs_ref.at[k], off_sems, device(moved(place, STEPS[k]), core))
    for k in range(1, 32):
        other = (tile + k) % 32
        cls = class_of(((grp // 2) * 2 + other % 2, (other // 2) % 4, other // 8))
        send(obj_ref.at[:, cls], held.at[pl.ds(2 * tile, 2)], row_sems, (grp, other))
    offs_ref[0] = mine[0]
    held[pl.ds(2 * tile, 2)] = obj_ref[:, my_class]
    arrived(offs_ref.at[pl.ds(1, 31)], off_sems, 1)
    copy = pltpu.make_async_copy(offs_ref, places, sem)
    copy.start()
    arrived(held.at[pl.ds(0, 62)], row_sems, 1)
    copy.wait()

    for c in range(2):
        line = jnp.concatenate(
            [held.reshape(512, 128)[pl.ds(2 * q + c, 64, stride=8), :] for q in range(4)], axis=1
        )
        for s in range(4):
            turned = line if s == 0 else pltpu.roll(line, 512 - 32 * s, 1)
            for q in range(4):
                shifted[s, c, q] = turned[:, 128 * q : 128 * q + 128]

    for k in range(32):
        for p in range(2):
            value = places[k, 0, 8 * p]
            a = value & 127
            b = value >> 7
            q = b >> 2
            s = b & 3
            for c in range(2):
                for h in range(2):
                    rows = shifted[s, c, q + h, pl.ds(a, 8), :]
                    if k == 0:
                        patch_ref[p, c, h, pl.ds(8 * my_class, 8), :] = rows
                    else:
                        stage[k, p, c, h] = rows
        if k:
            send(
                stage.at[k],
                patch_ref.at[:, :, :, pl.ds(8 * my_class, 8), :],
                patch_sems,
                device(moved(place, STEPS[k], -1), core),
            )
    arrived(patch_ref.at[:, :, :, pl.ds(0, 248), :], patch_sems, 1)
    arrived(offs_ref.at[pl.ds(1, 31)], off_sems, 0)
    arrived(held.at[pl.ds(0, 62)], row_sems, 0)
    arrived(stage.at[pl.ds(1, 31)], patch_sems, 0)


def gather_rows(obj, offsets):
    return pl.pallas_call(
        gather_kernel,
        out_shape=(
            jax.ShapeDtypeStruct((2, 2, 2, 256, 128), F32),
            jax.ShapeDtypeStruct((32, 1, 128), jnp.int32),
        ),
        in_specs=[
            pl.BlockSpec(memory_space=pltpu.VMEM),
            pl.BlockSpec(memory_space=pltpu.SMEM),
        ],
        out_specs=(
            pl.BlockSpec(memory_space=pltpu.VMEM),
            pl.BlockSpec(memory_space=pltpu.VMEM),
        ),
        scratch_shapes=[
            pltpu.VMEM((1, 1, 128), jnp.int32),
            pltpu.VMEM((64, 8, 128), F32),
            pltpu.VMEM((4, 2, 4, 64, 128), F32),
            pltpu.VMEM((32, 2, 2, 2, 8, 128), F32),
            pltpu.SMEM((32, 1, 128), jnp.int32),
            pltpu.SemaphoreType.DMA((2,)),
            pltpu.SemaphoreType.DMA((2,)),
            pltpu.SemaphoreType.DMA((2,)),
            pltpu.SemaphoreType.DMA,
        ],
        compiler_params=pltpu.CompilerParams(
            collective_id=1, has_side_effects=True, vmem_limit_bytes=VMEM_LIMIT
        ),
        name="gather_rows",
    )(obj, offsets)


def tables():
    line = np.arange(256)
    angle = 2.0 * np.pi / 256 * (line[:, None] * line[None, :] % 256)
    re = (np.cos(angle) / 16).astype(ml_dtypes.bfloat16)
    im = (-np.sin(angle) / 16).astype(ml_dtypes.bfloat16)

    def real_form(table_re, table_im, left):
        if left:
            return np.block([[table_re, -table_im], [table_im, table_re]])
        return np.block([[table_re, table_im], [-table_im, table_re]])

    made = []
    for odd in range(2):
        made.append(real_form(re[odd::2, :128], im[odd::2, :128], True))
    for odd in range(2):
        made.append(real_form(re[:128, odd::2], im[:128, odd::2], False))
    for odd in range(2):
        made.append(real_form(re[:128, odd::2], -im[:128, odd::2], True))
    for odd in range(2):
        made.append(real_form(re[odd::2, :128], -im[odd::2, :128], False))
    order = np.zeros((256, 256), ml_dtypes.bfloat16)
    order[np.concatenate([line[0::2], line[1::2]]), line] = 1
    made.append(order)
    return np.stack([table.astype(ml_dtypes.bfloat16) for table in made])


def dot(a, b):
    return jnp.dot(a, b, preferred_element_type=F32)


def rows2(a, b):
    return jnp.concatenate([a, b], axis=0)


def cols2(a, b):
    return jnp.concatenate([a, b], axis=1)


def frames_kernel(
    patch_ref, probe_ref, frames_ref, ids_ref, off_ref, table_ref, out_ref, light_ref, obj, far, power, weight, grad, columns, turned
):
    for p in range(2):
        for c in range(2):
            for a in range(8):
                for h in range(2):
                    obj[p, c, 32 * a : 32 * a + 32, 128 * h : 128 * h + 128] = patch_ref[
                        p, c, h, pl.ds(a, 32, stride=8), :
                    ]
    power[...] = jnp.zeros_like(power)
    light_ref[...] = jnp.zeros_like(light_ref)

    def forward(m, carry):
        probe_re = probe_ref[m, 0]
        probe_im = probe_ref[m, 1]
        light_ref[...] += probe_re * probe_re + probe_im * probe_im
        for p in range(2):
            obj_re = obj[p, 0]
            obj_im = obj[p, 1]
            exit_re = probe_re * obj_re - probe_im * obj_im
            exit_im = probe_re * obj_im + probe_im * obj_re
            both = rows2(exit_re[:128] + exit_re[128:], exit_im[:128] + exit_im[128:]).astype(BF16)
            less = rows2(exit_re[:128] - exit_re[128:], exit_im[:128] - exit_im[128:]).astype(BF16)
            half_even = dot(table_ref[0], both)
            half_odd = dot(table_ref[1], less)
            sums = []
            lesses = []
            for half in (half_even, half_odd):
                re, im = half[:128], half[128:]
                sums.append(cols2(re[:, :128] + re[:, 128:], im[:, :128] + im[:, 128:]))
                lesses.append(cols2(re[:, :128] - re[:, 128:], im[:, :128] - im[:, 128:]))
            far_even = dot(rows2(*sums).astype(BF16), table_ref[2])
            far_odd = dot(rows2(*lesses).astype(BF16), table_ref[3])
            far[p, m, 0] = far_even
            far[p, m, 1] = far_odd
            for odd, wave in enumerate((far_even, far_odd)):
                re, im = wave[:, :128], wave[:, 128:]
                power[p, :, odd * 128 : odd * 128 + 128] += re * re + im * im
        return carry

    lax.fori_loop(0, 8, forward, 0)

    for p in range(2):
        frame = ids_ref[p]
        for h in range(2):
            columns[h] = frames_ref[frame, :, 128 * h : 128 * h + 128]
        root = jnp.sqrt(
            rows2(*[cols2(*[columns[h, pl.ds(odd, 128, stride=2), :] for h in range(2)]) for odd in range(2)])
        )
        first = root.astype(BF16)
        rest = root - first.astype(F32)
        second = rest.astype(BF16)
        third = (rest - second.astype(F32)).astype(BF16)
        order = table_ref[8]
        root = dot(first, order) + dot(second, order) + dot(third, order)
        weight[p] = root / jnp.sqrt(jnp.maximum(power[p], 0.1)) - 1.0
    grad[...] = jnp.zeros_like(grad)

    def backward(m, carry):
        probe_re = probe_ref[m, 0]
        probe_im = probe_ref[m, 1]
        for p in range(2):
            weight_even = weight[p, :, :128]
            weight_odd = weight[p, :, 128:]
            even = far[p, m, 0]
            odd = far[p, m, 1]
            diff_re = cols2(even[:, :128] * weight_even, odd[:, :128] * weight_odd).astype(BF16)
            diff_im = cols2(even[:, 128:] * weight_even, odd[:, 128:] * weight_odd).astype(BF16)
            back_even = dot(table_ref[4], rows2(diff_re[:128], diff_im[:128]))
            back_odd = dot(table_ref[5], rows2(diff_re[128:], diff_im[128:]))
            both = back_even + back_odd
            less = back_even - back_odd
            back_re = rows2(both[:128], less[:128]).astype(BF16)
            back_im = rows2(both[128:], less[128:]).astype(BF16)
            chi_even = dot(cols2(back_re[:, :128], back_im[:, :128]), table_ref[6])
            chi_odd = dot(cols2(back_re[:, 128:], back_im[:, 128:]), table_ref[7])
            both = chi_even + chi_odd
            less = chi_even - chi_odd
            chi_re = cols2(both[:, :128], less[:, :128])
            chi_im = cols2(both[:, 128:], less[:, 128:])
            grad[p, 0] += probe_re * chi_re + probe_im * chi_im
            grad[p, 1] += probe_re * chi_im - probe_im * chi_re
        return carry

    lax.fori_loop(0, 8, backward, 0)

    for p in range(2):
        turn = off_ref[p, 1] & 127
        for c in range(2):
            rolled = pltpu.roll(grad[p, c], turn, 1)
            for h in range(2):
                turned[p, c, h] = rolled[:, 128 * h : 128 * h + 128]
                for i in range(32):
                    out_ref[i, p, c, h] = turned[p, c, h, pl.ds(i, 8, stride=32), :]


def frame_terms(patch, probe, frames, frame_ids, offsets):
    vmem = pl.BlockSpec(memory_space=pltpu.VMEM)
    smem = pl.BlockSpec(memory_space=pltpu.SMEM)
    return pl.pallas_call(
        frames_kernel,
        out_shape=(
            jax.ShapeDtypeStruct((32, 2, 2, 2, 8, 128), F32),
            jax.ShapeDtypeStruct((256, 256), F32),
        ),
        in_specs=[vmem, vmem, vmem, smem, smem, vmem],
        out_specs=(vmem, vmem),
        scratch_shapes=[
            pltpu.VMEM((2, 2, 256, 256), F32),
            pltpu.VMEM((2, 8, 2, 256, 256), F32),
            pltpu.VMEM((2, 256, 256), F32),
            pltpu.VMEM((2, 256, 256), F32),
            pltpu.VMEM((2, 2, 256, 256), F32),
            pltpu.VMEM((2, 256, 128), F32),
            pltpu.VMEM((2, 2, 2, 256, 128), F32),
        ],
        compiler_params=pltpu.CompilerParams(vmem_limit_bytes=VMEM_LIMIT),
        name="frame_terms",
    )(patch, probe, frames, frame_ids, offsets, jnp.asarray(tables()))


def scatter_kernel(
    terms_ref,
    offs_ref,
    places,
    light_ref,
    obj_ref,
    out_ref,
    recv,
    counts,
    counts_in,
    totals,
    light4,
    lit,
    hits,
    split,
    summed,
    halves,
    half_in,
    rows_in,
    half_out,
    half_back,
    term_sems,
    count_sems,
    half_sems,
    row_sems,
    out_sems,
):
    x, y, z, core = here()
    place = (x, y, z)
    tile = lax.axis_index("tile")
    my_class = class_of(place)
    opposite = device(moved(place, (2, 2, 2)), core)
    twin = device(place, 1 - core)

    enter(place, core)
    for k in range(1, 32):
        to = moved(place, STEPS[k])
        send(terms_ref.at[class_of(to)], recv.at[k], term_sems, device(to, core))
    recv[0] = terms_ref[my_class]

    grid_row = lax.broadcasted_iota(jnp.int32, (64, 128), 0)
    grid_col = lax.broadcasted_iota(jnp.int32, (64, 128), 1)
    found = jnp.zeros((64, 128), F32)
    for k in range(32):
        for p in range(2):
            value = places[k, 0, 8 * p]
            found += jnp.where((grid_row == (value & 127)) & (grid_col == (value >> 7)), 1.0, 0.0)
    counts[0] = found
    send(counts.at[0], counts_in.at[0], count_sems.at[0], opposite)

    lane = lanes_of((1, 128))
    parts = []
    for u in range(4):
        part = jnp.zeros((1, 128), jnp.int32)
        for kk in range(8):
            part = jnp.where(lane // 16 == kk, offs_ref[8 * u + kk], part)
        parts.append(part)
    key = jnp.concatenate(parts, axis=1)
    goal = (key >> 9) * 64 + (key & 127)
    hits[...] = jnp.where(
        lax.broadcasted_iota(jnp.int32, (192, 512), 0) == goal, 1.0, 0.0
    ).astype(BF16)

    light = cols2(light_ref[...], jnp.zeros((256, 128), F32))
    for s in range(4):
        light4[s] = light if s == 0 else pltpu.roll(light, 32 * s, 1)

    arrived(counts.at[0], count_sems.at[0], 1)
    counts[1] = counts[0] + counts_in[0]
    send(counts.at[1], counts_in.at[1], count_sems.at[1], twin)
    arrived(counts.at[1], count_sems.at[1], 1)
    totals[0:8] = jnp.zeros((8, 128), F32)
    totals[8:72] = counts[1] + counts_in[1]
    near = totals[pl.ds(2 * tile + 1, 9), :]
    for a2 in range(2):
        for j in range(4):
            lit[j, a2] = jnp.zeros((32, 128), F32)
        for da in range(8):
            for b in range(9):
                q, s = b // 4, b % 4
                many = jnp.broadcast_to(near[a2 + 7 - da : a2 + 8 - da, b : b + 1], (32, 128))
                for j in range(q, min(q + 3, 4)):
                    if j - q == 2 and s == 0:
                        continue
                    lit[j, a2] += many * light4[s, 32 * da : 32 * da + 32, 128 * (j - q) : 128 * (j - q) + 128]

    arrived(recv.at[pl.ds(1, 31)], term_sems, 1)
    for k in range(32):
        masks = []
        for p in range(2):
            masks.append(lane >= 32 * ((places[k, 0, 8 * p] >> 7) & 3))
        for c in range(2):
            lefts = [recv[k, p, c, 0] for p in range(2)]
            right = rows2(recv[k, 0, c, 1], recv[k, 1, c, 1])
            near_part = rows2(*[jnp.where(masks[p], lefts[p], 0.0) for p in range(2)])
            wrapped = rows2(*[jnp.where(masks[p], 0.0, lefts[p]) for p in range(2)])
            for kind, piece in enumerate((near_part, right, wrapped)):
                high = piece.astype(BF16)
                at = kind * 256 + c * 128
                split[0, 16 * k : 16 * k + 16, at : at + 128] = high
                split[1, 16 * k : 16 * k + 16, at : at + 128] = (piece - high.astype(F32)).astype(BF16)
    result = dot(hits[...], split[0]) + dot(hits[...], split[1])
    for j in range(4):
        for c in range(2):
            total = jnp.zeros((64, 128), F32)
            for kind in range(3):
                if 0 <= j - kind <= 2:
                    at = kind * 256 + c * 128
                    total += result[64 * (j - kind) : 64 * (j - kind) + 64, at : at + 128]
            summed[j, c] = total
    for j in range(4):
        for c in range(2):
            for a2 in range(2):
                halves[j // 2, pl.ds(a2 * 4 + (j % 2) * 2 + c, 32, stride=8), :] = summed[
                    j, c, pl.ds(a2, 32, stride=2), :
                ]
    send(halves.at[1 - core], half_in, half_sems, twin)
    arrived(half_in, half_sems, 1)
    arrived(half_in, half_sems, 0)
    halves[core] += half_in[...]

    mine = halves.at[core]
    for step in ALL_STEPS[1:]:
        to = moved(place, step)
        goal_tile = to[2] * 8 + to[1] * 2 + to[0] % 2
        send(
            mine.at[pl.ds(8 * goal_tile, 8)],
            rows_in.at[pl.ds(8 * ((x // 2) * 32 + my_class), 8)],
            row_sems,
            device(to, core),
        )
    rows_in[pl.ds(8 * ((x // 2) * 32 + my_class), 8)] = halves[core, pl.ds(8 * tile, 8)]
    arrived(rows_in.at[pl.ds(0, 504)], row_sems, 1)
    flat = out_ref.reshape(512, 128)
    source = obj_ref.reshape(512, 128)
    for a2 in range(2):
        for jj in range(2):
            under = lit[2 * core + jj, a2] + 0.1
            for c in range(2):
                e = a2 * 4 + jj * 2 + c
                total = rows_in[pl.ds(e, 32, stride=8), :] + rows_in[pl.ds(256 + e, 32, stride=8), :]
                at = pl.ds(a2 * 256 + core * 4 + jj * 2 + c, 32, stride=8)
                done = source[at, :] + total / under
                flat[at, :] = done
                half_out[pl.ds(e, 32, stride=8), :] = done
    send(half_out, half_back, out_sems, twin)
    arrived(half_back, out_sems, 1)
    for a2 in range(2):
        for e in range(4):
            flat[pl.ds(a2 * 256 + (1 - core) * 4 + e, 32, stride=8), :] = half_back[
                pl.ds(a2 * 4 + e, 32, stride=8), :
            ]
    arrived(recv.at[pl.ds(1, 31)], term_sems, 0)
    arrived(counts.at[0], count_sems.at[0], 0)
    arrived(counts.at[1], count_sems.at[1], 0)
    arrived(rows_in.at[pl.ds(0, 504)], row_sems, 0)
    arrived(half_out, out_sems, 0)


def scatter_rows(terms, offs, light, obj):
    vmem = pl.BlockSpec(memory_space=pltpu.VMEM)
    smem = pl.BlockSpec(memory_space=pltpu.SMEM)
    return pl.pallas_call(
        scatter_kernel,
        out_shape=jax.ShapeDtypeStruct((64, 8, 128), F32),
        in_specs=[vmem, vmem, smem, vmem, vmem],
        out_specs=vmem,
        scratch_shapes=[
            pltpu.VMEM((32, 2, 2, 2, 8, 128), F32),
            pltpu.VMEM((2, 64, 128), F32),
            pltpu.VMEM((2, 64, 128), F32),
            pltpu.VMEM((72, 128), F32),
            pltpu.VMEM((4, 256, 384), F32),
            pltpu.VMEM((4, 2, 32, 128), F32),
            pltpu.VMEM((192, 512), BF16),
            pltpu.VMEM((2, 512, 768), BF16),
            pltpu.VMEM((4, 2, 64, 128), F32),
            pltpu.VMEM((2, 256, 128), F32),
            pltpu.VMEM((256, 128), F32),
            pltpu.VMEM((512, 128), F32),
            pltpu.VMEM((256, 128), F32),
            pltpu.VMEM((256, 128), F32),
            pltpu.SemaphoreType.DMA((2,)),
            pltpu.SemaphoreType.DMA((2, 2)),
            pltpu.SemaphoreType.DMA((2,)),
            pltpu.SemaphoreType.DMA((2,)),
            pltpu.SemaphoreType.DMA((2,)),
        ],
        compiler_params=pltpu.CompilerParams(
            collective_id=2, has_side_effects=True, vmem_limit_bytes=VMEM_LIMIT
        ),
        name="scatter_rows",
    )(terms, offs, offs, light, obj)


def on_device(object_tile, probe, offsets, frame_ids, frames):
    obj = object_tile.reshape(64, 2, 4, 128).transpose(0, 2, 1, 3).reshape(64, 8, 128)
    patch, offs = gather_rows(obj.reshape(2, 32, 8, 128), offsets)
    terms, light = frame_terms(patch, probe, frames, frame_ids, offsets)
    updated = scatter_rows(terms, offs, light, obj)
    return updated.reshape(64, 4, 2, 128).transpose(0, 2, 1, 3).reshape(64, 2, 512)


def solution(mesh):
    in_specs = (
        P("tile", None, None),
        P(),
        P(("grp", "tile"), None),
        P(("grp", "tile")),
        P(("grp", "tile"), None, None),
    )
    out_specs = P("tile", None, None)
    return jax.shard_map(
        on_device, mesh=mesh, in_specs=in_specs, out_specs=out_specs, check_vma=False
    )
```

```python
import functools

import jax
import jax.numpy as jnp
import ml_dtypes
import numpy as np
from jax import lax
from jax.experimental import pallas as pl
from jax.experimental.pallas import tpu as pltpu
from jax.sharding import PartitionSpec as P

MESH = pl.DeviceIdType.MESH
BF16 = jnp.bfloat16
F32 = jnp.float32
VMEM_LIMIT = 60 << 20


def _weight(step):
    return sum(min(part, 4 - part) for part in step)


STEPS = sorted(
    [
        step
        for step in ((a, b, c) for a in range(4) for b in range(4) for c in range(4))
        if _weight(step) < 3
    ],
    key=_weight,
) + [
    (2, 1, 0),
    (2, 3, 0),
    (0, 2, 1),
    (0, 2, 3),
    (1, 0, 2),
    (3, 0, 2),
    (1, 1, 1),
    (1, 3, 3),
    (3, 1, 3),
    (3, 3, 1),
]
ALL_STEPS = [(a, b, c) for a in range(4) for b in range(4) for c in range(4)]


def here():
    grp = lax.axis_index("grp")
    tile = lax.axis_index("tile")
    x = (grp // 2) * 2 + tile % 2
    return x, (tile // 2) % 4, tile // 8, grp % 2


def moved(place, step, sign=1):
    return tuple((at + (sign * by) % 4) % 4 for at, by in zip(place, step))


def device(place, core):
    x, y, z = place
    return ((x // 2) * 2 + core, z * 8 + y * 2 + x % 2)


def class_of(place):
    x, y, z = place
    half = (x // 2) * 2
    return (x % 2) * 16 + ((y + half) % 4) * 4 + (z + half) % 4


def enter(place, core):
    barrier = pltpu.get_barrier_semaphore()
    for step in ALL_STEPS[1:]:
        pl.semaphore_signal(
            barrier, inc=1, device_id=device(moved(place, step), core), device_id_type=MESH
        )
    pl.semaphore_signal(barrier, inc=1, device_id=device(place, 1 - core), device_id_type=MESH)
    pl.semaphore_wait(barrier, 64)


def send(source, target, sems, to):
    copy = pltpu.make_async_remote_copy(
        src_ref=source,
        dst_ref=target,
        send_sem=sems.at[0],
        recv_sem=sems.at[1],
        device_id=to,
        device_id_type=MESH,
    )
    copy.start()


def arrived(ref, sems, which):
    pltpu.make_async_copy(ref, ref, sems.at[which]).wait()


def lanes_of(shape):
    return lax.broadcasted_iota(jnp.int32, shape, len(shape) - 1)


def tables():
    line = np.arange(256)
    angle = 2.0 * np.pi / 256 * (line[:, None] * line[None, :] % 256)
    re = (np.cos(angle) / 16).astype(ml_dtypes.bfloat16)
    im = (-np.sin(angle) / 16).astype(ml_dtypes.bfloat16)

    def real_form(table_re, table_im, left):
        if left:
            return np.block([[table_re, -table_im], [table_im, table_re]])
        return np.block([[table_re, table_im], [-table_im, table_re]])

    made = []
    for odd in range(2):
        made.append(real_form(re[odd::2, :128], im[odd::2, :128], True))
    for odd in range(2):
        made.append(real_form(re[:128, odd::2], im[:128, odd::2], False))
    for odd in range(2):
        made.append(real_form(re[:128, odd::2], -im[:128, odd::2], True))
    for odd in range(2):
        made.append(real_form(re[odd::2, :128], -im[odd::2, :128], False))
    order = np.zeros((256, 256), ml_dtypes.bfloat16)
    order[np.concatenate([line[0::2], line[1::2]]), line] = 1
    made.append(order)
    return np.stack([table.astype(ml_dtypes.bfloat16) for table in made])


def dot(a, b):
    return jnp.dot(a, b, preferred_element_type=F32)


def rows2(a, b):
    return jnp.concatenate([a, b], axis=0)


def cols2(a, b):
    return jnp.concatenate([a, b], axis=1)


def forward(p, m, obj, probe, table, far, power):
    gained = [0.0, 0.0]
    for mode in (2 * m, 2 * m + 1):
        probe_re = probe[mode, 0]
        probe_im = probe[mode, 1]
        obj_re = obj[0]
        obj_im = obj[1]
        exit_re = probe_re * obj_re - probe_im * obj_im
        exit_im = probe_re * obj_im + probe_im * obj_re
        both = rows2(exit_re[:128] + exit_re[128:], exit_im[:128] + exit_im[128:]).astype(BF16)
        less = rows2(exit_re[:128] - exit_re[128:], exit_im[:128] - exit_im[128:]).astype(BF16)
        sums = []
        lesses = []
        for half in (dot(table[0], both), dot(table[1], less)):
            re, im = half[:128], half[128:]
            sums.append(cols2(re[:, :128] + re[:, 128:], im[:, :128] + im[:, 128:]))
            lesses.append(cols2(re[:, :128] - re[:, 128:], im[:, :128] - im[:, 128:]))
        far_even = dot(rows2(*sums).astype(BF16), table[2])
        far_odd = dot(rows2(*lesses).astype(BF16), table[3])
        far[mode, 0] = far_even
        far[mode, 1] = far_odd
        for odd, wave in enumerate((far_even, far_odd)):
            re, im = wave[:, :128], wave[:, 128:]
            gained[odd] += re * re + im * im
    for odd in range(2):
        power[:, odd * 128 : odd * 128 + 128] += gained[odd]


def backward(m, probe, table, far, weight, grad):
    weight_even = weight[:, :128]
    weight_odd = weight[:, 128:]
    gained = [0.0, 0.0]
    for mode in (2 * m, 2 * m + 1):
        probe_re = probe[mode, 0]
        probe_im = probe[mode, 1]
        even = far[mode, 0]
        odd = far[mode, 1]
        diff_re = cols2(even[:, :128] * weight_even, odd[:, :128] * weight_odd).astype(BF16)
        diff_im = cols2(even[:, 128:] * weight_even, odd[:, 128:] * weight_odd).astype(BF16)
        back_even = dot(table[4], rows2(diff_re[:128], diff_im[:128]))
        back_odd = dot(table[5], rows2(diff_re[128:], diff_im[128:]))
        both = back_even + back_odd
        less = back_even - back_odd
        back_re = rows2(both[:128], less[:128]).astype(BF16)
        back_im = rows2(both[128:], less[128:]).astype(BF16)
        chi_even = dot(cols2(back_re[:, :128], back_im[:, :128]), table[6])
        chi_odd = dot(cols2(back_re[:, 128:], back_im[:, 128:]), table[7])
        both = chi_even + chi_odd
        less = chi_even - chi_odd
        chi_re = cols2(both[:, :128], less[:, :128])
        chi_im = cols2(both[:, 128:], less[:, 128:])
        gained[0] += probe_re * chi_re + probe_im * chi_im
        gained[1] += probe_re * chi_im - probe_im * chi_re
    for c in range(2):
        grad[c] += gained[c]


def detector_roots(frames, frame, columns, table, root):
    for h in range(2):
        columns[h] = frames[frame, :, 128 * h : 128 * h + 128]
    value = jnp.sqrt(
        rows2(*[cols2(*[columns[h, pl.ds(odd, 128, stride=2), :] for h in range(2)]) for odd in range(2)])
    )
    first = value.astype(BF16)
    rest = value - first.astype(F32)
    second = rest.astype(BF16)
    third = (rest - second.astype(F32)).astype(BF16)
    order = table[8]
    root[...] = dot(first, order) + dot(second, order) + dot(third, order)


def kernel(
    obj_hbm,
    probe_hbm,
    frames_hbm,
    table_hbm,
    off_ref,
    ids_ref,
    out_ref,
    tile_rows,
    probe,
    frames,
    table,
    mine,
    offs,
    places,
    held,
    shifted,
    stage,
    patch,
    obj,
    columns,
    roots,
    far,
    power,
    weight,
    grad,
    turned,
    terms,
    recv,
    counts,
    counts_in,
    totals,
    light4,
    lit,
    hits,
    split,
    result,
    summed,
    halves,
    half_in,
    rows_in,
    half_out,
    half_back,
    load_sems,
    off_sems,
    row_sems,
    patch_sems,
    term_sems,
    count_sems,
    half_sems,
    last_sems,
    out_sems,
):
    x, y, z, core = here()
    place = (x, y, z)
    grp = lax.axis_index("grp")
    tile = lax.axis_index("tile")
    my_class = class_of(place)
    opposite = device(moved(place, (2, 2, 2)), core)
    twin = device(place, 1 - core)
    loads = [
        pltpu.make_async_copy(source, target, load_sems.at[i])
        for i, (source, target) in enumerate(
            ((obj_hbm, tile_rows), (probe_hbm, probe), (table_hbm, table), (frames_hbm, frames))
        )
    ]
    for load in loads:
        load.start()

    lane = lanes_of((1, 128))
    for p in range(2):
        mine[0, p : p + 1] = (off_ref[p, 1] // 32) * 128 + off_ref[p, 0] // 32 + lane % 8
    enter(place, core)
    for k in range(1, 32):
        send(mine.at[0], offs.at[k], off_sems, device(moved(place, STEPS[k]), core))
    loads[0].wait()
    for k in range(1, 32):
        other = (tile + k) % 32
        cls = class_of(((grp // 2) * 2 + other % 2, (other // 2) % 4, other // 8))
        send(tile_rows.at[:, cls], held.at[pl.ds(2 * tile, 2)], row_sems, (grp, other))
    offs[0] = mine[0]
    held[pl.ds(2 * tile, 2)] = tile_rows[:, my_class]

    for load in loads[1:]:
        load.wait()

    def add_light(m, total):
        return total + probe[m, 0] * probe[m, 0] + probe[m, 1] * probe[m, 1]

    light = cols2(lax.fori_loop(0, 8, add_light, jnp.zeros((256, 256), F32)), jnp.zeros((256, 128), F32))
    for s in range(4):
        light4[s] = light if s == 0 else pltpu.roll(light, 32 * s, 1)
    for p in range(2):
        detector_roots(frames, ids_ref[p], columns, table, roots.at[p])
    for a2 in range(2):
        for j in range(4):
            lit[j, a2] = jnp.zeros((32, 128), F32)

    arrived(offs.at[pl.ds(1, 31)], off_sems, 1)
    copy = pltpu.make_async_copy(offs, places, load_sems.at[4])
    copy.start()
    arrived(held.at[pl.ds(0, 62)], row_sems, 1)
    copy.wait()
    for c in range(2):
        line = jnp.concatenate(
            [held.reshape(512, 128)[pl.ds(2 * q + c, 64, stride=8), :] for q in range(4)], axis=1
        )
        for s in range(4):
            moved_line = line if s == 0 else pltpu.roll(line, 512 - 32 * s, 1)
            for q in range(4):
                shifted[s, c, q] = moved_line[:, 128 * q : 128 * q + 128]
    for p in range(2):
        for k in range(32):
            value = places[k, p, 0]
            a = value & 127
            b = value >> 7
            q = b >> 2
            s = b & 3
            for c in range(2):
                for h in range(2):
                    rows = shifted[s, c, q + h, pl.ds(a, 8), :]
                    if k == 0:
                        patch[p, c, h, pl.ds(8 * my_class, 8), :] = rows
                    else:
                        stage[p, k, c, h] = rows
            if k:
                send(
                    stage.at[p, k],
                    patch.at[p, :, :, pl.ds(8 * my_class, 8), :],
                    patch_sems.at[p],
                    device(moved(place, STEPS[k], -1), core),
                )

    grid_row = lax.broadcasted_iota(jnp.int32, (64, 128), 0)
    grid_col = lax.broadcasted_iota(jnp.int32, (64, 128), 1)
    found = jnp.zeros((64, 128), F32)
    for k in range(32):
        for p in range(2):
            value = places[k, p, 0]
            found += jnp.where((grid_row == (value & 127)) & (grid_col == (value >> 7)), 1.0, 0.0)
    counts[0] = found
    send(counts.at[0], counts_in.at[0], count_sems.at[0], opposite)
    for p in range(2):
        parts = []
        for u in range(2):
            part = jnp.zeros((1, 128), jnp.int32)
            for kk in range(16):
                part = jnp.where(lane // 8 == kk, offs[16 * u + kk, p : p + 1], part)
            parts.append(part)
        key = cols2(*parts)
        goal = (key >> 9) * 64 + (key & 127)
        hits[p] = jnp.where(lax.broadcasted_iota(jnp.int32, (192, 256), 0) == goal, 1.0, 0.0).astype(BF16)

    for p in range(2):
        arrived(patch.at[p, :, :, pl.ds(0, 248), :], patch_sems.at[p], 1)
        for c in range(2):
            for a in range(8):
                for h in range(2):
                    obj[c, 32 * a : 32 * a + 32, 128 * h : 128 * h + 128] = patch[
                        p, c, h, pl.ds(a, 32, stride=8), :
                    ]
        power[...] = jnp.zeros_like(power)

        def ahead(m, carry):
            forward(p, m, obj, probe, table, far, power)
            return carry

        lax.fori_loop(0, 4, ahead, 0)
        weight[...] = roots[p] / jnp.sqrt(jnp.maximum(power[...], 0.1)) - 1.0
        grad[...] = jnp.zeros_like(grad)

        def behind(m, carry):
            backward(m, probe, table, far, weight, grad)
            return carry

        lax.fori_loop(0, 4, behind, 0)
        turn = off_ref[p, 1] & 127
        for c in range(2):
            rolled = pltpu.roll(grad[c], turn, 1)
            for h in range(2):
                turned[c, h] = rolled[:, 128 * h : 128 * h + 128]
        for i in range(32):
            for c in range(2):
                for h in range(2):
                    terms[p, i, c, h] = turned[c, h, pl.ds(i, 8, stride=32), :]
        for k in range(1, 32):
            to = moved(place, STEPS[k])
            send(terms.at[p, class_of(to)], recv.at[p, k], term_sems.at[p], device(to, core))
        recv[p, 0] = terms[p, my_class]
        if p == 0:
            arrived(counts.at[0], count_sems.at[0], 1)
            counts[1] = counts[0] + counts_in[0]
            send(counts.at[1], counts_in.at[1], count_sems.at[1], twin)

    arrived(counts.at[1], count_sems.at[1], 1)
    totals[0:8] = jnp.zeros((8, 128), F32)
    totals[8:72] = counts[1] + counts_in[1]
    near = totals[pl.ds(2 * tile + 1, 9), :]
    for a2 in range(2):
        for da in range(8):
            for b in range(9):
                q, s = b // 4, b % 4
                many = jnp.broadcast_to(near[a2 + 7 - da : a2 + 8 - da, b : b + 1], (32, 128))
                for j in range(q, min(q + 3, 4)):
                    if j - q == 2 and s == 0:
                        continue
                    lit[j, a2] += many * light4[s, 32 * da : 32 * da + 32, 128 * (j - q) : 128 * (j - q) + 128]

    for p in range(2):
        arrived(recv.at[p, pl.ds(1, 31)], term_sems.at[p], 1)
        for k in range(0, 32, 2):
            masks = [lane >= 32 * ((places[k + d, p, 0] >> 7) & 3) for d in range(2)]
            for c in range(2):
                lefts = [recv[p, k + d, c, 0] for d in range(2)]
                right = rows2(recv[p, k, c, 1], recv[p, k + 1, c, 1])
                own = rows2(*[jnp.where(masks[d], lefts[d], 0.0) for d in range(2)])
                wrapped = rows2(*[jnp.where(masks[d], 0.0, lefts[d]) for d in range(2)])
                for kind, piece in enumerate((own, right, wrapped)):
                    high = piece.astype(BF16)
                    at = kind * 256 + c * 128
                    split[0, 8 * k : 8 * k + 16, at : at + 128] = high
                    split[1, 8 * k : 8 * k + 16, at : at + 128] = (piece - high.astype(F32)).astype(BF16)
        part = dot(hits[p], split[0]) + dot(hits[p], split[1])
        if p == 0:
            result[...] = part
        else:
            result[...] += part
    for j in range(4):
        for c in range(2):
            total = jnp.zeros((64, 128), F32)
            for kind in range(3):
                if 0 <= j - kind <= 2:
                    at = kind * 256 + c * 128
                    total += result[64 * (j - kind) : 64 * (j - kind) + 64, at : at + 128]
            summed[j, c] = total
    for j in range(4):
        for c in range(2):
            for a2 in range(2):
                halves[j // 2, pl.ds(a2 * 4 + (j % 2) * 2 + c, 32, stride=8), :] = summed[
                    j, c, pl.ds(a2, 32, stride=2), :
                ]

    send(halves.at[1 - core], half_in, half_sems, twin)
    arrived(half_in, half_sems, 1)
    arrived(half_in, half_sems, 0)
    halves[core] += half_in[...]
    own_half = halves.at[core]
    for step in ALL_STEPS[1:]:
        to = moved(place, step)
        goal_tile = to[2] * 8 + to[1] * 2 + to[0] % 2
        send(
            own_half.at[pl.ds(8 * goal_tile, 8)],
            rows_in.at[pl.ds(8 * ((x // 2) * 32 + my_class), 8)],
            last_sems,
            device(to, core),
        )
    rows_in[pl.ds(8 * ((x // 2) * 32 + my_class), 8)] = halves[core, pl.ds(8 * tile, 8)]
    arrived(rows_in.at[pl.ds(0, 504)], last_sems, 1)
    flat = out_ref.reshape(512, 128)
    source = tile_rows.reshape(512, 128)
    for a2 in range(2):
        for jj in range(2):
            under = lit[2 * core + jj, a2] + 0.1
            for c in range(2):
                e = a2 * 4 + jj * 2 + c
                total = rows_in[pl.ds(e, 32, stride=8), :] + rows_in[pl.ds(256 + e, 32, stride=8), :]
                at = pl.ds(a2 * 256 + core * 4 + jj * 2 + c, 32, stride=8)
                done = source[at, :] + total / under
                flat[at, :] = done
                half_out[pl.ds(e, 32, stride=8), :] = done
    send(half_out, half_back, out_sems, twin)
    arrived(half_back, out_sems, 1)
    for a2 in range(2):
        for e in range(4):
            flat[pl.ds(a2 * 256 + (1 - core) * 4 + e, 32, stride=8), :] = half_back[
                pl.ds(a2 * 4 + e, 32, stride=8), :
            ]

    arrived(offs.at[pl.ds(1, 31)], off_sems, 0)
    arrived(held.at[pl.ds(0, 62)], row_sems, 0)
    for p in range(2):
        arrived(stage.at[p, pl.ds(1, 31)], patch_sems.at[p], 0)
        arrived(recv.at[p, pl.ds(1, 31)], term_sems.at[p], 0)
        arrived(counts.at[p], count_sems.at[p], 0)
    arrived(rows_in.at[pl.ds(0, 504)], last_sems, 0)
    arrived(half_out, out_sems, 0)


def on_device(object_tile, probe, offsets, frame_ids, frames):
    obj = object_tile.reshape(64, 2, 4, 128).transpose(0, 2, 1, 3).reshape(2, 32, 8, 128)
    smem = pl.BlockSpec(memory_space=pltpu.SMEM)
    hbm = pl.BlockSpec(memory_space=pl.ANY)
    pair = pltpu.SemaphoreType.DMA((2,))
    updated = pl.pallas_call(
        kernel,
        out_shape=jax.ShapeDtypeStruct((64, 8, 128), F32),
        in_specs=[hbm, hbm, hbm, hbm, smem, smem],
        out_specs=pl.BlockSpec(memory_space=pltpu.VMEM),
        scratch_shapes=[
            pltpu.VMEM((2, 32, 8, 128), F32),
            pltpu.VMEM((8, 2, 256, 256), F32),
            pltpu.VMEM((2, 256, 256), F32),
            pltpu.VMEM((9, 256, 256), BF16),
            pltpu.VMEM((1, 2, 128), jnp.int32),
            pltpu.VMEM((32, 2, 128), jnp.int32),
            pltpu.SMEM((32, 2, 128), jnp.int32),
            pltpu.VMEM((64, 8, 128), F32),
            pltpu.VMEM((4, 2, 4, 64, 128), F32),
            pltpu.VMEM((2, 32, 2, 2, 8, 128), F32),
            pltpu.VMEM((2, 2, 2, 256, 128), F32),
            pltpu.VMEM((2, 256, 256), F32),
            pltpu.VMEM((2, 256, 128), F32),
            pltpu.VMEM((2, 256, 256), F32),
            pltpu.VMEM((8, 2, 256, 256), F32),
            pltpu.VMEM((256, 256), F32),
            pltpu.VMEM((256, 256), F32),
            pltpu.VMEM((2, 256, 256), F32),
            pltpu.VMEM((2, 2, 256, 128), F32),
            pltpu.VMEM((2, 32, 2, 2, 8, 128), F32),
            pltpu.VMEM((2, 32, 2, 2, 8, 128), F32),
            pltpu.VMEM((2, 64, 128), F32),
            pltpu.VMEM((2, 64, 128), F32),
            pltpu.VMEM((72, 128), F32),
            pltpu.VMEM((4, 256, 384), F32),
            pltpu.VMEM((4, 2, 32, 128), F32),
            pltpu.VMEM((2, 192, 256), BF16),
            pltpu.VMEM((2, 256, 768), BF16),
            pltpu.VMEM((192, 768), F32),
            pltpu.VMEM((4, 2, 64, 128), F32),
            pltpu.VMEM((2, 256, 128), F32),
            pltpu.VMEM((256, 128), F32),
            pltpu.VMEM((512, 128), F32),
            pltpu.VMEM((256, 128), F32),
            pltpu.VMEM((256, 128), F32),
            pltpu.SemaphoreType.DMA((5,)),
            pair,
            pair,
            pltpu.SemaphoreType.DMA((2, 2)),
            pltpu.SemaphoreType.DMA((2, 2)),
            pltpu.SemaphoreType.DMA((2, 2)),
            pair,
            pair,
            pair,
        ],
        compiler_params=pltpu.CompilerParams(
            collective_id=1, has_side_effects=True, vmem_limit_bytes=VMEM_LIMIT
        ),
        name="iteration",
    )(obj, probe, frames, jnp.asarray(tables()), offsets, frame_ids)
    return updated.reshape(64, 4, 2, 128).transpose(0, 2, 1, 3).reshape(64, 2, 512)


def solution(mesh):
    in_specs = (
        P("tile", None, None),
        P(),
        P(("grp", "tile"), None),
        P(("grp", "tile")),
        P(("grp", "tile"), None, None),
    )
    out_specs = P("tile", None, None)
    return jax.shard_map(
        on_device, mesh=mesh, in_specs=in_specs, out_specs=out_specs, check_vma=False
    )
```

```python
import functools

import jax
import jax.numpy as jnp
import ml_dtypes
import numpy as np
from jax import lax
from jax.experimental import pallas as pl
from jax.experimental.pallas import tpu as pltpu
from jax.sharding import PartitionSpec as P

MESH = pl.DeviceIdType.MESH
BF16 = jnp.bfloat16
F32 = jnp.float32
VMEM_LIMIT = 60 << 20


def _weight(step):
    return sum(min(part, 4 - part) for part in step)


STEPS = sorted(
    [
        step
        for step in ((a, b, c) for a in range(4) for b in range(4) for c in range(4))
        if _weight(step) < 3
    ],
    key=_weight,
) + [
    (2, 1, 0),
    (2, 3, 0),
    (0, 2, 1),
    (0, 2, 3),
    (1, 0, 2),
    (3, 0, 2),
    (1, 1, 1),
    (1, 3, 3),
    (3, 1, 3),
    (3, 3, 1),
]
ALL_STEPS = sorted(
    ((a, b, c) for a in range(4) for b in range(4) for c in range(4)), key=_weight, reverse=True
)[:-1]
FAR_FIRST = sorted(range(1, 32), key=lambda k: _weight(STEPS[k]), reverse=True)


class Place:
    def __init__(self):
        grp = lax.axis_index("grp")
        tile = lax.axis_index("tile")
        self.grp, self.tile = grp, tile
        self.core = lax.rem(grp, 2)
        self.x = lax.div(grp, 2) * 2 + lax.rem(tile, 2)
        self.y = lax.rem(lax.div(tile, 2), 4)
        self.z = lax.div(tile, 8)
        self.known = {}

    def once(self, name, make):
        if name not in self.known:
            self.known[name] = make()
        return self.known[name]

    def at(self, axis, by):
        by %= 4
        return self.once((axis, by), lambda: lax.rem(getattr(self, axis) + by, 4) if by else getattr(self, axis))

    def half(self, dx):
        return self.once(("half", dx % 4), lambda: lax.div(self.at("x", dx), 2) * 2)

    def tile_at(self, dx, dy, dz):
        plane = self.once(("plane", dx % 4, dy % 4), lambda: self.at("y", dy) * 2 + lax.rem(self.at("x", dx), 2))
        return self.once(("z8", dz % 4), lambda: self.at("z", dz) * 8) + plane

    def device(self, step, sign=1):
        dx, dy, dz = (sign * by for by in step)
        grp = self.once(("grp", dx % 4), lambda: self.half(dx) + self.core)
        return grp, self.tile_at(dx, dy, dz)

    def twin(self):
        return self.half(0) + 1 - self.core, self.tile

    def class_at(self, dx, dy, dz):
        near = self.once(
            ("near", dx % 4, dy % 4),
            lambda: lax.rem(self.at("x", dx), 2) * 16 + lax.rem(self.at("y", dy) + self.half(dx), 4) * 4,
        )
        return near + self.once(("deep", dx % 4, dz % 4), lambda: lax.rem(self.at("z", dz) + self.half(dx), 4))


def enter(place):
    barrier = pltpu.get_barrier_semaphore()
    for to in row_partners(place):
        pl.semaphore_signal(barrier, inc=1, device_id=to[:2], device_id_type=MESH)
    odd = lax.rem(place.tile, 2)
    beside = [step for step in STEPS if step[0] == 2]
    for step in beside:
        pl.semaphore_signal(barrier, inc=1, device_id=place.device(step, -1), device_id_type=MESH)
    ups = [step for step in STEPS if step[0] == 1]
    downs = [step for step in STEPS if step[0] == 3]
    assert len(ups) == len(downs)
    for up, down in zip(ups, downs):
        grp_a, tile_a = place.device(up, -1)
        grp_b, tile_b = place.device(down, -1)
        to = (grp_a + odd * (grp_b - grp_a), tile_a + odd * (tile_b - tile_a))
        pl.semaphore_signal(barrier, inc=1, device_id=to, device_id_type=MESH)
    pl.semaphore_signal(barrier, inc=1, device_id=place.twin(), device_id_type=MESH)
    pl.semaphore_wait(barrier, 31 + len(beside) + len(ups) + 1)


def row_partners(place):
    across = lax.rem(place.tile + 1, 2) - lax.rem(place.tile, 2)
    partners = []
    for dx, dy, dz in sorted(
        ((a, b, c) for a in range(2) for b in range(4) for c in range(4)), key=_weight, reverse=True
    )[:-1]:
        plane = place.tile_at(0, dy, dz)
        cls = place.class_at(0, dy, dz)
        partners.append((place.grp, plane + dx * across, cls + 16 * dx * across))
    return partners


def send(source, target, sems, to):
    copy = pltpu.make_async_remote_copy(
        src_ref=source,
        dst_ref=target,
        send_sem=sems.at[0],
        recv_sem=sems.at[1],
        device_id=to,
        device_id_type=MESH,
    )
    copy.start()


def arrived(ref, sems, which):
    pltpu.make_async_copy(ref, ref, sems.at[which]).wait()


def lanes_of(shape):
    return lax.broadcasted_iota(jnp.int32, shape, len(shape) - 1)


def tables():
    line = np.arange(256)
    angle = 2.0 * np.pi / 256 * (line[:, None] * line[None, :] % 256)
    re = (np.cos(angle) / 16).astype(ml_dtypes.bfloat16)
    im = (-np.sin(angle) / 16).astype(ml_dtypes.bfloat16)

    def real_form(table_re, table_im, left):
        if left:
            return np.block([[table_re, -table_im], [table_im, table_re]])
        return np.block([[table_re, table_im], [-table_im, table_re]])

    made = []
    for odd in range(2):
        made.append(real_form(re[odd::2, :128], im[odd::2, :128], True))
    for odd in range(2):
        made.append(real_form(re[:128, odd::2], im[:128, odd::2], False))
    for odd in range(2):
        made.append(real_form(re[:128, odd::2], -im[:128, odd::2], True))
    for odd in range(2):
        made.append(real_form(re[odd::2, :128], -im[odd::2, :128], False))
    order = np.zeros((256, 256), ml_dtypes.bfloat16)
    order[np.concatenate([line[0::2], line[1::2]]), line] = 1
    made.append(order)
    return np.stack([table.astype(ml_dtypes.bfloat16) for table in made])


def dot(a, b):
    return jnp.dot(a, b, preferred_element_type=F32)


def rows2(a, b):
    return jnp.concatenate([a, b], axis=0)


def cols2(a, b):
    return jnp.concatenate([a, b], axis=1)


def forward(obj, probe, table, far, power):
    gained = [0.0, 0.0]
    for mode in range(8):
        probe_re = probe[mode, 0]
        probe_im = probe[mode, 1]
        obj_re = obj[0]
        obj_im = obj[1]
        exit_re = probe_re * obj_re - probe_im * obj_im
        exit_im = probe_re * obj_im + probe_im * obj_re
        both = rows2(exit_re[:128] + exit_re[128:], exit_im[:128] + exit_im[128:]).astype(BF16)
        less = rows2(exit_re[:128] - exit_re[128:], exit_im[:128] - exit_im[128:]).astype(BF16)
        sums = []
        lesses = []
        for half in (dot(table[0], both), dot(table[1], less)):
            re, im = half[:128], half[128:]
            sums.append(cols2(re[:, :128] + re[:, 128:], im[:, :128] + im[:, 128:]))
            lesses.append(cols2(re[:, :128] - re[:, 128:], im[:, :128] - im[:, 128:]))
        far_even = dot(rows2(*sums).astype(BF16), table[2])
        far_odd = dot(rows2(*lesses).astype(BF16), table[3])
        far[mode, 0] = far_even
        far[mode, 1] = far_odd
        for odd, wave in enumerate((far_even, far_odd)):
            re, im = wave[:, :128], wave[:, 128:]
            gained[odd] += re * re + im * im
    for odd in range(2):
        power[:, odd * 128 : odd * 128 + 128] = gained[odd]


def backward(probe, table, far, weight, grad):
    weight_even = weight[:, :128]
    weight_odd = weight[:, 128:]
    gained = [0.0, 0.0]
    for mode in range(8):
        probe_re = probe[mode, 0]
        probe_im = probe[mode, 1]
        even = far[mode, 0]
        odd = far[mode, 1]
        diff_re = cols2(even[:, :128] * weight_even, odd[:, :128] * weight_odd).astype(BF16)
        diff_im = cols2(even[:, 128:] * weight_even, odd[:, 128:] * weight_odd).astype(BF16)
        back_even = dot(table[4], rows2(diff_re[:128], diff_im[:128]))
        back_odd = dot(table[5], rows2(diff_re[128:], diff_im[128:]))
        both = back_even + back_odd
        less = back_even - back_odd
        back_re = rows2(both[:128], less[:128]).astype(BF16)
        back_im = rows2(both[128:], less[128:]).astype(BF16)
        chi_even = dot(cols2(back_re[:, :128], back_im[:, :128]), table[6])
        chi_odd = dot(cols2(back_re[:, 128:], back_im[:, 128:]), table[7])
        both = chi_even + chi_odd
        less = chi_even - chi_odd
        chi_re = cols2(both[:, :128], less[:, :128])
        chi_im = cols2(both[:, 128:], less[:, 128:])
        gained[0] += probe_re * chi_re + probe_im * chi_im
        gained[1] += probe_re * chi_im - probe_im * chi_re
    for c in range(2):
        grad[c] = gained[c]


def detector_roots(frames, frame, columns, table, root):
    for h in range(2):
        columns[h] = frames[frame, :, 128 * h : 128 * h + 128]
    value = jnp.sqrt(
        rows2(*[cols2(*[columns[h, pl.ds(odd, 128, stride=2), :] for h in range(2)]) for odd in range(2)])
    )
    first = value.astype(BF16)
    rest = value - first.astype(F32)
    second = rest.astype(BF16)
    third = (rest - second.astype(F32)).astype(BF16)
    order = table[8]
    root[...] = dot(first, order) + dot(second, order) + dot(third, order)


def kernel(
    obj_hbm,
    probe_hbm,
    frames_hbm,
    table_hbm,
    off_ref,
    ids_ref,
    out_ref,
    tile_rows,
    probe,
    frames,
    table,
    mine,
    offs,
    places,
    held,
    shifted,
    stage,
    patch,
    obj,
    columns,
    roots,
    far,
    power,
    weight,
    grad,
    turned,
    terms,
    recv,
    counts,
    counts_in,
    totals,
    light4,
    lit,
    hits,
    split,
    result,
    summed,
    halves,
    half_in,
    rows_in,
    half_out,
    half_back,
    load_sems,
    off_sems,
    row_sems,
    patch_sems,
    term_sems,
    count_sems,
    half_sems,
    last_sems,
    out_sems,
):
    place = Place()
    core, tile = place.core, place.tile
    my_class = place.class_at(0, 0, 0)
    opposite = place.device((2, 2, 2))
    twin = place.twin()
    loads = [
        pltpu.make_async_copy(source, target, load_sems.at[i])
        for i, (source, target) in enumerate(
            ((obj_hbm, tile_rows), (probe_hbm, probe), (table_hbm, table), (frames_hbm, frames))
        )
    ]
    for load in loads:
        load.start()

    lane = lanes_of((1, 128))
    for p in range(2):
        mine[0, p : p + 1] = (off_ref[p, 1] // 32) * 128 + off_ref[p, 0] // 32 + lane % 8
    enter(place)
    for k in FAR_FIRST:
        send(mine.at[0], offs.at[k], off_sems, place.device(STEPS[k]))
    loads[0].wait()
    for grp, other, cls in row_partners(place):
        send(tile_rows.at[:, cls], held.at[pl.ds(2 * tile, 2)], row_sems, (grp, other))
    offs[0] = mine[0]
    held[pl.ds(2 * tile, 2)] = tile_rows[:, my_class]

    for load in loads[1:]:
        load.wait()

    def add_light(m, total):
        return total + probe[m, 0] * probe[m, 0] + probe[m, 1] * probe[m, 1]

    light = cols2(lax.fori_loop(0, 8, add_light, jnp.zeros((256, 256), F32)), jnp.zeros((256, 128), F32))
    for s in range(4):
        light4[s] = light if s == 0 else pltpu.roll(light, 32 * s, 1)
    for p in range(2):
        detector_roots(frames, ids_ref[p], columns, table, roots.at[p])
    for a2 in range(2):
        for j in range(4):
            lit[j, a2] = jnp.zeros((32, 128), F32)

    arrived(offs.at[pl.ds(1, 31)], off_sems, 1)
    copy = pltpu.make_async_copy(offs, places, load_sems.at[4])
    copy.start()
    arrived(held.at[pl.ds(0, 62)], row_sems, 1)
    copy.wait()
    for c in range(2):
        line = jnp.concatenate(
            [held.reshape(512, 128)[pl.ds(2 * q + c, 64, stride=8), :] for q in range(4)], axis=1
        )
        for s in range(4):
            moved_line = line if s == 0 else pltpu.roll(line, 512 - 32 * s, 1)
            for q in range(4):
                shifted[s, c, q] = moved_line[:, 128 * q : 128 * q + 128]

    def give_rows(p):
        for k in FAR_FIRST + [0]:
            value = places[k, p, 0]
            a = value & 127
            b = value >> 7
            q = b >> 2
            s = b & 3
            for c in range(2):
                for h in range(2):
                    rows = shifted[s, c, q + h, pl.ds(a, 8), :]
                    if k == 0:
                        patch[p, c, h, pl.ds(8 * my_class, 8), :] = rows
                    else:
                        stage[p, k, c, h] = rows
            if k:
                send(
                    stage.at[p, k],
                    patch.at[p, :, :, pl.ds(8 * my_class, 8), :],
                    patch_sems.at[p],
                    place.device(STEPS[k], -1),
                )

    give_rows(0)

    grid_row = lax.broadcasted_iota(jnp.int32, (64, 128), 0)
    grid_col = lax.broadcasted_iota(jnp.int32, (64, 128), 1)
    found = jnp.zeros((64, 128), F32)
    for k in range(32):
        for p in range(2):
            value = places[k, p, 0]
            found += jnp.where((grid_row == (value & 127)) & (grid_col == (value >> 7)), 1.0, 0.0)
    counts[0] = found
    send(counts.at[0], counts_in.at[0], count_sems.at[0], opposite)
    for p in range(2):
        parts = []
        for u in range(2):
            part = jnp.zeros((1, 128), jnp.int32)
            for kk in range(16):
                part = jnp.where(lane // 8 == kk, offs[16 * u + kk, p : p + 1], part)
            parts.append(part)
        key = cols2(*parts)
        goal = (key >> 9) * 64 + (key & 127)
        hits[p] = jnp.where(lax.broadcasted_iota(jnp.int32, (192, 256), 0) == goal, 1.0, 0.0).astype(BF16)

    give_rows(1)
    arrived(counts.at[0], count_sems.at[0], 1)
    counts[1] = counts[0] + counts_in[0]
    send(counts.at[1], counts_in.at[1], count_sems.at[1], twin)

    def frame(p, carry):
        arrived(patch.at[p, :, :, pl.ds(0, 248), :], patch_sems.at[p], 1)
        for c in range(2):
            for a in range(8):
                for h in range(2):
                    obj[c, 32 * a : 32 * a + 32, 128 * h : 128 * h + 128] = patch[
                        p, c, h, pl.ds(a, 32, stride=8), :
                    ]
        forward(obj, probe, table, far, power)
        weight[...] = roots[p] / jnp.sqrt(jnp.maximum(power[...], 0.1)) - 1.0
        backward(probe, table, far, weight, grad)
        turn = off_ref[p, 1] & 127
        for c in range(2):
            rolled = pltpu.roll(grad[c], turn, 1)
            for h in range(2):
                turned[c, h] = rolled[:, 128 * h : 128 * h + 128]
        for i in range(32):
            for c in range(2):
                for h in range(2):
                    terms[p, i, c, h] = turned[c, h, pl.ds(i, 8, stride=32), :]
        for k in FAR_FIRST:
            send(terms.at[p, place.class_at(*STEPS[k])], recv.at[p, k], term_sems.at[p], place.device(STEPS[k]))
        recv[p, 0] = terms[p, my_class]
        return carry

    lax.fori_loop(0, 2, frame, 0)

    arrived(counts.at[1], count_sems.at[1], 1)
    totals[0:8] = jnp.zeros((8, 128), F32)
    totals[8:72] = counts[1] + counts_in[1]
    near = totals[pl.ds(2 * tile + 1, 9), :]
    for a2 in range(2):
        for da in range(8):
            for b in range(9):
                q, s = b // 4, b % 4
                many = jnp.broadcast_to(near[a2 + 7 - da : a2 + 8 - da, b : b + 1], (32, 128))
                for j in range(q, min(q + 3, 4)):
                    if j - q == 2 and s == 0:
                        continue
                    lit[j, a2] += many * light4[s, 32 * da : 32 * da + 32, 128 * (j - q) : 128 * (j - q) + 128]

    for p in range(2):
        arrived(recv.at[p, pl.ds(1, 31)], term_sems.at[p], 1)
        for k in range(0, 32, 2):
            masks = [lane >= 32 * ((places[k + d, p, 0] >> 7) & 3) for d in range(2)]
            for c in range(2):
                lefts = [recv[p, k + d, c, 0] for d in range(2)]
                right = rows2(recv[p, k, c, 1], recv[p, k + 1, c, 1])
                own = rows2(*[jnp.where(masks[d], lefts[d], 0.0) for d in range(2)])
                wrapped = rows2(*[jnp.where(masks[d], 0.0, lefts[d]) for d in range(2)])
                for kind, piece in enumerate((own, right, wrapped)):
                    high = piece.astype(BF16)
                    at = kind * 256 + c * 128
                    split[0, 8 * k : 8 * k + 16, at : at + 128] = high
                    split[1, 8 * k : 8 * k + 16, at : at + 128] = (piece - high.astype(F32)).astype(BF16)
        part = dot(hits[p], split[0]) + dot(hits[p], split[1])
        if p == 0:
            result[...] = part
        else:
            result[...] += part
    for j in range(4):
        for c in range(2):
            total = jnp.zeros((64, 128), F32)
            for kind in range(3):
                if 0 <= j - kind <= 2:
                    at = kind * 256 + c * 128
                    total += result[64 * (j - kind) : 64 * (j - kind) + 64, at : at + 128]
            summed[j, c] = total
    for j in range(4):
        for c in range(2):
            for a2 in range(2):
                halves[j // 2, pl.ds(a2 * 4 + (j % 2) * 2 + c, 32, stride=8), :] = summed[
                    j, c, pl.ds(a2, 32, stride=2), :
                ]

    send(halves.at[1 - core], half_in, half_sems, twin)
    arrived(half_in, half_sems, 1)
    arrived(half_in, half_sems, 0)
    halves[core] += half_in[...]
    own_half = halves.at[core]
    slot = 8 * (place.half(0) * 16 + my_class)
    for step in ALL_STEPS:
        send(
            own_half.at[pl.ds(8 * place.tile_at(*step), 8)],
            rows_in.at[pl.ds(slot, 8)],
            last_sems,
            place.device(step),
        )
    rows_in[pl.ds(slot, 8)] = halves[core, pl.ds(8 * tile, 8)]
    arrived(rows_in.at[pl.ds(0, 504)], last_sems, 1)
    flat = out_ref.reshape(512, 128)
    source = tile_rows.reshape(512, 128)
    for a2 in range(2):
        for jj in range(2):
            under = lit[2 * core + jj, a2] + 0.1
            for c in range(2):
                e = a2 * 4 + jj * 2 + c
                total = rows_in[pl.ds(e, 32, stride=8), :] + rows_in[pl.ds(256 + e, 32, stride=8), :]
                at = pl.ds(a2 * 256 + core * 4 + jj * 2 + c, 32, stride=8)
                done = source[at, :] + total / under
                flat[at, :] = done
                half_out[pl.ds(e, 32, stride=8), :] = done
    send(half_out, half_back, out_sems, twin)
    arrived(half_back, out_sems, 1)
    for a2 in range(2):
        for e in range(4):
            flat[pl.ds(a2 * 256 + (1 - core) * 4 + e, 32, stride=8), :] = half_back[
                pl.ds(a2 * 4 + e, 32, stride=8), :
            ]

    arrived(offs.at[pl.ds(1, 31)], off_sems, 0)
    arrived(held.at[pl.ds(0, 62)], row_sems, 0)
    for p in range(2):
        arrived(stage.at[p, pl.ds(1, 31)], patch_sems.at[p], 0)
        arrived(recv.at[p, pl.ds(1, 31)], term_sems.at[p], 0)
        arrived(counts.at[p], count_sems.at[p], 0)
    arrived(rows_in.at[pl.ds(0, 504)], last_sems, 0)
    arrived(half_out, out_sems, 0)


def on_device(object_tile, probe, offsets, frame_ids, frames):
    obj = object_tile.reshape(64, 2, 4, 128).transpose(0, 2, 1, 3).reshape(2, 32, 8, 128)
    smem = pl.BlockSpec(memory_space=pltpu.SMEM)
    hbm = pl.BlockSpec(memory_space=pltpu.HBM)
    pair = pltpu.SemaphoreType.DMA((2,))
    updated = pl.pallas_call(
        kernel,
        out_shape=pltpu.VMEM((64, 8, 128), F32),
        in_specs=[hbm, hbm, hbm, hbm, smem, smem],
        out_specs=pl.BlockSpec(memory_space=pltpu.VMEM),
        scratch_shapes=[
            pltpu.VMEM((2, 32, 8, 128), F32),
            pltpu.VMEM((8, 2, 256, 256), F32),
            pltpu.VMEM((2, 256, 256), F32),
            pltpu.VMEM((9, 256, 256), BF16),
            pltpu.VMEM((1, 2, 128), jnp.int32),
            pltpu.VMEM((32, 2, 128), jnp.int32),
            pltpu.SMEM((32, 2, 128), jnp.int32),
            pltpu.VMEM((64, 8, 128), F32),
            pltpu.VMEM((4, 2, 4, 64, 128), F32),
            pltpu.VMEM((2, 32, 2, 2, 8, 128), F32),
            pltpu.VMEM((2, 2, 2, 256, 128), F32),
            pltpu.VMEM((2, 256, 256), F32),
            pltpu.VMEM((2, 256, 128), F32),
            pltpu.VMEM((2, 256, 256), F32),
            pltpu.VMEM((8, 2, 256, 256), F32),
            pltpu.VMEM((256, 256), F32),
            pltpu.VMEM((256, 256), F32),
            pltpu.VMEM((2, 256, 256), F32),
            pltpu.VMEM((2, 2, 256, 128), F32),
            pltpu.VMEM((2, 32, 2, 2, 8, 128), F32),
            pltpu.VMEM((2, 32, 2, 2, 8, 128), F32),
            pltpu.VMEM((2, 64, 128), F32),
            pltpu.VMEM((2, 64, 128), F32),
            pltpu.VMEM((72, 128), F32),
            pltpu.VMEM((4, 256, 384), F32),
            pltpu.VMEM((4, 2, 32, 128), F32),
            pltpu.VMEM((2, 192, 256), BF16),
            pltpu.VMEM((2, 256, 768), BF16),
            pltpu.VMEM((192, 768), F32),
            pltpu.VMEM((4, 2, 64, 128), F32),
            pltpu.VMEM((2, 256, 128), F32),
            pltpu.VMEM((256, 128), F32),
            pltpu.VMEM((512, 128), F32),
            pltpu.VMEM((256, 128), F32),
            pltpu.VMEM((256, 128), F32),
            pltpu.SemaphoreType.DMA((5,)),
            pair,
            pair,
            pltpu.SemaphoreType.DMA((2, 2)),
            pltpu.SemaphoreType.DMA((2, 2)),
            pltpu.SemaphoreType.DMA((2, 2)),
            pair,
            pair,
            pair,
        ],
        compiler_params=pltpu.CompilerParams(
            collective_id=1, has_side_effects=True, vmem_limit_bytes=VMEM_LIMIT
        ),
        name="iteration",
    )(obj, probe, frames, jnp.asarray(tables()), offsets, frame_ids)
    return updated.reshape(64, 4, 2, 128).transpose(0, 2, 1, 3).reshape(64, 2, 512)


def solution(mesh):
    in_specs = (
        P("tile", None, None),
        P(),
        P(("grp", "tile"), None),
        P(("grp", "tile")),
        P(("grp", "tile"), None, None),
    )
    out_specs = P("tile", None, None)
    return jax.shard_map(
        on_device, mesh=mesh, in_specs=in_specs, out_specs=out_specs, check_vma=False
    )
```

```python
import functools

import jax
import jax.numpy as jnp
import ml_dtypes
import numpy as np
from jax import lax
from jax.experimental import pallas as pl
from jax.experimental.pallas import tpu as pltpu
from jax.sharding import PartitionSpec as P

MESH = pl.DeviceIdType.MESH
BF16 = jnp.bfloat16
F32 = jnp.float32
VMEM_LIMIT = 60 << 20


def _weight(step):
    return sum(min(part, 4 - part) for part in step)


STEPS = sorted(
    [
        step
        for step in ((a, b, c) for a in range(4) for b in range(4) for c in range(4))
        if _weight(step) < 3
    ],
    key=_weight,
) + [
    (2, 1, 0),
    (2, 3, 0),
    (0, 2, 1),
    (0, 2, 3),
    (1, 0, 2),
    (3, 0, 2),
    (1, 1, 1),
    (1, 3, 3),
    (3, 1, 3),
    (3, 3, 1),
]
ALL_STEPS = sorted(
    ((a, b, c) for a in range(4) for b in range(4) for c in range(4)), key=_weight, reverse=True
)[:-1]
FAR_FIRST = sorted(range(1, 32), key=lambda k: _weight(STEPS[k]), reverse=True)


class Place:
    def __init__(self):
        grp = lax.axis_index("grp")
        tile = lax.axis_index("tile")
        self.grp, self.tile = grp, tile
        self.core = lax.rem(grp, 2)
        self.x = lax.div(grp, 2) * 2 + lax.rem(tile, 2)
        self.y = lax.rem(lax.div(tile, 2), 4)
        self.z = lax.div(tile, 8)
        self.known = {}

    def once(self, name, make):
        if name not in self.known:
            self.known[name] = make()
        return self.known[name]

    def at(self, axis, by):
        by %= 4
        return self.once((axis, by), lambda: lax.rem(getattr(self, axis) + by, 4) if by else getattr(self, axis))

    def half(self, dx):
        return self.once(("half", dx % 4), lambda: lax.div(self.at("x", dx), 2) * 2)

    def tile_at(self, dx, dy, dz):
        plane = self.once(("plane", dx % 4, dy % 4), lambda: self.at("y", dy) * 2 + lax.rem(self.at("x", dx), 2))
        return self.once(("z8", dz % 4), lambda: self.at("z", dz) * 8) + plane

    def device(self, step, sign=1, other=0):
        dx, dy, dz = (sign * by for by in step)
        grp = self.once(("grp", dx % 4, other), lambda: self.half(dx) + (1 - self.core if other else self.core))
        return grp, self.tile_at(dx, dy, dz)

    def twin(self):
        return self.half(0) + 1 - self.core, self.tile

    def class_at(self, dx, dy, dz):
        near = self.once(
            ("near", dx % 4, dy % 4),
            lambda: lax.rem(self.at("x", dx), 2) * 16 + lax.rem(self.at("y", dy) + self.half(dx), 4) * 4,
        )
        return near + self.once(("deep", dx % 4, dz % 4), lambda: lax.rem(self.at("z", dz) + self.half(dx), 4))


def enter(place):
    barrier = pltpu.get_barrier_semaphore()
    for to in row_partners(place):
        pl.semaphore_signal(barrier, inc=1, device_id=to[:2], device_id_type=MESH)
    odd = lax.rem(place.tile, 2)
    beside = [step for step in STEPS if step[0] == 2]
    for step in beside:
        pl.semaphore_signal(barrier, inc=1, device_id=place.device(step, -1), device_id_type=MESH)
    ups = [step for step in STEPS if step[0] == 1]
    downs = [step for step in STEPS if step[0] == 3]
    assert len(ups) == len(downs)
    for up, down in zip(ups, downs):
        grp_a, tile_a = place.device(up, -1)
        grp_b, tile_b = place.device(down, -1)
        to = (grp_a + odd * (grp_b - grp_a), tile_a + odd * (tile_b - tile_a))
        pl.semaphore_signal(barrier, inc=1, device_id=to, device_id_type=MESH)
    pl.semaphore_signal(barrier, inc=1, device_id=place.twin(), device_id_type=MESH)
    pl.semaphore_wait(barrier, 31 + len(beside) + len(ups) + 1)


def row_partners(place):
    across = lax.rem(place.tile + 1, 2) - lax.rem(place.tile, 2)
    partners = []
    for dx, dy, dz in sorted(
        ((a, b, c) for a in range(2) for b in range(4) for c in range(4)), key=_weight, reverse=True
    )[:-1]:
        plane = place.tile_at(0, dy, dz)
        cls = place.class_at(0, dy, dz)
        partners.append((place.grp, plane + dx * across, cls + 16 * dx * across))
    return partners


def send(source, target, sems, to):
    copy = pltpu.make_async_remote_copy(
        src_ref=source,
        dst_ref=target,
        send_sem=sems.at[0],
        recv_sem=sems.at[1],
        device_id=to,
        device_id_type=MESH,
    )
    copy.start()


def arrived(ref, sems, which):
    pltpu.make_async_copy(ref, ref, sems.at[which]).wait()


def lanes_of(shape):
    return lax.broadcasted_iota(jnp.int32, shape, len(shape) - 1)


def tables():
    line = np.arange(256)
    angle = 2.0 * np.pi / 256 * (line[:, None] * line[None, :] % 256)
    re = (np.cos(angle) / 16).astype(ml_dtypes.bfloat16)
    im = (-np.sin(angle) / 16).astype(ml_dtypes.bfloat16)

    def real_form(table_re, table_im, left):
        if left:
            return np.block([[table_re, -table_im], [table_im, table_re]])
        return np.block([[table_re, table_im], [-table_im, table_re]])

    made = []
    for odd in range(2):
        made.append(real_form(re[odd::2, :128], im[odd::2, :128], True))
    for odd in range(2):
        made.append(real_form(re[:128, odd::2], im[:128, odd::2], False))
    for odd in range(2):
        made.append(real_form(re[:128, odd::2], -im[:128, odd::2], True))
    for odd in range(2):
        made.append(real_form(re[odd::2, :128], -im[odd::2, :128], False))
    order = np.zeros((256, 256), ml_dtypes.bfloat16)
    order[np.concatenate([line[0::2], line[1::2]]), line] = 1
    made.append(order)
    return np.stack([table.astype(ml_dtypes.bfloat16) for table in made])


def dot(a, b):
    return jnp.dot(a, b, preferred_element_type=F32)


def rows2(a, b):
    return jnp.concatenate([a, b], axis=0)


def cols2(a, b):
    return jnp.concatenate([a, b], axis=1)


def forward(obj, probe, table, far, power, between):
    gained = [0.0, 0.0]
    for mode in range(8):
        probe_re = probe[mode, 0]
        probe_im = probe[mode, 1]
        obj_re = obj[0]
        obj_im = obj[1]
        exit_re = probe_re * obj_re - probe_im * obj_im
        exit_im = probe_re * obj_im + probe_im * obj_re
        both = rows2(exit_re[:128] + exit_re[128:], exit_im[:128] + exit_im[128:]).astype(BF16)
        less = rows2(exit_re[:128] - exit_re[128:], exit_im[:128] - exit_im[128:]).astype(BF16)
        sums = []
        lesses = []
        for half in (dot(table[0], both), dot(table[1], less)):
            re, im = half[:128], half[128:]
            sums.append(cols2(re[:, :128] + re[:, 128:], im[:, :128] + im[:, 128:]))
            lesses.append(cols2(re[:, :128] - re[:, 128:], im[:, :128] - im[:, 128:]))
        far_even = dot(rows2(*sums).astype(BF16), table[2])
        far_odd = dot(rows2(*lesses).astype(BF16), table[3])
        far[mode, 0] = far_even
        far[mode, 1] = far_odd
        for odd, wave in enumerate((far_even, far_odd)):
            re, im = wave[:, :128], wave[:, 128:]
            gained[odd] += re * re + im * im
        between(mode)
    for odd in range(2):
        power[:, odd * 128 : odd * 128 + 128] = gained[odd]


def backward(probe, table, far, weight, grad):
    weight_even = weight[:, :128]
    weight_odd = weight[:, 128:]
    gained = [0.0, 0.0]
    for mode in range(8):
        probe_re = probe[mode, 0]
        probe_im = probe[mode, 1]
        even = far[mode, 0]
        odd = far[mode, 1]
        diff_re = cols2(even[:, :128] * weight_even, odd[:, :128] * weight_odd).astype(BF16)
        diff_im = cols2(even[:, 128:] * weight_even, odd[:, 128:] * weight_odd).astype(BF16)
        back_even = dot(table[4], rows2(diff_re[:128], diff_im[:128]))
        back_odd = dot(table[5], rows2(diff_re[128:], diff_im[128:]))
        both = back_even + back_odd
        less = back_even - back_odd
        back_re = rows2(both[:128], less[:128]).astype(BF16)
        back_im = rows2(both[128:], less[128:]).astype(BF16)
        chi_even = dot(cols2(back_re[:, :128], back_im[:, :128]), table[6])
        chi_odd = dot(cols2(back_re[:, 128:], back_im[:, 128:]), table[7])
        both = chi_even + chi_odd
        less = chi_even - chi_odd
        chi_re = cols2(both[:, :128], less[:, :128])
        chi_im = cols2(both[:, 128:], less[:, 128:])
        gained[0] += probe_re * chi_re + probe_im * chi_im
        gained[1] += probe_re * chi_im - probe_im * chi_re
    for c in range(2):
        grad[c] = gained[c]


def detector_roots(frames, frame, columns, table, root):
    for h in range(2):
        columns[h] = frames[frame, :, 128 * h : 128 * h + 128]
    value = jnp.sqrt(
        rows2(*[cols2(*[columns[h, pl.ds(odd, 128, stride=2), :] for h in range(2)]) for odd in range(2)])
    )
    first = value.astype(BF16)
    rest = value - first.astype(F32)
    second = rest.astype(BF16)
    third = (rest - second.astype(F32)).astype(BF16)
    order = table[8]
    root[...] = dot(first, order) + dot(second, order) + dot(third, order)


def kernel(
    obj_hbm,
    probe_hbm,
    frames_hbm,
    table_hbm,
    off_hbm,
    ids_hbm,
    out_ref,
    off_ref,
    ids_ref,
    tile_rows,
    probe,
    frames,
    table,
    own,
    theirs,
    mine,
    offs,
    listed,
    places,
    held,
    shifted,
    stage,
    patch_a,
    patch_b,
    obj,
    columns,
    roots,
    far,
    power,
    weight,
    grad,
    turned,
    terms,
    recv,
    counts,
    counts_in,
    totals,
    light4,
    lit,
    under,
    hits,
    split,
    result,
    ready,
    rows_in,
    load_sems,
    own_sems,
    off_sems,
    row_sems,
    patch_sems,
    term_sems,
    count_sems,
    last_sems,
    out_sems,
):
    place = Place()
    core, tile = place.core, place.tile
    my_class = place.class_at(0, 0, 0)
    my_slot = core * 32 + my_class
    cores = (core, 1 - core)
    everyone = [(k, other) for k in FAR_FIRST + [0] for other in range(2)]
    twin = place.twin()
    patches = (patch_a, patch_b)
    loads = [
        pltpu.make_async_copy(source, target, load_sems.at[i])
        for i, (source, target) in enumerate(
            (
                (obj_hbm, tile_rows),
                (off_hbm, off_ref),
                (ids_hbm, ids_ref),
                (probe_hbm, probe),
                (table_hbm, table),
                (frames_hbm, frames),
            )
        )
    ]
    for load in loads:
        load.start()

    loads[1].wait()
    lane = lanes_of((1, 128))
    nodes = [(off_ref[p, 1] // 32) * 128 + off_ref[p, 0] // 32 for p in range(2)]
    own[...] = jnp.where(lane // 2 % 2 == core, jnp.where(lane % 2 == 0, nodes[0], nodes[1]), 0)
    enter(place)
    send(own, theirs, own_sems, twin)
    loads[0].wait()
    for grp, other, cls in row_partners(place):
        send(tile_rows.at[core, cls], held.at[tile], row_sems, (grp, other))
    arrived(theirs, own_sems, 1)
    mine[0] = own[...] + theirs[...]
    for k in FAR_FIRST:
        send(mine.at[0], offs.at[k], off_sems, place.device(STEPS[k]))
    offs[0] = mine[0]
    held[tile] = tile_rows[core, my_class]

    for load in loads[2:]:
        load.wait()

    def add_light(m, total):
        return total + probe[m, 0] * probe[m, 0] + probe[m, 1] * probe[m, 1]

    light = cols2(lax.fori_loop(0, 8, add_light, jnp.zeros((256, 256), F32)), jnp.zeros((256, 128), F32))
    for s in range(4):
        light4[s] = light if s == 0 else pltpu.roll(light, 32 * s, 1)
    for p in range(2):
        detector_roots(frames, ids_ref[p], columns, table, roots.at[p])
    for j in range(4):
        lit[j] = jnp.zeros((32, 128), F32)

    arrived(offs.at[pl.ds(1, 31)], off_sems, 1)
    packed = jnp.zeros((1, 128), jnp.int32)
    for k in range(32):
        packed = jnp.where(lane // 4 == k, offs[k], packed)
    listed[...] = packed
    copy = pltpu.make_async_copy(listed, places, load_sems.at[6])
    copy.start()
    arrived(held.at[pl.ds(0, 31)], row_sems, 1)
    copy.wait()
    for c in range(2):
        line = jnp.concatenate(
            [held.reshape(256, 128)[pl.ds(2 * q + c, 32, stride=8), :] for q in range(4)], axis=1
        )
        for s in range(4):
            moved_line = line if s == 0 else pltpu.roll(line, 512 - 32 * s, 1)
            for q in range(4):
                shifted[s, c, q] = moved_line[:, 128 * q : 128 * q + 128]

    def give_rows(p):
        for k, other in everyone:
            value = places[0, 4 * k + 2 * cores[other] + p]
            a = ((value & 127) + 1 - core) >> 1
            b = value >> 7
            q = b >> 2
            s = b & 3
            for c in range(2):
                for h in range(2):
                    rows = shifted[s, c, q + h, pl.ds(a, 4), :]
                    if k or other:
                        stage[p, 32 * other + k, c, 4 * h : 4 * h + 4] = rows
                    else:
                        patches[p][my_slot, c, 4 * h : 4 * h + 4] = rows
            if k or other:
                send(
                    stage.at[p, 32 * other + k],
                    patches[p].at[my_slot],
                    patch_sems.at[p],
                    place.device(STEPS[k], -1, other),
                )

    give_rows(0)

    for p in range(2):
        parts = []
        for u in range(4):
            part = jnp.zeros((1, 128), jnp.int32)
            for kk in range(16):
                part = jnp.where(lane // 8 == kk, places[0, 4 * (16 * (u % 2) + kk) + 2 * (u // 2) + p], part)
            parts.append(part)
        key = jnp.concatenate(parts, axis=1)
        step = lanes_of((1, 512))
        goal = (key >> 9) * 32 + (((key & 127) + 1 - core) >> 1) + step % 4
        rows = lax.broadcasted_iota(jnp.int32, (128, 512), 0)
        hits[p, 0] = jnp.where(rows == goal + (step // 4) % 2 * 32, 1.0, 0.0).astype(BF16)
        hits[p, 1] = jnp.where(rows == goal + 64, 1.0, 0.0).astype(BF16)
    give_rows(1)
    grid_row = lax.broadcasted_iota(jnp.int32, (64, 128), 0)
    grid_col = lax.broadcasted_iota(jnp.int32, (64, 128), 1)
    found = jnp.zeros((64, 128), F32)
    for k in range(32):
        for row in range(4):
            value = places[0, 4 * k + row]
            found += jnp.where((grid_row == (value & 127)) & (grid_col == (value >> 7)), 1.0, 0.0)
    counts[...] = found
    send(counts, counts_in, count_sems, place.device((2, 2, 2)))

    def frame(p, between):
        arrived(patches[p].at[pl.ds(0, 63)], patch_sems.at[p], 1)
        odd = (off_ref[p, 0] // 32) & 1
        flat = patches[p].reshape(1024, 128)
        for c in range(2):
            for a in range(8):
                for h in range(2):
                    start = ((odd + a) & 1) * 512 + c * 8 + h * 4 + a // 2
                    obj[c, 32 * a : 32 * a + 32, 128 * h : 128 * h + 128] = flat[pl.ds(start, 32, stride=16), :]
        forward(obj, probe, table, far, power, between)
        weight[...] = roots[p] / jnp.sqrt(jnp.maximum(power[...], 0.1)) - 1.0
        backward(probe, table, far, weight, grad)
        turn = off_ref[p, 1] & 127
        for c in range(2):
            rolled = pltpu.roll(grad[c], turn, 1)
            for h in range(2):
                turned[c, h] = rolled[:, 128 * h : 128 * h + 128]
        for even in range(2):
            start = ((even + odd) & 1) * 32
            for i in range(32):
                for c in range(2):
                    for h in range(2):
                        terms[p, even, i, c, 4 * h : 4 * h + 4] = turned[c, h, pl.ds(start + i, 4, stride=64), :]
        recv[p, core * 32] = terms[p, core, my_class]

    def give_terms(p, some):
        for k, other in some:
            if k or other:
                send(
                    terms.at[p, cores[other], place.class_at(*STEPS[k])],
                    recv.at[p, core * 32 + k],
                    term_sems.at[p],
                    place.device(STEPS[k], 1, other),
                )

    frame(0, lambda mode: None)
    frame(1, lambda mode: give_terms(0, everyone[8 * mode : 8 * mode + 8]))
    give_terms(1, everyone)

    arrived(counts, count_sems, 1)
    totals[0:8] = jnp.zeros((8, 128), F32)
    totals[8:72] = counts[...] + counts_in[...]
    near = totals[pl.ds(2 * tile + core + 1, 8), :]
    for da in range(8):
        for b in range(9):
            q, s = b // 4, b % 4
            many = jnp.broadcast_to(near[7 - da : 8 - da, b : b + 1], (32, 128))
            for j in range(q, min(q + 3, 4)):
                if j - q == 2 and s == 0:
                    continue
                lit[j] += many * light4[s, 32 * da : 32 * da + 32, 128 * (j - q) : 128 * (j - q) + 128]
    for j in range(4):
        for c in range(2):
            under.reshape(256, 128)[pl.ds(2 * j + c, 32, stride=8), :] = lit[j] + 0.1

    sub = lax.broadcasted_iota(jnp.int32, (8, 128), 0)
    full_lane = lanes_of((8, 128))
    for p in range(2):
        arrived(recv.at[p, pl.ds(0, 63)], term_sems.at[p], 1)
        for slot in range(0, 64, 2):
            masks = []
            for d in range(2):
                turn = (places[0, 4 * ((slot + d) % 32) + 2 * (slot // 32) + p] >> 7) & 3
                masks.append((sub >= 4) | (full_lane >= 32 * turn))
            for c in range(2):
                pieces = [recv[p, slot + d, c] for d in range(2)]
                kept = rows2(*[jnp.where(masks[d], pieces[d], 0.0) for d in range(2)])
                wrapped = rows2(*[jnp.where(masks[d], 0.0, pieces[d]) for d in range(2)])
                for kind, piece in enumerate((kept, wrapped)):
                    high = piece.astype(BF16)
                    split[kind, 0, 8 * slot : 8 * slot + 16, 128 * c : 128 * c + 128] = high
                    split[kind, 1, 8 * slot : 8 * slot + 16, 128 * c : 128 * c + 128] = (
                        piece - high.astype(F32)
                    ).astype(BF16)
        part = 0.0
        for kind in range(2):
            part += dot(hits[p, kind], split[kind, 0]) + dot(hits[p, kind], split[kind, 1])
        if p == 0:
            result[...] = part
        else:
            result[...] += part
    for j in range(4):
        for c in range(2):
            ready.reshape(256, 128)[pl.ds(2 * j + c, 32, stride=8), :] = result[
                32 * j : 32 * j + 32, 128 * c : 128 * c + 128
            ]

    slot = place.half(0) * 16 + my_class
    for step in ALL_STEPS:
        send(ready.at[place.tile_at(*step)], rows_in.at[slot], last_sems, place.device(step))
    rows_in[slot] = ready[tile]
    arrived(rows_in.at[pl.ds(0, 63)], last_sems, 1)
    here = pl.ds(32 * core, 32)
    out_ref[here] = tile_rows[core] + (rows_in[0:32] + rows_in[32:64]) / under[...]
    send(out_ref.at[here], out_ref.at[here], out_sems, twin)
    arrived(out_ref.at[pl.ds(0, 32)], out_sems, 1)

    arrived(own, own_sems, 0)
    arrived(offs.at[pl.ds(1, 31)], off_sems, 0)
    arrived(held.at[pl.ds(0, 31)], row_sems, 0)
    for p in range(2):
        arrived(patches[p].at[pl.ds(0, 63)], patch_sems.at[p], 0)
        arrived(recv.at[p, pl.ds(0, 63)], term_sems.at[p], 0)
    arrived(counts, count_sems, 0)
    arrived(rows_in.at[pl.ds(0, 63)], last_sems, 0)
    arrived(out_ref.at[pl.ds(0, 32)], out_sems, 0)


def on_device(object_tile, probe, offsets, frame_ids, frames):
    obj = object_tile.reshape(64, 2, 4, 128).transpose(0, 2, 1, 3).reshape(2, 32, 8, 128)
    hbm = pl.BlockSpec(memory_space=pltpu.HBM)
    pair = pltpu.SemaphoreType.DMA((2,))
    pairs = pltpu.SemaphoreType.DMA((2, 2))
    updated = pl.pallas_call(
        kernel,
        out_shape=pltpu.VMEM((64, 8, 128), F32),
        in_specs=[hbm] * 6,
        out_specs=pl.BlockSpec(memory_space=pltpu.VMEM),
        scratch_shapes=[
            pltpu.SMEM((2, 2), jnp.int32),
            pltpu.SMEM((2,), jnp.int32),
            pltpu.VMEM((2, 32, 8, 128), F32),
            pltpu.VMEM((8, 2, 256, 256), F32),
            pltpu.VMEM((2, 256, 256), F32),
            pltpu.VMEM((9, 256, 256), BF16),
            pltpu.VMEM((1, 128), jnp.int32),
            pltpu.VMEM((1, 128), jnp.int32),
            pltpu.VMEM((1, 1, 128), jnp.int32),
            pltpu.VMEM((32, 1, 128), jnp.int32),
            pltpu.VMEM((1, 128), jnp.int32),
            pltpu.SMEM((1, 128), jnp.int32),
            pltpu.VMEM((32, 8, 128), F32),
            pltpu.VMEM((4, 2, 4, 32, 128), F32),
            pltpu.VMEM((2, 64, 2, 8, 128), F32),
            pltpu.VMEM((64, 2, 8, 128), F32),
            pltpu.VMEM((64, 2, 8, 128), F32),
            pltpu.VMEM((2, 256, 256), F32),
            pltpu.VMEM((2, 256, 128), F32),
            pltpu.VMEM((2, 256, 256), F32),
            pltpu.VMEM((8, 2, 256, 256), F32),
            pltpu.VMEM((256, 256), F32),
            pltpu.VMEM((256, 256), F32),
            pltpu.VMEM((2, 256, 256), F32),
            pltpu.VMEM((2, 2, 256, 128), F32),
            pltpu.VMEM((2, 2, 32, 2, 8, 128), F32),
            pltpu.VMEM((2, 64, 2, 8, 128), F32),
            pltpu.VMEM((64, 128), F32),
            pltpu.VMEM((64, 128), F32),
            pltpu.VMEM((72, 128), F32),
            pltpu.VMEM((4, 256, 384), F32),
            pltpu.VMEM((4, 32, 128), F32),
            pltpu.VMEM((32, 8, 128), F32),
            pltpu.VMEM((2, 2, 128, 512), BF16),
            pltpu.VMEM((2, 2, 512, 256), BF16),
            pltpu.VMEM((128, 256), F32),
            pltpu.VMEM((32, 8, 128), F32),
            pltpu.VMEM((64, 8, 128), F32),
            pltpu.SemaphoreType.DMA((7,)),
            pair,
            pair,
            pair,
            pairs,
            pairs,
            pair,
            pair,
            pair,
        ],
        compiler_params=pltpu.CompilerParams(
            collective_id=1, has_side_effects=True, vmem_limit_bytes=VMEM_LIMIT
        ),
        name="iteration",
    )(obj, probe, frames, jnp.asarray(tables()), offsets, frame_ids)
    return updated.reshape(64, 4, 2, 128).transpose(0, 2, 1, 3).reshape(64, 2, 512)


def solution(mesh):
    in_specs = (
        P("tile", None, None),
        P(),
        P(("grp", "tile"), None),
        P(("grp", "tile")),
        P(("grp", "tile"), None, None),
    )
    out_specs = P("tile", None, None)
    return jax.shard_map(
        on_device, mesh=mesh, in_specs=in_specs, out_specs=out_specs, check_vma=False
    )
```

```python
import functools

import jax
import jax.numpy as jnp
import ml_dtypes
import numpy as np
from jax import lax
from jax.experimental import pallas as pl
from jax.experimental.pallas import tpu as pltpu
from jax.sharding import PartitionSpec as P

MESH = pl.DeviceIdType.MESH
BF16 = jnp.bfloat16
F32 = jnp.float32
VMEM_LIMIT = 60 << 20


def _weight(step):
    return sum(min(part, 4 - part) for part in step)


STEPS = sorted(
    [
        step
        for step in ((a, b, c) for a in range(4) for b in range(4) for c in range(4))
        if _weight(step) < 3
    ],
    key=_weight,
) + [
    (2, 1, 0),
    (2, 3, 0),
    (0, 2, 1),
    (0, 2, 3),
    (1, 0, 2),
    (3, 0, 2),
    (1, 1, 1),
    (1, 3, 3),
    (3, 1, 3),
    (3, 3, 1),
]
ALL_STEPS = sorted(
    ((a, b, c) for a in range(4) for b in range(4) for c in range(4)), key=_weight, reverse=True
)[:-1]
FAR_FIRST = sorted(range(1, 32), key=lambda k: _weight(STEPS[k]), reverse=True)


class Place:
    def __init__(self):
        grp = lax.axis_index("grp")
        tile = lax.axis_index("tile")
        self.grp, self.tile = grp, tile
        self.core = lax.rem(grp, 2)
        self.x = lax.div(grp, 2) * 2 + lax.rem(tile, 2)
        self.y = lax.rem(lax.div(tile, 2), 4)
        self.z = lax.div(tile, 8)
        self.known = {}

    def once(self, name, make):
        if name not in self.known:
            self.known[name] = make()
        return self.known[name]

    def at(self, axis, by):
        by %= 4
        return self.once((axis, by), lambda: lax.rem(getattr(self, axis) + by, 4) if by else getattr(self, axis))

    def half(self, dx):
        return self.once(("half", dx % 4), lambda: lax.div(self.at("x", dx), 2) * 2)

    def tile_at(self, dx, dy, dz):
        plane = self.once(("plane", dx % 4, dy % 4), lambda: self.at("y", dy) * 2 + lax.rem(self.at("x", dx), 2))
        return self.once(("z8", dz % 4), lambda: self.at("z", dz) * 8) + plane

    def device(self, step, sign=1, other=0):
        dx, dy, dz = (sign * by for by in step)
        grp = self.once(("grp", dx % 4, other), lambda: self.half(dx) + (1 - self.core if other else self.core))
        return grp, self.tile_at(dx, dy, dz)

    def twin(self):
        return self.half(0) + 1 - self.core, self.tile

    def class_at(self, dx, dy, dz):
        near = self.once(
            ("near", dx % 4, dy % 4),
            lambda: lax.rem(self.at("x", dx), 2) * 16 + lax.rem(self.at("y", dy) + self.half(dx), 4) * 4,
        )
        return near + self.once(("deep", dx % 4, dz % 4), lambda: lax.rem(self.at("z", dz) + self.half(dx), 4))


def enter(place):
    barrier = pltpu.get_barrier_semaphore()
    for to in row_partners(place):
        pl.semaphore_signal(barrier, inc=1, device_id=to[:2], device_id_type=MESH)
    odd = lax.rem(place.tile, 2)
    beside = [step for step in STEPS if step[0] == 2]
    for step in beside:
        pl.semaphore_signal(barrier, inc=1, device_id=place.device(step, -1), device_id_type=MESH)
    ups = [step for step in STEPS if step[0] == 1]
    downs = [step for step in STEPS if step[0] == 3]
    assert len(ups) == len(downs)
    for up, down in zip(ups, downs):
        grp_a, tile_a = place.device(up, -1)
        grp_b, tile_b = place.device(down, -1)
        to = (grp_a + odd * (grp_b - grp_a), tile_a + odd * (tile_b - tile_a))
        pl.semaphore_signal(barrier, inc=1, device_id=to, device_id_type=MESH)
    pl.semaphore_signal(barrier, inc=1, device_id=place.twin(), device_id_type=MESH)
    pl.semaphore_wait(barrier, 31 + len(beside) + len(ups) + 1)


def row_partners(place):
    across = lax.rem(place.tile + 1, 2) - lax.rem(place.tile, 2)
    partners = []
    for dx, dy, dz in sorted(
        ((a, b, c) for a in range(2) for b in range(4) for c in range(4)), key=_weight, reverse=True
    )[:-1]:
        plane = place.tile_at(0, dy, dz)
        cls = place.class_at(0, dy, dz)
        partners.append((place.grp, plane + dx * across, cls + 16 * dx * across))
    return partners


def send(source, target, sems, to):
    copy = pltpu.make_async_remote_copy(
        src_ref=source,
        dst_ref=target,
        send_sem=sems.at[0],
        recv_sem=sems.at[1],
        device_id=to,
        device_id_type=MESH,
    )
    copy.start()


def arrived(ref, sems, which):
    pltpu.make_async_copy(ref, ref, sems.at[which]).wait()


def lanes_of(shape):
    return lax.broadcasted_iota(jnp.int32, shape, len(shape) - 1)


def tables():
    line = np.arange(256)
    angle = 2.0 * np.pi / 256 * (line[:, None] * line[None, :] % 256)
    re = (np.cos(angle) / 16).astype(ml_dtypes.bfloat16)
    im = (-np.sin(angle) / 16).astype(ml_dtypes.bfloat16)

    def real_form(table_re, table_im, left):
        if left:
            return np.block([[table_re, -table_im], [table_im, table_re]])
        return np.block([[table_re, table_im], [-table_im, table_re]])

    made = []
    for odd in range(2):
        made.append(real_form(re[odd::2, :128], im[odd::2, :128], True))
    for odd in range(2):
        made.append(real_form(re[:128, odd::2], im[:128, odd::2], False))
    for odd in range(2):
        made.append(real_form(re[:128, odd::2], -im[:128, odd::2], True))
    for odd in range(2):
        made.append(real_form(re[odd::2, :128], -im[odd::2, :128], False))
    order = np.zeros((256, 256), ml_dtypes.bfloat16)
    order[np.concatenate([line[0::2], line[1::2]]), line] = 1
    made.append(order)
    return np.stack([table.astype(ml_dtypes.bfloat16) for table in made])


def dot(a, b):
    return jnp.dot(a, b, preferred_element_type=F32)


def rows2(a, b):
    return jnp.concatenate([a, b], axis=0)


def cols2(a, b):
    return jnp.concatenate([a, b], axis=1)


def forward(obj, probe, table, far, power, between):
    gained = [0.0, 0.0]
    for mode in range(8):
        probe_re = probe[mode, 0]
        probe_im = probe[mode, 1]
        obj_re = obj[0]
        obj_im = obj[1]
        exit_re = probe_re * obj_re - probe_im * obj_im
        exit_im = probe_re * obj_im + probe_im * obj_re
        both = rows2(exit_re[:128] + exit_re[128:], exit_im[:128] + exit_im[128:]).astype(BF16)
        less = rows2(exit_re[:128] - exit_re[128:], exit_im[:128] - exit_im[128:]).astype(BF16)
        sums = []
        lesses = []
        for half in (dot(table[0], both), dot(table[1], less)):
            re, im = half[:128], half[128:]
            sums.append(cols2(re[:, :128] + re[:, 128:], im[:, :128] + im[:, 128:]))
            lesses.append(cols2(re[:, :128] - re[:, 128:], im[:, :128] - im[:, 128:]))
        far_even = dot(rows2(*sums).astype(BF16), table[2])
        far_odd = dot(rows2(*lesses).astype(BF16), table[3])
        far[mode, 0] = far_even
        far[mode, 1] = far_odd
        for odd, wave in enumerate((far_even, far_odd)):
            re, im = wave[:, :128], wave[:, 128:]
            gained[odd] += re * re + im * im
        between(mode)
    for odd in range(2):
        power[:, odd * 128 : odd * 128 + 128] = gained[odd]


def backward(probe, table, far, weight, grad):
    weight_even = weight[:, :128]
    weight_odd = weight[:, 128:]
    gained = [0.0, 0.0]
    for mode in range(8):
        probe_re = probe[mode, 0]
        probe_im = probe[mode, 1]
        even = far[mode, 0]
        odd = far[mode, 1]
        diff_re = cols2(even[:, :128] * weight_even, odd[:, :128] * weight_odd).astype(BF16)
        diff_im = cols2(even[:, 128:] * weight_even, odd[:, 128:] * weight_odd).astype(BF16)
        back_even = dot(table[4], rows2(diff_re[:128], diff_im[:128]))
        back_odd = dot(table[5], rows2(diff_re[128:], diff_im[128:]))
        both = back_even + back_odd
        less = back_even - back_odd
        back_re = rows2(both[:128], less[:128]).astype(BF16)
        back_im = rows2(both[128:], less[128:]).astype(BF16)
        chi_even = dot(cols2(back_re[:, :128], back_im[:, :128]), table[6])
        chi_odd = dot(cols2(back_re[:, 128:], back_im[:, 128:]), table[7])
        both = chi_even + chi_odd
        less = chi_even - chi_odd
        chi_re = cols2(both[:, :128], less[:, :128])
        chi_im = cols2(both[:, 128:], less[:, 128:])
        gained[0] += probe_re * chi_re + probe_im * chi_im
        gained[1] += probe_re * chi_im - probe_im * chi_re
    for c in range(2):
        grad[c] = gained[c]


def detector_roots(frames, frame, columns, table, root):
    for h in range(2):
        columns[h] = frames[frame, :, 128 * h : 128 * h + 128]
    value = jnp.sqrt(
        rows2(*[cols2(*[columns[h, pl.ds(odd, 128, stride=2), :] for h in range(2)]) for odd in range(2)])
    )
    first = value.astype(BF16)
    rest = value - first.astype(F32)
    second = rest.astype(BF16)
    third = (rest - second.astype(F32)).astype(BF16)
    order = table[8]
    root[...] = dot(first, order) + dot(second, order) + dot(third, order)


def kernel(
    obj_hbm,
    probe_hbm,
    frames_hbm,
    table_hbm,
    off_hbm,
    ids_hbm,
    out_ref,
    off_ref,
    ids_ref,
    tile_rows,
    probe,
    frames,
    table,
    own,
    theirs,
    mine,
    offs,
    listed,
    places,
    held,
    shifted,
    stage,
    patch_a,
    patch_b,
    obj,
    columns,
    roots,
    far,
    power,
    weight,
    grad,
    turned,
    terms,
    recv,
    counts,
    counts_in,
    totals,
    light4,
    lit,
    under,
    hits,
    split,
    result,
    ready,
    rows_in,
    load_sems,
    own_sems,
    off_sems,
    row_sems,
    patch_sems,
    term_sems,
    count_sems,
    last_sems,
    out_sems,
):
    place = Place()
    core, tile = place.core, place.tile
    my_class = place.class_at(0, 0, 0)
    cores = (core, 1 - core)
    twin = place.twin()
    patches = (patch_a, patch_b)
    loads = [
        pltpu.make_async_copy(source, target, load_sems.at[i])
        for i, (source, target) in enumerate(
            (
                (obj_hbm, tile_rows),
                (off_hbm, off_ref),
                (ids_hbm, ids_ref),
                (probe_hbm, probe),
                (table_hbm, table),
                (frames_hbm, frames),
            )
        )
    ]
    for load in loads:
        load.start()

    loads[1].wait()
    lane = lanes_of((1, 128))
    nodes = [(off_ref[p, 1] // 32) * 128 + off_ref[p, 0] // 32 for p in range(2)]
    own[...] = jnp.where(lane // 2 % 2 == core, jnp.where(lane % 2 == 0, nodes[0], nodes[1]), 0)
    enter(place)
    send(own, theirs, own_sems, twin)
    loads[0].wait()
    for grp, other, cls in row_partners(place):
        send(tile_rows.at[:, cls], held.at[pl.ds(2 * tile, 2)], row_sems, (grp, other))
    arrived(theirs, own_sems, 1)
    mine[0] = own[...] + theirs[...]
    for k in FAR_FIRST:
        send(mine.at[0], offs.at[k], off_sems, place.device(STEPS[k]))
    offs[0] = mine[0]
    held[pl.ds(2 * tile, 2)] = tile_rows[:, my_class]

    for load in loads[2:]:
        load.wait()

    def add_light(m, total):
        return total + probe[m, 0] * probe[m, 0] + probe[m, 1] * probe[m, 1]

    light = cols2(lax.fori_loop(0, 8, add_light, jnp.zeros((256, 256), F32)), jnp.zeros((256, 128), F32))
    for s in range(4):
        light4[s] = light if s == 0 else pltpu.roll(light, 32 * s, 1)
    for p in range(2):
        detector_roots(frames, ids_ref[p], columns, table, roots.at[p])
    for j in range(4):
        lit[j] = jnp.zeros((32, 128), F32)

    arrived(offs.at[pl.ds(1, 31)], off_sems, 1)
    packed = jnp.zeros((1, 128), jnp.int32)
    for k in range(32):
        packed = jnp.where(lane // 4 == k, offs[k], packed)
    listed[...] = packed
    copy = pltpu.make_async_copy(listed, places, load_sems.at[6])
    copy.start()
    arrived(held.at[pl.ds(0, 62)], row_sems, 1)
    copy.wait()
    for c in range(2):
        line = jnp.concatenate(
            [held.reshape(512, 128)[pl.ds(2 * q + c, 64, stride=8), :] for q in range(4)], axis=1
        )
        for s in range(4):
            moved_line = line if s == 0 else pltpu.roll(line, 512 - 32 * s, 1)
            for q in range(4):
                shifted[s, c, q] = moved_line[:, 128 * q : 128 * q + 128]

    def give_rows(p):
        for k in FAR_FIRST + [0]:
            value = places[0, 4 * k + 2 * cores[1 if k else 0] + p]
            a = value & 127
            b = value >> 7
            q = b >> 2
            s = b & 3
            for c in range(2):
                for h in range(2):
                    rows = shifted[s, c, q + h, pl.ds(a, 8), :]
                    if k:
                        stage[p, k, c, h] = rows
                    else:
                        patches[p][my_class, c, h] = rows
            if k:
                send(
                    stage.at[p, k],
                    patches[p].at[my_class],
                    patch_sems.at[p],
                    place.device(STEPS[k], -1, 1),
                )

    give_rows(0)

    for p in range(2):
        parts = []
        for u in range(4):
            part = jnp.zeros((1, 128), jnp.int32)
            for kk in range(16):
                part = jnp.where(lane // 8 == kk, places[0, 4 * (16 * (u % 2) + kk) + 2 * cores[u // 2] + p], part)
            parts.append(part)
        key = jnp.concatenate(parts, axis=1)
        step = lanes_of((1, 512))
        goal = (key >> 9) * 32 + (((key & 127) + 1 - core) >> 1) + step % 4
        rows = lax.broadcasted_iota(jnp.int32, (128, 512), 0)
        hits[p, 0] = jnp.where(rows == goal + (step // 4) % 2 * 32, 1.0, 0.0).astype(BF16)
        hits[p, 1] = jnp.where(rows == goal + 64, 1.0, 0.0).astype(BF16)
    grid_row = lax.broadcasted_iota(jnp.int32, (64, 128), 0)
    grid_col = lax.broadcasted_iota(jnp.int32, (64, 128), 1)
    found = jnp.zeros((64, 128), F32)
    for k in range(32):
        for row in range(4):
            value = places[0, 4 * k + row]
            found += jnp.where((grid_row == (value & 127)) & (grid_col == (value >> 7)), 1.0, 0.0)
    counts[...] = found
    send(counts, counts_in, count_sems, place.device((2, 2, 2)))
    give_rows(1)

    def frame(p, between):
        arrived(patches[p].at[pl.ds(0, 31)], patch_sems.at[p], 1)
        flat = patches[p].reshape(1024, 128)
        for c in range(2):
            for a in range(8):
                for h in range(2):
                    start = c * 16 + h * 8 + a
                    obj[c, 32 * a : 32 * a + 32, 128 * h : 128 * h + 128] = flat[pl.ds(start, 32, stride=32), :]
        forward(obj, probe, table, far, power, between)
        weight[...] = roots[p] / jnp.sqrt(jnp.maximum(power[...], 0.1)) - 1.0
        backward(probe, table, far, weight, grad)
        turn = off_ref[p, 1] & 127
        for c in range(2):
            rolled = pltpu.roll(grad[c], turn, 1)
            for h in range(2):
                turned[c, h] = rolled[:, 128 * h : 128 * h + 128]

    def lay_terms(p, other):
        start = ((cores[other] + off_ref[p, 0] // 32) & 1) * 32
        for i in range(32):
            for c in range(2):
                for h in range(2):
                    terms[p, other, i, c, 4 * h : 4 * h + 4] = turned[c, h, pl.ds(start + i, 4, stride=64), :]
        if not other:
            recv[p, 0] = terms[p, 0, my_class]

    def give_terms(p, some):
        for k, other in some:
            if k or other:
                send(
                    terms.at[p, other, place.class_at(*STEPS[k])],
                    recv.at[p, 32 * other + k],
                    term_sems.at[p, other],
                    place.device(STEPS[k], 1, other),
                )

    apart = [(k, 1) for k in FAR_FIRST + [0]]
    alike = [(k, 0) for k in FAR_FIRST]
    frame(0, lambda mode: None)
    lay_terms(0, 1)
    lay_terms(0, 0)
    frame(1, lambda mode: give_terms(0, (apart + alike)[8 * mode : 8 * mode + 8]))
    lay_terms(1, 1)
    give_terms(1, apart)
    lay_terms(1, 0)
    give_terms(1, alike)

    arrived(counts, count_sems, 1)
    totals[0:8] = jnp.zeros((8, 128), F32)
    totals[8:72] = counts[...] + counts_in[...]
    near = totals[pl.ds(2 * tile + core + 1, 8), :]
    for da in range(8):
        for b in range(9):
            q, s = b // 4, b % 4
            many = jnp.broadcast_to(near[7 - da : 8 - da, b : b + 1], (32, 128))
            for j in range(q, min(q + 3, 4)):
                if j - q == 2 and s == 0:
                    continue
                lit[j] += many * light4[s, 32 * da : 32 * da + 32, 128 * (j - q) : 128 * (j - q) + 128]
    for j in range(4):
        for c in range(2):
            under.reshape(256, 128)[pl.ds(2 * j + c, 32, stride=8), :] = lit[j] + 0.1

    sub = lax.broadcasted_iota(jnp.int32, (8, 128), 0)
    full_lane = lanes_of((8, 128))
    for p in range(2):
        for slot in list(range(32, 64, 2)) + list(range(0, 32, 2)):
            if slot == 32:
                arrived(recv.at[p, pl.ds(32, 32)], term_sems.at[p, 1], 1)
            if slot == 0:
                arrived(recv.at[p, pl.ds(1, 31)], term_sems.at[p, 0], 1)
            masks = []
            for d in range(2):
                turn = (places[0, 4 * ((slot + d) % 32) + 2 * cores[slot // 32] + p] >> 7) & 3
                masks.append((sub >= 4) | (full_lane >= 32 * turn))
            for c in range(2):
                pieces = [recv[p, slot + d, c] for d in range(2)]
                kept = rows2(*[jnp.where(masks[d], pieces[d], 0.0) for d in range(2)])
                wrapped = rows2(*[jnp.where(masks[d], 0.0, pieces[d]) for d in range(2)])
                for kind, piece in enumerate((kept, wrapped)):
                    high = piece.astype(BF16)
                    split[kind, 0, 8 * slot : 8 * slot + 16, 128 * c : 128 * c + 128] = high
                    split[kind, 1, 8 * slot : 8 * slot + 16, 128 * c : 128 * c + 128] = (
                        piece - high.astype(F32)
                    ).astype(BF16)
        part = 0.0
        for kind in range(2):
            part += dot(hits[p, kind], split[kind, 0]) + dot(hits[p, kind], split[kind, 1])
        if p == 0:
            result[...] = part
        else:
            result[...] += part
    for j in range(4):
        for c in range(2):
            ready.reshape(256, 128)[pl.ds(2 * j + c, 32, stride=8), :] = result[
                32 * j : 32 * j + 32, 128 * c : 128 * c + 128
            ]

    slot = place.half(0) * 16 + my_class
    for step in ALL_STEPS:
        send(ready.at[place.tile_at(*step)], rows_in.at[slot], last_sems, place.device(step))
    rows_in[slot] = ready[tile]
    arrived(rows_in.at[pl.ds(0, 63)], last_sems, 1)
    here = pl.ds(32 * core, 32)
    out_ref[here] = tile_rows[core] + (rows_in[0:32] + rows_in[32:64]) / under[...]
    send(out_ref.at[here], out_ref.at[here], out_sems, twin)
    arrived(out_ref.at[pl.ds(0, 32)], out_sems, 1)

    arrived(own, own_sems, 0)
    arrived(offs.at[pl.ds(1, 31)], off_sems, 0)
    arrived(held.at[pl.ds(0, 62)], row_sems, 0)
    for p in range(2):
        arrived(patches[p].at[pl.ds(0, 31)], patch_sems.at[p], 0)
        arrived(recv.at[p, pl.ds(1, 31)], term_sems.at[p, 0], 0)
        arrived(recv.at[p, pl.ds(32, 32)], term_sems.at[p, 1], 0)
    arrived(counts, count_sems, 0)
    arrived(rows_in.at[pl.ds(0, 63)], last_sems, 0)
    arrived(out_ref.at[pl.ds(0, 32)], out_sems, 0)


def on_device(object_tile, probe, offsets, frame_ids, frames):
    obj = object_tile.reshape(64, 2, 4, 128).transpose(0, 2, 1, 3).reshape(2, 32, 8, 128)
    hbm = pl.BlockSpec(memory_space=pltpu.HBM)
    pair = pltpu.SemaphoreType.DMA((2,))
    pairs = pltpu.SemaphoreType.DMA((2, 2))
    updated = pl.pallas_call(
        kernel,
        out_shape=pltpu.VMEM((64, 8, 128), F32),
        in_specs=[hbm] * 6,
        out_specs=pl.BlockSpec(memory_space=pltpu.VMEM),
        scratch_shapes=[
            pltpu.SMEM((2, 2), jnp.int32),
            pltpu.SMEM((2,), jnp.int32),
            pltpu.VMEM((2, 32, 8, 128), F32),
            pltpu.VMEM((8, 2, 256, 256), F32),
            pltpu.VMEM((2, 256, 256), F32),
            pltpu.VMEM((9, 256, 256), BF16),
            pltpu.VMEM((1, 128), jnp.int32),
            pltpu.VMEM((1, 128), jnp.int32),
            pltpu.VMEM((1, 1, 128), jnp.int32),
            pltpu.VMEM((32, 1, 128), jnp.int32),
            pltpu.VMEM((1, 128), jnp.int32),
            pltpu.SMEM((1, 128), jnp.int32),
            pltpu.VMEM((64, 8, 128), F32),
            pltpu.VMEM((4, 2, 4, 64, 128), F32),
            pltpu.VMEM((2, 32, 2, 2, 8, 128), F32),
            pltpu.VMEM((32, 2, 2, 8, 128), F32),
            pltpu.VMEM((32, 2, 2, 8, 128), F32),
            pltpu.VMEM((2, 256, 256), F32),
            pltpu.VMEM((2, 256, 128), F32),
            pltpu.VMEM((2, 256, 256), F32),
            pltpu.VMEM((8, 2, 256, 256), F32),
            pltpu.VMEM((256, 256), F32),
            pltpu.VMEM((256, 256), F32),
            pltpu.VMEM((2, 256, 256), F32),
            pltpu.VMEM((2, 2, 256, 128), F32),
            pltpu.VMEM((2, 2, 32, 2, 8, 128), F32),
            pltpu.VMEM((2, 64, 2, 8, 128), F32),
            pltpu.VMEM((64, 128), F32),
            pltpu.VMEM((64, 128), F32),
            pltpu.VMEM((72, 128), F32),
            pltpu.VMEM((4, 256, 384), F32),
            pltpu.VMEM((4, 32, 128), F32),
            pltpu.VMEM((32, 8, 128), F32),
            pltpu.VMEM((2, 2, 128, 512), BF16),
            pltpu.VMEM((2, 2, 512, 256), BF16),
            pltpu.VMEM((128, 256), F32),
            pltpu.VMEM((32, 8, 128), F32),
            pltpu.VMEM((64, 8, 128), F32),
            pltpu.SemaphoreType.DMA((7,)),
            pair,
            pair,
            pair,
            pairs,
            pltpu.SemaphoreType.DMA((2, 2, 2)),
            pair,
            pair,
            pair,
        ],
        compiler_params=pltpu.CompilerParams(
            collective_id=1, has_side_effects=True, vmem_limit_bytes=VMEM_LIMIT
        ),
        name="iteration",
    )(obj, probe, frames, jnp.asarray(tables()), offsets, frame_ids)
    return updated.reshape(64, 4, 2, 128).transpose(0, 2, 1, 3).reshape(64, 2, 512)


def solution(mesh):
    in_specs = (
        P("tile", None, None),
        P(),
        P(("grp", "tile"), None),
        P(("grp", "tile")),
        P(("grp", "tile"), None, None),
    )
    out_specs = P("tile", None, None)
    return jax.shard_map(
        on_device, mesh=mesh, in_specs=in_specs, out_specs=out_specs, check_vma=False
    )
```

```python
import functools

import jax
import jax.numpy as jnp
import ml_dtypes
import numpy as np
from jax import lax
from jax.experimental import pallas as pl
from jax.experimental.pallas import tpu as pltpu
from jax.sharding import PartitionSpec as P

MESH = pl.DeviceIdType.MESH
BF16 = jnp.bfloat16
F32 = jnp.float32
VMEM_LIMIT = 60 << 20


def _weight(step):
    return sum(min(part, 4 - part) for part in step)


STEPS = sorted(
    [
        step
        for step in ((a, b, c) for a in range(4) for b in range(4) for c in range(4))
        if _weight(step) < 3
    ],
    key=_weight,
) + [
    (2, 1, 0),
    (2, 3, 0),
    (0, 2, 1),
    (0, 2, 3),
    (1, 0, 2),
    (3, 0, 2),
    (1, 1, 1),
    (1, 3, 3),
    (3, 1, 3),
    (3, 3, 1),
]
ALL_STEPS = sorted(
    ((a, b, c) for a in range(4) for b in range(4) for c in range(4)), key=_weight, reverse=True
)[:-1]
FAR_FIRST = sorted(range(1, 32), key=lambda k: _weight(STEPS[k]), reverse=True)


class Place:
    def __init__(self):
        grp = lax.axis_index("grp")
        tile = lax.axis_index("tile")
        self.grp, self.tile = grp, tile
        self.core = lax.rem(grp, 2)
        self.x = lax.div(grp, 2) * 2 + lax.rem(tile, 2)
        self.y = lax.rem(lax.div(tile, 2), 4)
        self.z = lax.div(tile, 8)
        self.known = {}

    def once(self, name, make):
        if name not in self.known:
            self.known[name] = make()
        return self.known[name]

    def at(self, axis, by):
        by %= 4
        return self.once((axis, by), lambda: lax.rem(getattr(self, axis) + by, 4) if by else getattr(self, axis))

    def half(self, dx):
        return self.once(("half", dx % 4), lambda: lax.div(self.at("x", dx), 2) * 2)

    def tile_at(self, dx, dy, dz):
        plane = self.once(("plane", dx % 4, dy % 4), lambda: self.at("y", dy) * 2 + lax.rem(self.at("x", dx), 2))
        return self.once(("z8", dz % 4), lambda: self.at("z", dz) * 8) + plane

    def device(self, step, sign=1, other=0):
        dx, dy, dz = (sign * by for by in step)
        grp = self.once(("grp", dx % 4, other), lambda: self.half(dx) + (1 - self.core if other else self.core))
        return grp, self.tile_at(dx, dy, dz)

    def twin(self):
        return self.half(0) + 1 - self.core, self.tile

    def class_at(self, dx, dy, dz):
        near = self.once(
            ("near", dx % 4, dy % 4),
            lambda: lax.rem(self.at("x", dx), 2) * 16 + lax.rem(self.at("y", dy) + self.half(dx), 4) * 4,
        )
        return near + self.once(("deep", dx % 4, dz % 4), lambda: lax.rem(self.at("z", dz) + self.half(dx), 4))


def greet(place):
    barrier = pltpu.get_barrier_semaphore()
    for to in row_partners(place):
        pl.semaphore_signal(barrier, inc=1, device_id=to[:2], device_id_type=MESH)
    odd = lax.rem(place.tile, 2)
    beside = [step for step in STEPS if step[0] == 2]
    for step in beside:
        pl.semaphore_signal(barrier, inc=1, device_id=place.device(step, -1), device_id_type=MESH)
    ups = [step for step in STEPS if step[0] == 1]
    downs = [step for step in STEPS if step[0] == 3]
    assert len(ups) == len(downs)
    for up, down in zip(ups, downs):
        grp_a, tile_a = place.device(up, -1)
        grp_b, tile_b = place.device(down, -1)
        to = (grp_a + odd * (grp_b - grp_a), tile_a + odd * (tile_b - tile_a))
        pl.semaphore_signal(barrier, inc=1, device_id=to, device_id_type=MESH)
    pl.semaphore_signal(barrier, inc=1, device_id=place.twin(), device_id_type=MESH)
    return 31 + len(beside) + len(ups) + 1


def row_partners(place):
    across = lax.rem(place.tile + 1, 2) - lax.rem(place.tile, 2)
    partners = []
    for dx, dy, dz in sorted(
        ((a, b, c) for a in range(2) for b in range(4) for c in range(4)), key=_weight, reverse=True
    )[:-1]:
        plane = place.tile_at(0, dy, dz)
        cls = place.class_at(0, dy, dz)
        partners.append((place.grp, plane + dx * across, cls + 16 * dx * across))
    return partners


def send(source, target, sems, to):
    copy = pltpu.make_async_remote_copy(
        src_ref=source,
        dst_ref=target,
        send_sem=sems.at[0],
        recv_sem=sems.at[1],
        device_id=to,
        device_id_type=MESH,
    )
    copy.start()


def arrived(ref, sems, which):
    pltpu.make_async_copy(ref, ref, sems.at[which]).wait()


def lanes_of(shape):
    return lax.broadcasted_iota(jnp.int32, shape, len(shape) - 1)


def tables():
    line = np.arange(256)
    angle = 2.0 * np.pi / 256 * (line[:, None] * line[None, :] % 256)
    re = (np.cos(angle) / 16).astype(ml_dtypes.bfloat16)
    im = (-np.sin(angle) / 16).astype(ml_dtypes.bfloat16)

    def real_form(table_re, table_im, left):
        if left:
            return np.block([[table_re, -table_im], [table_im, table_re]])
        return np.block([[table_re, table_im], [-table_im, table_re]])

    made = []
    for odd in range(2):
        made.append(real_form(re[odd::2, :128], im[odd::2, :128], True))
    for odd in range(2):
        made.append(real_form(re[:128, odd::2], im[:128, odd::2], False))
    for odd in range(2):
        made.append(real_form(re[:128, odd::2], -im[:128, odd::2], True))
    for odd in range(2):
        made.append(real_form(re[odd::2, :128], -im[odd::2, :128], False))
    order = np.zeros((256, 256), ml_dtypes.bfloat16)
    order[np.concatenate([line[0::2], line[1::2]]), line] = 1
    made.append(order)
    return np.stack([table.astype(ml_dtypes.bfloat16) for table in made])


def dot(a, b):
    return jnp.dot(a, b, preferred_element_type=F32)


def rows2(a, b):
    return jnp.concatenate([a, b], axis=0)


def cols2(a, b):
    return jnp.concatenate([a, b], axis=1)


def forward(obj, probe, table, far, power, between):
    gained = [0.0, 0.0]
    for mode in range(8):
        probe_re = probe[mode, 0]
        probe_im = probe[mode, 1]
        obj_re = obj[0]
        obj_im = obj[1]
        exit_re = probe_re * obj_re - probe_im * obj_im
        exit_im = probe_re * obj_im + probe_im * obj_re
        both = rows2(exit_re[:128] + exit_re[128:], exit_im[:128] + exit_im[128:]).astype(BF16)
        less = rows2(exit_re[:128] - exit_re[128:], exit_im[:128] - exit_im[128:]).astype(BF16)
        sums = []
        lesses = []
        for half in (dot(table[0], both), dot(table[1], less)):
            re, im = half[:128], half[128:]
            sums.append(cols2(re[:, :128] + re[:, 128:], im[:, :128] + im[:, 128:]))
            lesses.append(cols2(re[:, :128] - re[:, 128:], im[:, :128] - im[:, 128:]))
        far_even = dot(rows2(*sums).astype(BF16), table[2])
        far_odd = dot(rows2(*lesses).astype(BF16), table[3])
        far[mode, 0] = far_even
        far[mode, 1] = far_odd
        for odd, wave in enumerate((far_even, far_odd)):
            re, im = wave[:, :128], wave[:, 128:]
            gained[odd] += re * re + im * im
        between(mode)
    for odd in range(2):
        power[:, odd * 128 : odd * 128 + 128] = gained[odd]


def backward(probe, table, far, weight, grad):
    weight_even = weight[:, :128]
    weight_odd = weight[:, 128:]
    gained = [0.0, 0.0]
    for mode in range(8):
        probe_re = probe[mode, 0]
        probe_im = probe[mode, 1]
        even = far[mode, 0]
        odd = far[mode, 1]
        diff_re = cols2(even[:, :128] * weight_even, odd[:, :128] * weight_odd).astype(BF16)
        diff_im = cols2(even[:, 128:] * weight_even, odd[:, 128:] * weight_odd).astype(BF16)
        back_even = dot(table[4], rows2(diff_re[:128], diff_im[:128]))
        back_odd = dot(table[5], rows2(diff_re[128:], diff_im[128:]))
        both = back_even + back_odd
        less = back_even - back_odd
        back_re = rows2(both[:128], less[:128]).astype(BF16)
        back_im = rows2(both[128:], less[128:]).astype(BF16)
        chi_even = dot(cols2(back_re[:, :128], back_im[:, :128]), table[6])
        chi_odd = dot(cols2(back_re[:, 128:], back_im[:, 128:]), table[7])
        both = chi_even + chi_odd
        less = chi_even - chi_odd
        chi_re = cols2(both[:, :128], less[:, :128])
        chi_im = cols2(both[:, 128:], less[:, 128:])
        gained[0] += probe_re * chi_re + probe_im * chi_im
        gained[1] += probe_re * chi_im - probe_im * chi_re
    for c in range(2):
        grad[c] = gained[c]


def detector_roots(frames, frame, columns, table, root):
    for h in range(2):
        columns[h] = frames[frame, :, 128 * h : 128 * h + 128]
    value = jnp.sqrt(
        rows2(*[cols2(*[columns[h, pl.ds(odd, 128, stride=2), :] for h in range(2)]) for odd in range(2)])
    )
    first = value.astype(BF16)
    rest = value - first.astype(F32)
    second = rest.astype(BF16)
    third = (rest - second.astype(F32)).astype(BF16)
    order = table[8]
    root[...] = dot(first, order) + dot(second, order) + dot(third, order)


def kernel(
    obj_hbm,
    probe_hbm,
    frames_hbm,
    table_hbm,
    off_hbm,
    ids_hbm,
    out_ref,
    off_ref,
    ids_ref,
    tile_rows,
    probe,
    frames,
    table,
    own,
    theirs,
    mine,
    offs,
    listed,
    places,
    held,
    shifted,
    stage,
    patch_a,
    patch_b,
    obj,
    columns,
    roots,
    far,
    power,
    weight,
    grad,
    turned,
    terms,
    recv,
    counts,
    counts_in,
    totals,
    light4,
    lit,
    under,
    hits,
    split,
    result,
    ready,
    rows_in,
    load_sems,
    own_sems,
    off_sems,
    row_sems,
    patch_sems,
    term_sems,
    count_sems,
    last_sems,
    out_sems,
):
    place = Place()
    core, tile = place.core, place.tile
    my_class = place.class_at(0, 0, 0)
    cores = (core, 1 - core)
    twin = place.twin()
    patches = (patch_a, patch_b)
    loads = [
        pltpu.make_async_copy(source, target, load_sems.at[i])
        for i, (source, target) in enumerate(
            (
                (obj_hbm, tile_rows),
                (off_hbm, off_ref),
                (ids_hbm, ids_ref),
                (probe_hbm, probe),
                (table_hbm, table),
                (frames_hbm, frames),
            )
        )
    ]
    loads[0].start()
    met = greet(place)
    for load in loads[1:]:
        load.start()

    loads[1].wait()
    lane = lanes_of((1, 128))
    nodes = [(off_ref[p, 1] // 32) * 128 + off_ref[p, 0] // 32 for p in range(2)]
    own[...] = jnp.where(lane // 2 % 2 == core, jnp.where(lane % 2 == 0, nodes[0], nodes[1]), 0)
    pl.semaphore_wait(pltpu.get_barrier_semaphore(), met)
    send(own, theirs, own_sems, twin)
    loads[0].wait()
    for grp, other, cls in row_partners(place):
        send(tile_rows.at[:, cls], held.at[pl.ds(2 * tile, 2)], row_sems, (grp, other))
    arrived(theirs, own_sems, 1)
    mine[0] = own[...] + theirs[...]
    for k in FAR_FIRST:
        send(mine.at[0], offs.at[k], off_sems, place.device(STEPS[k]))
    offs[0] = mine[0]
    held[pl.ds(2 * tile, 2)] = tile_rows[:, my_class]

    for load in loads[2:]:
        load.wait()

    def add_light(m, total):
        return total + probe[m, 0] * probe[m, 0] + probe[m, 1] * probe[m, 1]

    light = cols2(lax.fori_loop(0, 8, add_light, jnp.zeros((256, 256), F32)), jnp.zeros((256, 128), F32))
    for s in range(4):
        light4[s] = light if s == 0 else pltpu.roll(light, 32 * s, 1)
    for p in range(2):
        detector_roots(frames, ids_ref[p], columns, table, roots.at[p])
    for j in range(4):
        lit[j] = jnp.zeros((32, 128), F32)

    arrived(offs.at[pl.ds(1, 31)], off_sems, 1)
    packed = jnp.zeros((1, 128), jnp.int32)
    for k in range(32):
        packed = jnp.where(lane // 4 == k, offs[k], packed)
    listed[...] = packed
    copy = pltpu.make_async_copy(listed, places, load_sems.at[6])
    copy.start()
    arrived(held.at[pl.ds(0, 62)], row_sems, 1)
    copy.wait()
    for c in range(2):
        line = jnp.concatenate(
            [held.reshape(512, 128)[pl.ds(2 * q + c, 64, stride=8), :] for q in range(4)], axis=1
        )
        for s in range(4):
            moved_line = line if s == 0 else pltpu.roll(line, 512 - 32 * s, 1)
            for q in range(4):
                shifted[s, c, q] = moved_line[:, 128 * q : 128 * q + 128]

    def give_rows(p):
        for k in FAR_FIRST + [0]:
            value = places[0, 4 * k + 2 * cores[1 if k else 0] + p]
            a = value & 127
            b = value >> 7
            q = b >> 2
            s = b & 3
            for c in range(2):
                for h in range(2):
                    rows = shifted[s, c, q + h, pl.ds(a, 8), :]
                    if k:
                        stage[p, k, c, h] = rows
                    else:
                        patches[p][my_class, c, h] = rows
            if k:
                send(
                    stage.at[p, k],
                    patches[p].at[my_class],
                    patch_sems.at[p],
                    place.device(STEPS[k], -1, 1),
                )

    give_rows(0)

    for p in range(2):
        parts = []
        for u in range(4):
            part = jnp.zeros((1, 128), jnp.int32)
            for kk in range(16):
                part = jnp.where(lane // 8 == kk, places[0, 4 * (16 * (u % 2) + kk) + 2 * cores[u // 2] + p], part)
            parts.append(part)
        key = jnp.concatenate(parts, axis=1)
        step = lanes_of((1, 512))
        goal = (key >> 9) * 32 + (((key & 127) + 1 - core) >> 1) + step % 4
        rows = lax.broadcasted_iota(jnp.int32, (128, 512), 0)
        hits[p, 0] = jnp.where(rows == goal + (step // 4) % 2 * 32, 1.0, 0.0).astype(BF16)
        hits[p, 1] = jnp.where(rows == goal + 64, 1.0, 0.0).astype(BF16)
    grid_row = lax.broadcasted_iota(jnp.int32, (64, 128), 0)
    grid_col = lax.broadcasted_iota(jnp.int32, (64, 128), 1)
    found = jnp.zeros((64, 128), F32)
    for k in range(32):
        for row in range(4):
            value = places[0, 4 * k + row]
            found += jnp.where((grid_row == (value & 127)) & (grid_col == (value >> 7)), 1.0, 0.0)
    counts[...] = found
    send(counts, counts_in, count_sems, place.device((2, 2, 2)))
    give_rows(1)

    def frame(p, between):
        arrived(patches[p].at[pl.ds(0, 31)], patch_sems.at[p], 1)
        flat = patches[p].reshape(1024, 128)
        for c in range(2):
            for a in range(8):
                for h in range(2):
                    start = c * 16 + h * 8 + a
                    obj[c, 32 * a : 32 * a + 32, 128 * h : 128 * h + 128] = flat[pl.ds(start, 32, stride=32), :]
        forward(obj, probe, table, far, power, between)
        weight[...] = roots[p] / jnp.sqrt(jnp.maximum(power[...], 0.1)) - 1.0
        backward(probe, table, far, weight, grad)
        turn = off_ref[p, 1] & 127
        for c in range(2):
            rolled = pltpu.roll(grad[c], turn, 1)
            for h in range(2):
                turned[c, h] = rolled[:, 128 * h : 128 * h + 128]

    def lay_terms(p, other):
        start = ((cores[other] + off_ref[p, 0] // 32) & 1) * 32
        for i in range(32):
            for c in range(2):
                for h in range(2):
                    terms[p, other, i, c, 4 * h : 4 * h + 4] = turned[c, h, pl.ds(start + i, 4, stride=64), :]
        if not other:
            recv[p, 0] = terms[p, 0, my_class]

    def give_terms(p, some):
        for k, other in some:
            if k or other:
                send(
                    terms.at[p, other, place.class_at(*STEPS[k])],
                    recv.at[p, 32 * other + k],
                    term_sems.at[p, other],
                    place.device(STEPS[k], 1, other),
                )

    apart = [(k, 1) for k in FAR_FIRST + [0]]
    alike = [(k, 0) for k in FAR_FIRST]
    frame(0, lambda mode: None)
    lay_terms(0, 1)
    lay_terms(0, 0)
    frame(1, lambda mode: give_terms(0, (apart + alike)[8 * mode : 8 * mode + 8]))
    lay_terms(1, 1)
    give_terms(1, apart)
    lay_terms(1, 0)
    give_terms(1, alike)

    arrived(counts, count_sems, 1)
    totals[0:8] = jnp.zeros((8, 128), F32)
    totals[8:72] = counts[...] + counts_in[...]
    near = totals[pl.ds(2 * tile + core + 1, 8), :]
    for da in range(8):
        for b in range(9):
            q, s = b // 4, b % 4
            many = jnp.broadcast_to(near[7 - da : 8 - da, b : b + 1], (32, 128))
            for j in range(q, min(q + 3, 4)):
                if j - q == 2 and s == 0:
                    continue
                lit[j] += many * light4[s, 32 * da : 32 * da + 32, 128 * (j - q) : 128 * (j - q) + 128]
    for j in range(4):
        for c in range(2):
            under.reshape(256, 128)[pl.ds(2 * j + c, 32, stride=8), :] = lit[j] + 0.1

    sub = lax.broadcasted_iota(jnp.int32, (8, 128), 0)
    full_lane = lanes_of((8, 128))
    for p in range(2):
        for slot in list(range(32, 64, 2)) + list(range(0, 32, 2)):
            if slot == 32:
                arrived(recv.at[p, pl.ds(32, 32)], term_sems.at[p, 1], 1)
            if slot == 0:
                arrived(recv.at[p, pl.ds(1, 31)], term_sems.at[p, 0], 1)
            masks = []
            for d in range(2):
                turn = (places[0, 4 * ((slot + d) % 32) + 2 * cores[slot // 32] + p] >> 7) & 3
                masks.append((sub >= 4) | (full_lane >= 32 * turn))
            for c in range(2):
                pieces = [recv[p, slot + d, c] for d in range(2)]
                kept = rows2(*[jnp.where(masks[d], pieces[d], 0.0) for d in range(2)])
                wrapped = rows2(*[jnp.where(masks[d], 0.0, pieces[d]) for d in range(2)])
                for kind, piece in enumerate((kept, wrapped)):
                    high = piece.astype(BF16)
                    split[kind, 0, 8 * slot : 8 * slot + 16, 128 * c : 128 * c + 128] = high
                    split[kind, 1, 8 * slot : 8 * slot + 16, 128 * c : 128 * c + 128] = (
                        piece - high.astype(F32)
                    ).astype(BF16)
        part = 0.0
        for kind in range(2):
            part += dot(hits[p, kind], split[kind, 0]) + dot(hits[p, kind], split[kind, 1])
        if p == 0:
            result[...] = part
        else:
            result[...] += part
    for j in range(4):
        for c in range(2):
            ready.reshape(256, 128)[pl.ds(2 * j + c, 32, stride=8), :] = result[
                32 * j : 32 * j + 32, 128 * c : 128 * c + 128
            ]

    slot = place.half(0) * 16 + my_class
    for step in ALL_STEPS:
        send(ready.at[place.tile_at(*step)], rows_in.at[slot], last_sems, place.device(step))
    rows_in[slot] = ready[tile]
    arrived(rows_in.at[pl.ds(0, 63)], last_sems, 1)
    here = pl.ds(32 * core, 32)
    out_ref[here] = tile_rows[core] + (rows_in[0:32] + rows_in[32:64]) / under[...]
    send(out_ref.at[here], out_ref.at[here], out_sems, twin)
    arrived(out_ref.at[pl.ds(0, 32)], out_sems, 1)

    arrived(own, own_sems, 0)
    arrived(offs.at[pl.ds(1, 31)], off_sems, 0)
    arrived(held.at[pl.ds(0, 62)], row_sems, 0)
    for p in range(2):
        arrived(patches[p].at[pl.ds(0, 31)], patch_sems.at[p], 0)
        arrived(recv.at[p, pl.ds(1, 31)], term_sems.at[p, 0], 0)
        arrived(recv.at[p, pl.ds(32, 32)], term_sems.at[p, 1], 0)
    arrived(counts, count_sems, 0)
    arrived(rows_in.at[pl.ds(0, 63)], last_sems, 0)
    arrived(out_ref.at[pl.ds(0, 32)], out_sems, 0)


def on_device(object_tile, probe, offsets, frame_ids, frames):
    obj = object_tile.reshape(64, 2, 4, 128).transpose(0, 2, 1, 3).reshape(2, 32, 8, 128)
    hbm = pl.BlockSpec(memory_space=pltpu.HBM)
    pair = pltpu.SemaphoreType.DMA((2,))
    pairs = pltpu.SemaphoreType.DMA((2, 2))
    updated = pl.pallas_call(
        kernel,
        out_shape=pltpu.VMEM((64, 8, 128), F32),
        in_specs=[hbm] * 6,
        out_specs=pl.BlockSpec(memory_space=pltpu.VMEM),
        scratch_shapes=[
            pltpu.SMEM((2, 2), jnp.int32),
            pltpu.SMEM((2,), jnp.int32),
            pltpu.VMEM((2, 32, 8, 128), F32),
            pltpu.VMEM((8, 2, 256, 256), F32),
            pltpu.VMEM((2, 256, 256), F32),
            pltpu.VMEM((9, 256, 256), BF16),
            pltpu.VMEM((1, 128), jnp.int32),
            pltpu.VMEM((1, 128), jnp.int32),
            pltpu.VMEM((1, 1, 128), jnp.int32),
            pltpu.VMEM((32, 1, 128), jnp.int32),
            pltpu.VMEM((1, 128), jnp.int32),
            pltpu.SMEM((1, 128), jnp.int32),
            pltpu.VMEM((64, 8, 128), F32),
            pltpu.VMEM((4, 2, 4, 64, 128), F32),
            pltpu.VMEM((2, 32, 2, 2, 8, 128), F32),
            pltpu.VMEM((32, 2, 2, 8, 128), F32),
            pltpu.VMEM((32, 2, 2, 8, 128), F32),
            pltpu.VMEM((2, 256, 256), F32),
            pltpu.VMEM((2, 256, 128), F32),
            pltpu.VMEM((2, 256, 256), F32),
            pltpu.VMEM((8, 2, 256, 256), F32),
            pltpu.VMEM((256, 256), F32),
            pltpu.VMEM((256, 256), F32),
            pltpu.VMEM((2, 256, 256), F32),
            pltpu.VMEM((2, 2, 256, 128), F32),
            pltpu.VMEM((2, 2, 32, 2, 8, 128), F32),
            pltpu.VMEM((2, 64, 2, 8, 128), F32),
            pltpu.VMEM((64, 128), F32),
            pltpu.VMEM((64, 128), F32),
            pltpu.VMEM((72, 128), F32),
            pltpu.VMEM((4, 256, 384), F32),
            pltpu.VMEM((4, 32, 128), F32),
            pltpu.VMEM((32, 8, 128), F32),
            pltpu.VMEM((2, 2, 128, 512), BF16),
            pltpu.VMEM((2, 2, 512, 256), BF16),
            pltpu.VMEM((128, 256), F32),
            pltpu.VMEM((32, 8, 128), F32),
            pltpu.VMEM((64, 8, 128), F32),
            pltpu.SemaphoreType.DMA((7,)),
            pair,
            pair,
            pair,
            pairs,
            pltpu.SemaphoreType.DMA((2, 2, 2)),
            pair,
            pair,
            pair,
        ],
        compiler_params=pltpu.CompilerParams(
            collective_id=1, has_side_effects=True, vmem_limit_bytes=VMEM_LIMIT
        ),
        name="iteration",
    )(obj, probe, frames, jnp.asarray(tables()), offsets, frame_ids)
    return updated.reshape(64, 4, 2, 128).transpose(0, 2, 1, 3).reshape(64, 2, 512)


def solution(mesh):
    in_specs = (
        P("tile", None, None),
        P(),
        P(("grp", "tile"), None),
        P(("grp", "tile")),
        P(("grp", "tile"), None, None),
    )
    out_specs = P("tile", None, None)
    return jax.shard_map(
        on_device, mesh=mesh, in_specs=in_specs, out_specs=out_specs, check_vma=False
    )
```

```python
import functools

import jax
import jax.numpy as jnp
import ml_dtypes
import numpy as np
from jax import lax
from jax.experimental import pallas as pl
from jax.experimental.pallas import tpu as pltpu
from jax.sharding import PartitionSpec as P

MESH = pl.DeviceIdType.MESH
BF16 = jnp.bfloat16
F32 = jnp.float32
VMEM_LIMIT = 60 << 20


def _weight(step):
    return sum(min(part, 4 - part) for part in step)


STEPS = sorted(
    [
        step
        for step in ((a, b, c) for a in range(4) for b in range(4) for c in range(4))
        if _weight(step) < 3
    ],
    key=_weight,
) + [
    (2, 1, 0),
    (2, 3, 0),
    (0, 2, 1),
    (0, 2, 3),
    (1, 0, 2),
    (3, 0, 2),
    (1, 1, 1),
    (1, 3, 3),
    (3, 1, 3),
    (3, 3, 1),
]
ALL_STEPS = sorted(
    ((a, b, c) for a in range(4) for b in range(4) for c in range(4)), key=_weight, reverse=True
)[:-1]
FAR_FIRST = sorted(range(1, 32), key=lambda k: _weight(STEPS[k]), reverse=True)


class Place:
    def __init__(self):
        grp = lax.axis_index("grp")
        tile = lax.axis_index("tile")
        self.grp, self.tile = grp, tile
        self.core = lax.rem(grp, 2)
        self.x = lax.div(grp, 2) * 2 + lax.rem(tile, 2)
        self.y = lax.rem(lax.div(tile, 2), 4)
        self.z = lax.div(tile, 8)
        self.known = {}

    def once(self, name, make):
        if name not in self.known:
            self.known[name] = make()
        return self.known[name]

    def at(self, axis, by):
        by %= 4
        return self.once((axis, by), lambda: lax.rem(getattr(self, axis) + by, 4) if by else getattr(self, axis))

    def half(self, dx):
        return self.once(("half", dx % 4), lambda: lax.div(self.at("x", dx), 2) * 2)

    def tile_at(self, dx, dy, dz):
        plane = self.once(("plane", dx % 4, dy % 4), lambda: self.at("y", dy) * 2 + lax.rem(self.at("x", dx), 2))
        return self.once(("z8", dz % 4), lambda: self.at("z", dz) * 8) + plane

    def device(self, step, sign=1, other=0):
        dx, dy, dz = (sign * by for by in step)
        grp = self.once(("grp", dx % 4, other), lambda: self.half(dx) + (1 - self.core if other else self.core))
        return grp, self.tile_at(dx, dy, dz)

    def twin(self):
        return self.half(0) + 1 - self.core, self.tile

    def class_at(self, dx, dy, dz):
        near = self.once(
            ("near", dx % 4, dy % 4),
            lambda: lax.rem(self.at("x", dx), 2) * 16 + lax.rem(self.at("y", dy) + self.half(dx), 4) * 4,
        )
        return near + self.once(("deep", dx % 4, dz % 4), lambda: lax.rem(self.at("z", dz) + self.half(dx), 4))


def greet(place):
    barrier = pltpu.get_barrier_semaphore()
    for to in row_partners(place):
        pl.semaphore_signal(barrier, inc=1, device_id=to[:2], device_id_type=MESH)
    odd = lax.rem(place.tile, 2)
    beside = [step for step in STEPS if step[0] == 2]
    for step in beside:
        pl.semaphore_signal(barrier, inc=1, device_id=place.device(step, -1), device_id_type=MESH)
    ups = [step for step in STEPS if step[0] == 1]
    downs = [step for step in STEPS if step[0] == 3]
    assert len(ups) == len(downs)
    for up, down in zip(ups, downs):
        grp_a, tile_a = place.device(up, -1)
        grp_b, tile_b = place.device(down, -1)
        to = (grp_a + odd * (grp_b - grp_a), tile_a + odd * (tile_b - tile_a))
        pl.semaphore_signal(barrier, inc=1, device_id=to, device_id_type=MESH)
    pl.semaphore_signal(barrier, inc=1, device_id=place.twin(), device_id_type=MESH)
    return 31 + len(beside) + len(ups) + 1


def row_partners(place):
    across = lax.rem(place.tile + 1, 2) - lax.rem(place.tile, 2)
    partners = []
    for dx, dy, dz in sorted(
        ((a, b, c) for a in range(2) for b in range(4) for c in range(4)), key=_weight, reverse=True
    )[:-1]:
        plane = place.tile_at(0, dy, dz)
        cls = place.class_at(0, dy, dz)
        partners.append((place.grp, plane + dx * across, cls + 16 * dx * across))
    return partners


def send(source, target, sems, to):
    copy = pltpu.make_async_remote_copy(
        src_ref=source,
        dst_ref=target,
        send_sem=sems.at[0],
        recv_sem=sems.at[1],
        device_id=to,
        device_id_type=MESH,
    )
    copy.start()


def arrived(ref, sems, which):
    pltpu.make_async_copy(ref, ref, sems.at[which]).wait()


def lanes_of(shape):
    return lax.broadcasted_iota(jnp.int32, shape, len(shape) - 1)


def tables():
    line = np.arange(256)
    angle = 2.0 * np.pi / 256 * (line[:, None] * line[None, :] % 256)
    re = (np.cos(angle) / 16).astype(ml_dtypes.bfloat16)
    im = (-np.sin(angle) / 16).astype(ml_dtypes.bfloat16)

    def real_form(table_re, table_im, left):
        if left:
            return np.block([[table_re, -table_im], [table_im, table_re]])
        return np.block([[table_re, table_im], [-table_im, table_re]])

    made = []
    for odd in range(2):
        made.append(real_form(re[odd::2, :128], im[odd::2, :128], True))
    for odd in range(2):
        made.append(real_form(re[:128, odd::2], im[:128, odd::2], False))
    for odd in range(2):
        made.append(real_form(re[:128, odd::2], -im[:128, odd::2], True))
    for odd in range(2):
        made.append(real_form(re[odd::2, :128], -im[odd::2, :128], False))
    order = np.zeros((256, 256), ml_dtypes.bfloat16)
    order[np.concatenate([line[0::2], line[1::2]]), line] = 1
    made.append(order)
    return np.stack([table.astype(ml_dtypes.bfloat16) for table in made])


def dot(a, b):
    return jnp.dot(a, b, preferred_element_type=F32)


def rows2(a, b):
    return jnp.concatenate([a, b], axis=0)


def cols2(a, b):
    return jnp.concatenate([a, b], axis=1)


def forward(obj, probe, table, far, power, between):
    gained = [0.0, 0.0]
    for mode in range(8):
        probe_re = probe[mode, 0]
        probe_im = probe[mode, 1]
        obj_re = obj[0]
        obj_im = obj[1]
        exit_re = probe_re * obj_re - probe_im * obj_im
        exit_im = probe_re * obj_im + probe_im * obj_re
        both = rows2(exit_re[:128] + exit_re[128:], exit_im[:128] + exit_im[128:]).astype(BF16)
        less = rows2(exit_re[:128] - exit_re[128:], exit_im[:128] - exit_im[128:]).astype(BF16)
        sums = []
        lesses = []
        for half in (dot(table[0], both), dot(table[1], less)):
            re, im = half[:128], half[128:]
            sums.append(cols2(re[:, :128] + re[:, 128:], im[:, :128] + im[:, 128:]))
            lesses.append(cols2(re[:, :128] - re[:, 128:], im[:, :128] - im[:, 128:]))
        far_even = dot(rows2(*sums).astype(BF16), table[2])
        far_odd = dot(rows2(*lesses).astype(BF16), table[3])
        far[mode, 0] = far_even
        far[mode, 1] = far_odd
        for odd, wave in enumerate((far_even, far_odd)):
            re, im = wave[:, :128], wave[:, 128:]
            gained[odd] += re * re + im * im
        between(mode)
    for odd in range(2):
        power[:, odd * 128 : odd * 128 + 128] = gained[odd]


def backward(probe, table, far, weight, grad):
    weight_even = weight[:, :128]
    weight_odd = weight[:, 128:]
    gained = [0.0, 0.0]
    for mode in range(8):
        probe_re = probe[mode, 0]
        probe_im = probe[mode, 1]
        even = far[mode, 0]
        odd = far[mode, 1]
        diff_re = cols2(even[:, :128] * weight_even, odd[:, :128] * weight_odd).astype(BF16)
        diff_im = cols2(even[:, 128:] * weight_even, odd[:, 128:] * weight_odd).astype(BF16)
        back_even = dot(table[4], rows2(diff_re[:128], diff_im[:128]))
        back_odd = dot(table[5], rows2(diff_re[128:], diff_im[128:]))
        both = back_even + back_odd
        less = back_even - back_odd
        back_re = rows2(both[:128], less[:128]).astype(BF16)
        back_im = rows2(both[128:], less[128:]).astype(BF16)
        chi_even = dot(cols2(back_re[:, :128], back_im[:, :128]), table[6])
        chi_odd = dot(cols2(back_re[:, 128:], back_im[:, 128:]), table[7])
        both = chi_even + chi_odd
        less = chi_even - chi_odd
        chi_re = cols2(both[:, :128], less[:, :128])
        chi_im = cols2(both[:, 128:], less[:, 128:])
        gained[0] += probe_re * chi_re + probe_im * chi_im
        gained[1] += probe_re * chi_im - probe_im * chi_re
    for c in range(2):
        grad[c] = gained[c]


def detector_roots(frames, frame, columns, table, root):
    for h in range(2):
        columns[h] = frames[frame, :, 128 * h : 128 * h + 128]
    value = jnp.sqrt(
        rows2(*[cols2(*[columns[h, pl.ds(odd, 128, stride=2), :] for h in range(2)]) for odd in range(2)])
    )
    first = value.astype(BF16)
    rest = value - first.astype(F32)
    second = rest.astype(BF16)
    third = (rest - second.astype(F32)).astype(BF16)
    order = table[8]
    root[...] = dot(first, order) + dot(second, order) + dot(third, order)


def kernel(
    obj_hbm,
    probe_hbm,
    frames_hbm,
    table_hbm,
    off_hbm,
    ids_hbm,
    out_ref,
    off_ref,
    ids_ref,
    tile_rows,
    probe,
    frames,
    table,
    own,
    theirs,
    mine,
    offs,
    listed,
    places,
    held,
    shifted,
    stage,
    patch_a,
    patch_b,
    obj,
    columns,
    roots,
    far,
    power,
    weight,
    grad,
    turned,
    terms,
    recv,
    counts,
    counts_in,
    totals,
    light4,
    lit,
    under,
    hits,
    split,
    result,
    ready,
    rows_in,
    load_sems,
    own_sems,
    off_sems,
    row_sems,
    patch_sems,
    term_sems,
    count_sems,
    last_sems,
    out_sems,
):
    place = Place()
    core, tile = place.core, place.tile
    my_class = place.class_at(0, 0, 0)
    cores = (core, 1 - core)
    twin = place.twin()
    patches = (patch_a, patch_b)
    loads = [
        pltpu.make_async_copy(source, target, load_sems.at[i])
        for i, (source, target) in enumerate(
            (
                (obj_hbm, tile_rows),
                (off_hbm, off_ref),
                (ids_hbm, ids_ref),
                (probe_hbm, probe),
                (table_hbm, table),
                (frames_hbm, frames),
            )
        )
    ]
    loads[0].start()
    met = greet(place)
    for load in loads[1:]:
        load.start()

    loads[1].wait()
    lane = lanes_of((1, 128))
    nodes = [(off_ref[p, 1] // 32) * 128 + off_ref[p, 0] // 32 for p in range(2)]
    own[...] = jnp.where(lane // 2 % 2 == core, jnp.where(lane % 2 == 0, nodes[0], nodes[1]), 0)
    pl.semaphore_wait(pltpu.get_barrier_semaphore(), met)
    send(own, theirs, own_sems, twin)
    loads[0].wait()
    for grp, other, cls in row_partners(place):
        send(tile_rows.at[:, cls], held.at[pl.ds(2 * tile, 2)], row_sems, (grp, other))
    arrived(theirs, own_sems, 1)
    mine[0] = own[...] + theirs[...]
    for k in FAR_FIRST:
        send(mine.at[0], offs.at[k], off_sems, place.device(STEPS[k]))
    offs[0] = mine[0]
    held[pl.ds(2 * tile, 2)] = tile_rows[:, my_class]

    for load in loads[2:]:
        load.wait()

    def add_light(m, total):
        return total + probe[m, 0] * probe[m, 0] + probe[m, 1] * probe[m, 1]

    light = cols2(lax.fori_loop(0, 8, add_light, jnp.zeros((256, 256), F32)), jnp.zeros((256, 128), F32))
    for s in range(4):
        light4[s] = light if s == 0 else pltpu.roll(light, 32 * s, 1)
    for p in range(2):
        detector_roots(frames, ids_ref[p], columns, table, roots.at[p])
    for j in range(4):
        lit[j] = jnp.zeros((32, 128), F32)

    arrived(offs.at[pl.ds(1, 31)], off_sems, 1)
    packed = jnp.zeros((1, 128), jnp.int32)
    for k in range(32):
        packed = jnp.where(lane // 4 == k, offs[k], packed)
    listed[...] = packed
    copy = pltpu.make_async_copy(listed, places, load_sems.at[6])
    copy.start()
    arrived(held.at[pl.ds(0, 62)], row_sems, 1)
    copy.wait()
    for c in range(2):
        line = jnp.concatenate(
            [held.reshape(512, 128)[pl.ds(2 * q + c, 64, stride=8), :] for q in range(4)], axis=1
        )
        for s in range(4):
            moved_line = line if s == 0 else pltpu.roll(line, 512 - 32 * s, 1)
            for q in range(4):
                shifted[s, c, q] = moved_line[:, 128 * q : 128 * q + 128]

    def give_rows(p):
        for k in FAR_FIRST + [0]:
            value = places[0, 4 * k + 2 * cores[1 if k else 0] + p]
            a = value & 127
            b = value >> 7
            q = b >> 2
            s = b & 3
            for c in range(2):
                for h in range(2):
                    rows = shifted[s, c, q + h, pl.ds(a, 8), :]
                    if k:
                        stage[p, k, c, h] = rows
                    else:
                        patches[p][my_class, c, h] = rows
            if k:
                send(
                    stage.at[p, k],
                    patches[p].at[my_class],
                    patch_sems.at[p],
                    place.device(STEPS[k], -1, 1),
                )

    give_rows(0)

    for p in range(2):
        parts = []
        for u in range(4):
            part = jnp.zeros((1, 128), jnp.int32)
            for kk in range(16):
                part = jnp.where(lane // 8 == kk, places[0, 4 * (16 * (u % 2) + kk) + 2 * cores[u // 2] + p], part)
            parts.append(part)
        key = jnp.concatenate(parts, axis=1)
        step = lanes_of((1, 512))
        goal = (key >> 9) * 32 + (((key & 127) + 1 - core) >> 1) + step % 4
        rows = lax.broadcasted_iota(jnp.int32, (128, 512), 0)
        hits[p, 0] = jnp.where(rows == goal + (step // 4) % 2 * 32, 1.0, 0.0).astype(BF16)
        hits[p, 1] = jnp.where(rows == goal + 64, 1.0, 0.0).astype(BF16)
    grid_row = lax.broadcasted_iota(jnp.int32, (64, 128), 0)
    grid_col = lax.broadcasted_iota(jnp.int32, (64, 128), 1)
    found = jnp.zeros((64, 128), F32)
    for k in range(32):
        for row in range(4):
            value = places[0, 4 * k + row]
            found += jnp.where((grid_row == (value & 127)) & (grid_col == (value >> 7)), 1.0, 0.0)
    counts[...] = found
    send(counts, counts_in, count_sems, place.device((2, 2, 2)))
    give_rows(1)

    def frame(p, between):
        arrived(patches[p].at[pl.ds(0, 31)], patch_sems.at[p], 1)
        flat = patches[p].reshape(1024, 128)
        for c in range(2):
            for a in range(8):
                for h in range(2):
                    start = c * 16 + h * 8 + a
                    obj[c, 32 * a : 32 * a + 32, 128 * h : 128 * h + 128] = flat[pl.ds(start, 32, stride=32), :]
        forward(obj, probe, table, far, power, between)
        weight[...] = roots[p] / jnp.sqrt(jnp.maximum(power[...], 0.1)) - 1.0
        backward(probe, table, far, weight, grad)
        turn = off_ref[p, 1] & 127
        for c in range(2):
            rolled = pltpu.roll(grad[c], turn, 1)
            for h in range(2):
                turned[c, h] = rolled[:, 128 * h : 128 * h + 128]

    def lay_terms(p, other):
        start = ((cores[other] + off_ref[p, 0] // 32) & 1) * 32
        for i in range(32):
            for c in range(2):
                for h in range(2):
                    terms[p, other, i, c, 4 * h : 4 * h + 4] = turned[c, h, pl.ds(start + i, 4, stride=64), :]
        if not other:
            recv[p, 0] = terms[p, 0, my_class]

    def give_terms(p, some):
        for k, other in some:
            if k or other:
                send(
                    terms.at[p, other, place.class_at(*STEPS[k])],
                    recv.at[p, 32 * other + k],
                    term_sems.at[p, other],
                    place.device(STEPS[k], 1, other),
                )

    apart = [(k, 1) for k in FAR_FIRST + [0]]
    alike = [(k, 0) for k in FAR_FIRST]
    frame(0, lambda mode: None)
    lay_terms(0, 1)
    lay_terms(0, 0)
    frame(1, lambda mode: give_terms(0, (apart + alike)[8 * mode : 8 * mode + 8]))
    lay_terms(1, 1)
    give_terms(1, apart)
    lay_terms(1, 0)
    give_terms(1, alike)

    arrived(counts, count_sems, 1)
    totals[0:8] = jnp.zeros((8, 128), F32)
    totals[8:72] = counts[...] + counts_in[...]
    near = totals[pl.ds(2 * tile + core + 1, 8), :]
    for da in range(8):
        for b in range(9):
            q, s = b // 4, b % 4
            many = jnp.broadcast_to(near[7 - da : 8 - da, b : b + 1], (32, 128))
            for j in range(q, min(q + 3, 4)):
                if j - q == 2 and s == 0:
                    continue
                lit[j] += many * light4[s, 32 * da : 32 * da + 32, 128 * (j - q) : 128 * (j - q) + 128]
    for j in range(4):
        for c in range(2):
            under.reshape(256, 128)[pl.ds(2 * j + c, 32, stride=8), :] = lit[j] + 0.1

    sub = lax.broadcasted_iota(jnp.int32, (8, 128), 0)
    full_lane = lanes_of((8, 128))
    for p in range(2):
        part = 0.0
        for slot in list(range(32, 64, 2)) + list(range(0, 32, 2)):
            if slot == 32:
                arrived(recv.at[p, pl.ds(32, 32)], term_sems.at[p, 1], 1)
            if slot == 0:
                arrived(recv.at[p, pl.ds(1, 31)], term_sems.at[p, 0], 1)
            masks = []
            for d in range(2):
                turn = (places[0, 4 * ((slot + d) % 32) + 2 * cores[slot // 32] + p] >> 7) & 3
                masks.append((sub >= 4) | (full_lane >= 32 * turn))
            for c in range(2):
                pieces = [recv[p, slot + d, c] for d in range(2)]
                kept = rows2(*[jnp.where(masks[d], pieces[d], 0.0) for d in range(2)])
                wrapped = rows2(*[jnp.where(masks[d], 0.0, pieces[d]) for d in range(2)])
                for kind, piece in enumerate((kept, wrapped)):
                    high = piece.astype(BF16)
                    split[kind, 0, 8 * slot : 8 * slot + 16, 128 * c : 128 * c + 128] = high
                    split[kind, 1, 8 * slot : 8 * slot + 16, 128 * c : 128 * c + 128] = (
                        piece - high.astype(F32)
                    ).astype(BF16)
            if slot % 32 == 30:
                group = slice(8 * slot - 240, 8 * slot + 16)
                for kind in range(2):
                    for piece in range(2):
                        part += dot(hits[p, kind, :, group], split[kind, piece, group])
        if p == 0:
            result[...] = part
        else:
            result[...] += part
    for j in range(4):
        for c in range(2):
            ready.reshape(256, 128)[pl.ds(2 * j + c, 32, stride=8), :] = result[
                32 * j : 32 * j + 32, 128 * c : 128 * c + 128
            ]

    slot = place.half(0) * 16 + my_class
    for step in ALL_STEPS:
        send(ready.at[place.tile_at(*step)], rows_in.at[slot], last_sems, place.device(step))
    rows_in[slot] = ready[tile]
    arrived(rows_in.at[pl.ds(0, 63)], last_sems, 1)
    here = pl.ds(32 * core, 32)
    out_ref[here] = tile_rows[core] + (rows_in[0:32] + rows_in[32:64]) / under[...]
    send(out_ref.at[here], out_ref.at[here], out_sems, twin)
    arrived(out_ref.at[pl.ds(0, 32)], out_sems, 1)

    arrived(own, own_sems, 0)
    arrived(offs.at[pl.ds(1, 31)], off_sems, 0)
    arrived(held.at[pl.ds(0, 62)], row_sems, 0)
    for p in range(2):
        arrived(patches[p].at[pl.ds(0, 31)], patch_sems.at[p], 0)
        arrived(recv.at[p, pl.ds(1, 31)], term_sems.at[p, 0], 0)
        arrived(recv.at[p, pl.ds(32, 32)], term_sems.at[p, 1], 0)
    arrived(counts, count_sems, 0)
    arrived(rows_in.at[pl.ds(0, 63)], last_sems, 0)
    arrived(out_ref.at[pl.ds(0, 32)], out_sems, 0)


def on_device(object_tile, probe, offsets, frame_ids, frames):
    obj = object_tile.reshape(64, 2, 4, 128).transpose(0, 2, 1, 3).reshape(2, 32, 8, 128)
    hbm = pl.BlockSpec(memory_space=pltpu.HBM)
    pair = pltpu.SemaphoreType.DMA((2,))
    pairs = pltpu.SemaphoreType.DMA((2, 2))
    updated = pl.pallas_call(
        kernel,
        out_shape=pltpu.VMEM((64, 8, 128), F32),
        in_specs=[hbm] * 6,
        out_specs=pl.BlockSpec(memory_space=pltpu.VMEM),
        scratch_shapes=[
            pltpu.SMEM((2, 2), jnp.int32),
            pltpu.SMEM((2,), jnp.int32),
            pltpu.VMEM((2, 32, 8, 128), F32),
            pltpu.VMEM((8, 2, 256, 256), F32),
            pltpu.VMEM((2, 256, 256), F32),
            pltpu.VMEM((9, 256, 256), BF16),
            pltpu.VMEM((1, 128), jnp.int32),
            pltpu.VMEM((1, 128), jnp.int32),
            pltpu.VMEM((1, 1, 128), jnp.int32),
            pltpu.VMEM((32, 1, 128), jnp.int32),
            pltpu.VMEM((1, 128), jnp.int32),
            pltpu.SMEM((1, 128), jnp.int32),
            pltpu.VMEM((64, 8, 128), F32),
            pltpu.VMEM((4, 2, 4, 64, 128), F32),
            pltpu.VMEM((2, 32, 2, 2, 8, 128), F32),
            pltpu.VMEM((32, 2, 2, 8, 128), F32),
            pltpu.VMEM((32, 2, 2, 8, 128), F32),
            pltpu.VMEM((2, 256, 256), F32),
            pltpu.VMEM((2, 256, 128), F32),
            pltpu.VMEM((2, 256, 256), F32),
            pltpu.VMEM((8, 2, 256, 256), F32),
            pltpu.VMEM((256, 256), F32),
            pltpu.VMEM((256, 256), F32),
            pltpu.VMEM((2, 256, 256), F32),
            pltpu.VMEM((2, 2, 256, 128), F32),
            pltpu.VMEM((2, 2, 32, 2, 8, 128), F32),
            pltpu.VMEM((2, 64, 2, 8, 128), F32),
            pltpu.VMEM((64, 128), F32),
            pltpu.VMEM((64, 128), F32),
            pltpu.VMEM((72, 128), F32),
            pltpu.VMEM((4, 256, 384), F32),
            pltpu.VMEM((4, 32, 128), F32),
            pltpu.VMEM((32, 8, 128), F32),
            pltpu.VMEM((2, 2, 128, 512), BF16),
            pltpu.VMEM((2, 2, 512, 256), BF16),
            pltpu.VMEM((128, 256), F32),
            pltpu.VMEM((32, 8, 128), F32),
            pltpu.VMEM((64, 8, 128), F32),
            pltpu.SemaphoreType.DMA((7,)),
            pair,
            pair,
            pair,
            pairs,
            pltpu.SemaphoreType.DMA((2, 2, 2)),
            pair,
            pair,
            pair,
        ],
        compiler_params=pltpu.CompilerParams(
            collective_id=1, has_side_effects=True, vmem_limit_bytes=VMEM_LIMIT
        ),
        name="iteration",
    )(obj, probe, frames, jnp.asarray(tables()), offsets, frame_ids)
    return updated.reshape(64, 4, 2, 128).transpose(0, 2, 1, 3).reshape(64, 2, 512)


def solution(mesh):
    in_specs = (
        P("tile", None, None),
        P(),
        P(("grp", "tile"), None),
        P(("grp", "tile")),
        P(("grp", "tile"), None, None),
    )
    out_specs = P("tile", None, None)
    return jax.shard_map(
        on_device, mesh=mesh, in_specs=in_specs, out_specs=out_specs, check_vma=False
    )
```

```python
import functools

import jax
import jax.numpy as jnp
import ml_dtypes
import numpy as np
from jax import lax
from jax.experimental import pallas as pl
from jax.experimental.pallas import tpu as pltpu
from jax.sharding import PartitionSpec as P

MESH = pl.DeviceIdType.MESH
BF16 = jnp.bfloat16
F32 = jnp.float32
VMEM_LIMIT = 60 << 20


def _weight(step):
    return sum(min(part, 4 - part) for part in step)


STEPS = sorted(
    [
        step
        for step in ((a, b, c) for a in range(4) for b in range(4) for c in range(4))
        if _weight(step) < 3
    ],
    key=_weight,
) + [
    (2, 1, 0),
    (2, 3, 0),
    (0, 2, 1),
    (0, 2, 3),
    (1, 0, 2),
    (3, 0, 2),
    (1, 1, 1),
    (1, 3, 3),
    (3, 1, 3),
    (3, 3, 1),
]
ALL_STEPS = sorted(
    ((a, b, c) for a in range(4) for b in range(4) for c in range(4)), key=_weight, reverse=True
)[:-1]
FAR_FIRST = sorted(range(1, 32), key=lambda k: _weight(STEPS[k]), reverse=True)


class Place:
    def __init__(self):
        grp = lax.axis_index("grp")
        tile = lax.axis_index("tile")
        self.grp, self.tile = grp, tile
        self.core = lax.rem(grp, 2)
        self.x = lax.div(grp, 2) * 2 + lax.rem(tile, 2)
        self.y = lax.rem(lax.div(tile, 2), 4)
        self.z = lax.div(tile, 8)
        self.known = {}

    def once(self, name, make):
        if name not in self.known:
            self.known[name] = make()
        return self.known[name]

    def at(self, axis, by):
        by %= 4
        return self.once((axis, by), lambda: lax.rem(getattr(self, axis) + by, 4) if by else getattr(self, axis))

    def half(self, dx):
        return self.once(("half", dx % 4), lambda: lax.div(self.at("x", dx), 2) * 2)

    def tile_at(self, dx, dy, dz):
        plane = self.once(("plane", dx % 4, dy % 4), lambda: self.at("y", dy) * 2 + lax.rem(self.at("x", dx), 2))
        return self.once(("z8", dz % 4), lambda: self.at("z", dz) * 8) + plane

    def device(self, step, sign=1, other=0):
        dx, dy, dz = (sign * by for by in step)
        grp = self.once(("grp", dx % 4, other), lambda: self.half(dx) + (1 - self.core if other else self.core))
        return grp, self.tile_at(dx, dy, dz)

    def twin(self):
        return self.half(0) + 1 - self.core, self.tile

    def class_at(self, dx, dy, dz):
        near = self.once(
            ("near", dx % 4, dy % 4),
            lambda: lax.rem(self.at("x", dx), 2) * 16 + lax.rem(self.at("y", dy) + self.half(dx), 4) * 4,
        )
        return near + self.once(("deep", dx % 4, dz % 4), lambda: lax.rem(self.at("z", dz) + self.half(dx), 4))


def greet(place):
    barrier = pltpu.get_barrier_semaphore()
    for to in row_partners(place):
        pl.semaphore_signal(barrier, inc=1, device_id=to[:2], device_id_type=MESH)
    odd = lax.rem(place.tile, 2)
    beside = [step for step in STEPS if step[0] == 2]
    for step in beside:
        pl.semaphore_signal(barrier, inc=1, device_id=place.device(step, -1), device_id_type=MESH)
    ups = [step for step in STEPS if step[0] == 1]
    downs = [step for step in STEPS if step[0] == 3]
    assert len(ups) == len(downs)
    for up, down in zip(ups, downs):
        grp_a, tile_a = place.device(up, -1)
        grp_b, tile_b = place.device(down, -1)
        to = (grp_a + odd * (grp_b - grp_a), tile_a + odd * (tile_b - tile_a))
        pl.semaphore_signal(barrier, inc=1, device_id=to, device_id_type=MESH)
    pl.semaphore_signal(barrier, inc=1, device_id=place.twin(), device_id_type=MESH)
    return 31 + len(beside) + len(ups) + 1


def row_partners(place):
    across = lax.rem(place.tile + 1, 2) - lax.rem(place.tile, 2)
    partners = []
    for dx, dy, dz in sorted(
        ((a, b, c) for a in range(2) for b in range(4) for c in range(4)), key=_weight, reverse=True
    )[:-1]:
        plane = place.tile_at(0, dy, dz)
        cls = place.class_at(0, dy, dz)
        partners.append((place.grp, plane + dx * across, cls + 16 * dx * across))
    return partners


def send(source, target, sems, to):
    copy = pltpu.make_async_remote_copy(
        src_ref=source,
        dst_ref=target,
        send_sem=sems.at[0],
        recv_sem=sems.at[1],
        device_id=to,
        device_id_type=MESH,
    )
    copy.start()


def arrived(ref, sems, which):
    pltpu.make_async_copy(ref, ref, sems.at[which]).wait()


def lanes_of(shape):
    return lax.broadcasted_iota(jnp.int32, shape, len(shape) - 1)


def tables():
    line = np.arange(256)
    angle = 2.0 * np.pi / 256 * (line[:, None] * line[None, :] % 256)
    re = (np.cos(angle) / 16).astype(ml_dtypes.bfloat16)
    im = (-np.sin(angle) / 16).astype(ml_dtypes.bfloat16)

    def real_form(table_re, table_im, left):
        if left:
            return np.block([[table_re, -table_im], [table_im, table_re]])
        return np.block([[table_re, table_im], [-table_im, table_re]])

    made = []
    for odd in range(2):
        made.append(real_form(re[odd::2, :128], im[odd::2, :128], True))
    for odd in range(2):
        made.append(real_form(re[:128, odd::2], im[:128, odd::2], False))
    for odd in range(2):
        made.append(real_form(re[:128, odd::2], -im[:128, odd::2], True))
    for odd in range(2):
        made.append(real_form(re[odd::2, :128], -im[odd::2, :128], False))
    order = np.zeros((256, 256), ml_dtypes.bfloat16)
    order[np.concatenate([line[0::2], line[1::2]]), line] = 1
    made.append(order)
    return np.stack([table.astype(ml_dtypes.bfloat16) for table in made])


def dot(a, b):
    return jnp.dot(a, b, preferred_element_type=F32)


def rows2(a, b):
    return jnp.concatenate([a, b], axis=0)


def cols2(a, b):
    return jnp.concatenate([a, b], axis=1)


def forward(obj, probe, table, far, power, between):
    gained = [0.0, 0.0]
    for mode in range(8):
        probe_re = probe[mode, 0]
        probe_im = probe[mode, 1]
        obj_re = obj[0]
        obj_im = obj[1]
        exit_re = probe_re * obj_re - probe_im * obj_im
        exit_im = probe_re * obj_im + probe_im * obj_re
        both = rows2(exit_re[:128] + exit_re[128:], exit_im[:128] + exit_im[128:]).astype(BF16)
        less = rows2(exit_re[:128] - exit_re[128:], exit_im[:128] - exit_im[128:]).astype(BF16)
        sums = []
        lesses = []
        for half in (dot(table[0], both), dot(table[1], less)):
            re, im = half[:128], half[128:]
            sums.append(cols2(re[:, :128] + re[:, 128:], im[:, :128] + im[:, 128:]))
            lesses.append(cols2(re[:, :128] - re[:, 128:], im[:, :128] - im[:, 128:]))
        far_even = dot(rows2(*sums).astype(BF16), table[2])
        far_odd = dot(rows2(*lesses).astype(BF16), table[3])
        far[mode, 0] = far_even
        far[mode, 1] = far_odd
        for odd, wave in enumerate((far_even, far_odd)):
            re, im = wave[:, :128], wave[:, 128:]
            gained[odd] += re * re + im * im
        between(mode)
    for odd in range(2):
        power[:, odd * 128 : odd * 128 + 128] = gained[odd]


def backward(probe, table, far, weight, grad):
    weight_even = weight[:, :128]
    weight_odd = weight[:, 128:]
    gained = [0.0, 0.0]
    for mode in range(8):
        probe_re = probe[mode, 0]
        probe_im = probe[mode, 1]
        even = far[mode, 0]
        odd = far[mode, 1]
        diff_re = cols2(even[:, :128] * weight_even, odd[:, :128] * weight_odd).astype(BF16)
        diff_im = cols2(even[:, 128:] * weight_even, odd[:, 128:] * weight_odd).astype(BF16)
        back_even = dot(table[4], rows2(diff_re[:128], diff_im[:128]))
        back_odd = dot(table[5], rows2(diff_re[128:], diff_im[128:]))
        both = back_even + back_odd
        less = back_even - back_odd
        back_re = rows2(both[:128], less[:128]).astype(BF16)
        back_im = rows2(both[128:], less[128:]).astype(BF16)
        chi_even = dot(cols2(back_re[:, :128], back_im[:, :128]), table[6])
        chi_odd = dot(cols2(back_re[:, 128:], back_im[:, 128:]), table[7])
        both = chi_even + chi_odd
        less = chi_even - chi_odd
        chi_re = cols2(both[:, :128], less[:, :128])
        chi_im = cols2(both[:, 128:], less[:, 128:])
        gained[0] += probe_re * chi_re + probe_im * chi_im
        gained[1] += probe_re * chi_im - probe_im * chi_re
    for c in range(2):
        grad[c] = gained[c]


def detector_roots(frames, frame, columns, table, root):
    for h in range(2):
        columns[h] = frames[frame, :, 128 * h : 128 * h + 128]
    value = jnp.sqrt(
        rows2(*[cols2(*[columns[h, pl.ds(odd, 128, stride=2), :] for h in range(2)]) for odd in range(2)])
    )
    first = value.astype(BF16)
    rest = value - first.astype(F32)
    second = rest.astype(BF16)
    third = (rest - second.astype(F32)).astype(BF16)
    order = table[8]
    root[...] = dot(first, order) + dot(second, order) + dot(third, order)


def kernel(
    obj_hbm,
    probe_hbm,
    frames_hbm,
    table_hbm,
    off_hbm,
    ids_hbm,
    out_ref,
    off_ref,
    ids_ref,
    tile_rows,
    probe,
    frames,
    table,
    own,
    theirs,
    mine,
    offs,
    listed,
    places,
    held,
    shifted,
    stage,
    patch_a,
    patch_b,
    obj,
    columns,
    roots,
    far,
    power,
    weight,
    grad,
    turned,
    terms,
    recv,
    counts,
    counts_in,
    totals,
    light4,
    lit,
    under,
    hits,
    split,
    result,
    ready,
    rows_in,
    load_sems,
    own_sems,
    off_sems,
    row_sems,
    patch_sems,
    term_sems,
    count_sems,
    last_sems,
    out_sems,
):
    place = Place()
    core, tile = place.core, place.tile
    my_class = place.class_at(0, 0, 0)
    cores = (core, 1 - core)
    twin = place.twin()
    patches = (patch_a, patch_b)
    loads = [
        pltpu.make_async_copy(source, target, load_sems.at[i])
        for i, (source, target) in enumerate(
            (
                (obj_hbm.at[0], tile_rows.at[:, 0]),
                (obj_hbm.at[1], tile_rows.at[:, 1]),
                (off_hbm, off_ref),
                (ids_hbm, ids_ref),
                (probe_hbm, probe),
                (table_hbm, table),
                (frames_hbm, frames),
            )
        )
    ]
    loads[0].start()
    loads[1].start()
    met = greet(place)
    for load in loads[2:]:
        load.start()

    loads[2].wait()
    lane = lanes_of((1, 128))
    nodes = [(off_ref[p, 1] // 32) * 128 + off_ref[p, 0] // 32 for p in range(2)]
    own[...] = jnp.where(lane // 2 % 2 == core, jnp.where(lane % 2 == 0, nodes[0], nodes[1]), 0)
    pl.semaphore_wait(pltpu.get_barrier_semaphore(), met)
    send(own, theirs, own_sems, twin)
    loads[0].wait()
    loads[1].wait()
    for grp, other, cls in row_partners(place):
        send(tile_rows.at[cls], held.at[pl.ds(2 * tile, 2)], row_sems, (grp, other))
    arrived(theirs, own_sems, 1)
    mine[0] = own[...] + theirs[...]
    for k in FAR_FIRST:
        send(mine.at[0], offs.at[k], off_sems, place.device(STEPS[k]))
    offs[0] = mine[0]
    held[pl.ds(2 * tile, 2)] = tile_rows[my_class]

    for load in loads[3:]:
        load.wait()

    def add_light(m, total):
        return total + probe[m, 0] * probe[m, 0] + probe[m, 1] * probe[m, 1]

    light = cols2(lax.fori_loop(0, 8, add_light, jnp.zeros((256, 256), F32)), jnp.zeros((256, 128), F32))
    for s in range(4):
        light4[s] = light if s == 0 else pltpu.roll(light, 32 * s, 1)
    for p in range(2):
        detector_roots(frames, ids_ref[p], columns, table, roots.at[p])
    for j in range(4):
        lit[j] = jnp.zeros((32, 128), F32)

    arrived(offs.at[pl.ds(1, 31)], off_sems, 1)
    packed = jnp.zeros((1, 128), jnp.int32)
    for k in range(32):
        packed = jnp.where(lane // 4 == k, offs[k], packed)
    listed[...] = packed
    copy = pltpu.make_async_copy(listed, places, load_sems.at[7])
    copy.start()
    arrived(held.at[pl.ds(0, 62)], row_sems, 1)
    copy.wait()
    for c in range(2):
        line = jnp.concatenate(
            [held.reshape(512, 128)[pl.ds(2 * q + c, 64, stride=8), :] for q in range(4)], axis=1
        )
        for s in range(4):
            moved_line = line if s == 0 else pltpu.roll(line, 512 - 32 * s, 1)
            for q in range(4):
                shifted[s, c, q] = moved_line[:, 128 * q : 128 * q + 128]

    def give_rows(p):
        for k in FAR_FIRST + [0]:
            value = places[0, 4 * k + 2 * cores[1 if k else 0] + p]
            a = value & 127
            b = value >> 7
            q = b >> 2
            s = b & 3
            for c in range(2):
                for h in range(2):
                    rows = shifted[s, c, q + h, pl.ds(a, 8), :]
                    if k:
                        stage[p, k, c, h] = rows
                    else:
                        patches[p][my_class, c, h] = rows
            if k:
                send(
                    stage.at[p, k],
                    patches[p].at[my_class],
                    patch_sems.at[p],
                    place.device(STEPS[k], -1, 1),
                )

    give_rows(0)

    for p in range(2):
        parts = []
        for u in range(4):
            part = jnp.zeros((1, 128), jnp.int32)
            for kk in range(16):
                part = jnp.where(lane // 8 == kk, places[0, 4 * (16 * (u % 2) + kk) + 2 * cores[u // 2] + p], part)
            parts.append(part)
        key = jnp.concatenate(parts, axis=1)
        step = lanes_of((1, 512))
        goal = (key >> 9) * 32 + (((key & 127) + 1 - core) >> 1) + step % 4
        rows = lax.broadcasted_iota(jnp.int32, (128, 512), 0)
        hits[p, 0] = jnp.where(rows == goal + (step // 4) % 2 * 32, 1.0, 0.0).astype(BF16)
        hits[p, 1] = jnp.where(rows == goal + 64, 1.0, 0.0).astype(BF16)
    grid_row = lax.broadcasted_iota(jnp.int32, (64, 128), 0)
    grid_col = lax.broadcasted_iota(jnp.int32, (64, 128), 1)
    found = jnp.zeros((64, 128), F32)
    for k in range(32):
        for row in range(4):
            value = places[0, 4 * k + row]
            found += jnp.where((grid_row == (value & 127)) & (grid_col == (value >> 7)), 1.0, 0.0)
    counts[...] = found
    send(counts, counts_in, count_sems, place.device((2, 2, 2)))
    give_rows(1)

    def frame(p, between):
        arrived(patches[p].at[pl.ds(0, 31)], patch_sems.at[p], 1)
        flat = patches[p].reshape(1024, 128)
        for c in range(2):
            for a in range(8):
                for h in range(2):
                    start = c * 16 + h * 8 + a
                    obj[c, 32 * a : 32 * a + 32, 128 * h : 128 * h + 128] = flat[pl.ds(start, 32, stride=32), :]
        forward(obj, probe, table, far, power, between)
        weight[...] = roots[p] / jnp.sqrt(jnp.maximum(power[...], 0.1)) - 1.0
        backward(probe, table, far, weight, grad)
        turn = off_ref[p, 1] & 127
        for c in range(2):
            rolled = pltpu.roll(grad[c], turn, 1)
            for h in range(2):
                turned[c, h] = rolled[:, 128 * h : 128 * h + 128]

    def lay_terms(p, other):
        start = ((cores[other] + off_ref[p, 0] // 32) & 1) * 32
        for i in range(32):
            for c in range(2):
                for h in range(2):
                    terms[p, other, i, c, 4 * h : 4 * h + 4] = turned[c, h, pl.ds(start + i, 4, stride=64), :]
        if not other:
            recv[p, 0] = terms[p, 0, my_class]

    def give_terms(p, some):
        for k, other in some:
            if k or other:
                send(
                    terms.at[p, other, place.class_at(*STEPS[k])],
                    recv.at[p, 32 * other + k],
                    term_sems.at[p, other],
                    place.device(STEPS[k], 1, other),
                )

    apart = [(k, 1) for k in FAR_FIRST + [0]]
    alike = [(k, 0) for k in FAR_FIRST]
    frame(0, lambda mode: None)
    lay_terms(0, 1)
    lay_terms(0, 0)
    frame(1, lambda mode: give_terms(0, (apart + alike)[8 * mode : 8 * mode + 8]))
    lay_terms(1, 1)
    give_terms(1, apart)
    lay_terms(1, 0)
    give_terms(1, alike)

    arrived(counts, count_sems, 1)
    totals[0:8] = jnp.zeros((8, 128), F32)
    totals[8:72] = counts[...] + counts_in[...]
    near = totals[pl.ds(2 * tile + core + 1, 8), :]
    for da in range(8):
        for b in range(9):
            q, s = b // 4, b % 4
            many = jnp.broadcast_to(near[7 - da : 8 - da, b : b + 1], (32, 128))
            for j in range(q, min(q + 3, 4)):
                if j - q == 2 and s == 0:
                    continue
                lit[j] += many * light4[s, 32 * da : 32 * da + 32, 128 * (j - q) : 128 * (j - q) + 128]
    for j in range(4):
        for c in range(2):
            under.reshape(256, 128)[pl.ds(2 * j + c, 32, stride=8), :] = lit[j] + 0.1

    sub = lax.broadcasted_iota(jnp.int32, (8, 128), 0)
    full_lane = lanes_of((8, 128))
    for p in range(2):
        part = 0.0
        for slot in list(range(32, 64, 2)) + list(range(0, 32, 2)):
            if slot == 32:
                arrived(recv.at[p, pl.ds(32, 32)], term_sems.at[p, 1], 1)
            if slot == 0:
                arrived(recv.at[p, pl.ds(1, 31)], term_sems.at[p, 0], 1)
            masks = []
            for d in range(2):
                turn = (places[0, 4 * ((slot + d) % 32) + 2 * cores[slot // 32] + p] >> 7) & 3
                masks.append((sub >= 4) | (full_lane >= 32 * turn))
            for c in range(2):
                pieces = [recv[p, slot + d, c] for d in range(2)]
                kept = rows2(*[jnp.where(masks[d], pieces[d], 0.0) for d in range(2)])
                wrapped = rows2(*[jnp.where(masks[d], 0.0, pieces[d]) for d in range(2)])
                for kind, piece in enumerate((kept, wrapped)):
                    high = piece.astype(BF16)
                    split[kind, 0, 8 * slot : 8 * slot + 16, 128 * c : 128 * c + 128] = high
                    split[kind, 1, 8 * slot : 8 * slot + 16, 128 * c : 128 * c + 128] = (
                        piece - high.astype(F32)
                    ).astype(BF16)
            if slot % 32 == 30:
                group = slice(8 * slot - 240, 8 * slot + 16)
                for kind in range(2):
                    for piece in range(2):
                        part += dot(hits[p, kind, :, group], split[kind, piece, group])
        if p == 0:
            result[...] = part
        else:
            result[...] += part
    for j in range(4):
        for c in range(2):
            ready.reshape(256, 128)[pl.ds(2 * j + c, 32, stride=8), :] = result[
                32 * j : 32 * j + 32, 128 * c : 128 * c + 128
            ]

    slot = place.half(0) * 16 + my_class
    for step in ALL_STEPS:
        send(ready.at[place.tile_at(*step)], rows_in.at[slot], last_sems, place.device(step))
    rows_in[slot] = ready[tile]
    arrived(rows_in.at[pl.ds(0, 63)], last_sems, 1)
    here = pl.ds(32 * core, 32)
    out_ref[here] = tile_rows[:, core] + (rows_in[0:32] + rows_in[32:64]) / under[...]
    send(out_ref.at[here], out_ref.at[here], out_sems, twin)
    arrived(out_ref.at[pl.ds(0, 32)], out_sems, 1)

    arrived(own, own_sems, 0)
    arrived(offs.at[pl.ds(1, 31)], off_sems, 0)
    arrived(held.at[pl.ds(0, 62)], row_sems, 0)
    for p in range(2):
        arrived(patches[p].at[pl.ds(0, 31)], patch_sems.at[p], 0)
        arrived(recv.at[p, pl.ds(1, 31)], term_sems.at[p, 0], 0)
        arrived(recv.at[p, pl.ds(32, 32)], term_sems.at[p, 1], 0)
    arrived(counts, count_sems, 0)
    arrived(rows_in.at[pl.ds(0, 63)], last_sems, 0)
    arrived(out_ref.at[pl.ds(0, 32)], out_sems, 0)


def on_device(object_tile, probe, offsets, frame_ids, frames):
    obj = object_tile.reshape(64, 2, 4, 128).transpose(0, 2, 1, 3).reshape(2, 32, 8, 128)
    hbm = pl.BlockSpec(memory_space=pltpu.HBM)
    pair = pltpu.SemaphoreType.DMA((2,))
    pairs = pltpu.SemaphoreType.DMA((2, 2))
    updated = pl.pallas_call(
        kernel,
        out_shape=pltpu.VMEM((64, 8, 128), F32),
        in_specs=[hbm] * 6,
        out_specs=pl.BlockSpec(memory_space=pltpu.VMEM),
        scratch_shapes=[
            pltpu.SMEM((2, 2), jnp.int32),
            pltpu.SMEM((2,), jnp.int32),
            pltpu.VMEM((32, 2, 8, 128), F32),
            pltpu.VMEM((8, 2, 256, 256), F32),
            pltpu.VMEM((2, 256, 256), F32),
            pltpu.VMEM((9, 256, 256), BF16),
            pltpu.VMEM((1, 128), jnp.int32),
            pltpu.VMEM((1, 128), jnp.int32),
            pltpu.VMEM((1, 1, 128), jnp.int32),
            pltpu.VMEM((32, 1, 128), jnp.int32),
            pltpu.VMEM((1, 128), jnp.int32),
            pltpu.SMEM((1, 128), jnp.int32),
            pltpu.VMEM((64, 8, 128), F32),
            pltpu.VMEM((4, 2, 4, 64, 128), F32),
            pltpu.VMEM((2, 32, 2, 2, 8, 128), F32),
            pltpu.VMEM((32, 2, 2, 8, 128), F32),
            pltpu.VMEM((32, 2, 2, 8, 128), F32),
            pltpu.VMEM((2, 256, 256), F32),
            pltpu.VMEM((2, 256, 128), F32),
            pltpu.VMEM((2, 256, 256), F32),
            pltpu.VMEM((8, 2, 256, 256), F32),
            pltpu.VMEM((256, 256), F32),
            pltpu.VMEM((256, 256), F32),
            pltpu.VMEM((2, 256, 256), F32),
            pltpu.VMEM((2, 2, 256, 128), F32),
            pltpu.VMEM((2, 2, 32, 2, 8, 128), F32),
            pltpu.VMEM((2, 64, 2, 8, 128), F32),
            pltpu.VMEM((64, 128), F32),
            pltpu.VMEM((64, 128), F32),
            pltpu.VMEM((72, 128), F32),
            pltpu.VMEM((4, 256, 384), F32),
            pltpu.VMEM((4, 32, 128), F32),
            pltpu.VMEM((32, 8, 128), F32),
            pltpu.VMEM((2, 2, 128, 512), BF16),
            pltpu.VMEM((2, 2, 512, 256), BF16),
            pltpu.VMEM((128, 256), F32),
            pltpu.VMEM((32, 8, 128), F32),
            pltpu.VMEM((64, 8, 128), F32),
            pltpu.SemaphoreType.DMA((8,)),
            pair,
            pair,
            pair,
            pairs,
            pltpu.SemaphoreType.DMA((2, 2, 2)),
            pair,
            pair,
            pair,
        ],
        compiler_params=pltpu.CompilerParams(
            collective_id=1, has_side_effects=True, vmem_limit_bytes=VMEM_LIMIT
        ),
        name="iteration",
    )(obj, probe, frames, jnp.asarray(tables()), offsets, frame_ids)
    return updated.reshape(64, 4, 2, 128).transpose(0, 2, 1, 3).reshape(64, 2, 512)


def solution(mesh):
    in_specs = (
        P("tile", None, None),
        P(),
        P(("grp", "tile"), None),
        P(("grp", "tile")),
        P(("grp", "tile"), None, None),
    )
    out_specs = P("tile", None, None)
    return jax.shard_map(
        on_device, mesh=mesh, in_specs=in_specs, out_specs=out_specs, check_vma=False
    )
```
